32 devices in a mesh: mem: 2 (over x), fsdp: 16 (over z, y, core).
Axes of the slice: x: 2, y: 2, z: 4, core: 2. Of those that a mesh axis runs over, the one named last changes fastest.
Arguments:
- tokens: bfloat16 [32, 1024, 768], P('fsdp', 'mem'), may hold values from -6 to 6
- memory: bfloat16 [32, 256, 768], P('fsdp', 'mem'), may hold values from -6 to 6
- cotangent: bfloat16 [32, 1024, 768], P('fsdp', 'mem'), may hold values from -6 to 6
- text_len: int32 [32], P('fsdp'), may hold values from 1 to 1024, as said below
- mem_len: int32 [32], P('fsdp'), may hold values from 1 to 256
- image_flag: int32 [32], P('fsdp'), may hold values from 0 to 1
- self_qkv: bfloat16 [3, 768, 768], P(None, 'fsdp'), may hold values from -0.3125 to 0.3125
- self_out: bfloat16 [768, 768], P('fsdp'), may hold values from -0.875 to 0.875
- cross_qkv: bfloat16 [3, 768, 768], P(None, 'fsdp'), may hold values from -0.3125 to 0.3125
- cross_out: bfloat16 [768, 768], P('fsdp'), may hold values from -0.625 to 0.625
- w_in: bfloat16 [768, 3072], P('fsdp'), may hold values from -0.21875 to 0.21875
- w_out: bfloat16 [3072, 768], P('fsdp'), may hold values from -0.109375 to 0.109375
- b_in: bfloat16 [3072], P('fsdp'), may hold values from -3 to 3
- b_out: bfloat16 [768], P('fsdp'), may hold values from -2 to 2
- norm_gain: bfloat16 [3, 768], P(None, 'fsdp'), may hold values from 0.099609375 to 1.8984375
- norm_bias: bfloat16 [3, 768], P(None, 'fsdp'), may hold values from -2 to 2
Outputs:
- mixed: bfloat16 [32, 1024, 768], P('fsdp', 'mem')
- grad_tokens: float32 [32, 1024, 768], P('fsdp', 'mem')
- grad_memory: float32 [32, 256, 768], P('fsdp', 'mem')
- grad_self_qkv: float32 [3, 768, 768], P(None, 'fsdp')
- grad_self_out: float32 [768, 768], P('fsdp')
- grad_cross_qkv: float32 [3, 768, 768], P(None, 'fsdp')
- grad_cross_out: float32 [768, 768], P('fsdp')
- grad_w_in: float32 [768, 3072], P('fsdp')
- grad_w_out: float32 [3072, 768], P('fsdp')
- grad_b_in: float32 [3072], P('fsdp')
- grad_b_out: float32 [768], P('fsdp')
- grad_norm_gain: float32 [3, 768], P(None, 'fsdp')
- grad_norm_bias: float32 [3, 768], P(None, 'fsdp')
The draws below stay inside these ranges and needn't reach their ends.
Inputs may be any that keep to these rules, and one draw needn't show every extreme that they name: In each aligned run of 2 sequences one has text_len 1024, mem_len 256 and image_flag 1.
All inputs are finite; a program needn't handle non-finite values.
Results may differ from the reference program's by a relative error of at most 0.029.
The reference program's roundings to bfloat16 on the way count: a program that leaves them out, or rounds other values in their place, can miss the bound.
Values may be sent and summed in bfloat16 or wider, within the bound.
A program may use at most 256 MiB of HBM per device.

```python
import jax
import jax.numpy as jnp
from jax import lax

D = 768
HEAD_FEATURES = 64
FF = 3072
LEN = 1024
MEM = 256
SEQ_DEV = 2
SEQS = 32


def full_pick(key):
    chosen = jax.random.randint(key, (SEQS // SEQ_DEV,), 0, SEQ_DEV)
    slot = jnp.arange(SEQS, dtype=jnp.int32) % SEQ_DEV
    return slot == jnp.repeat(chosen, SEQ_DEV)


def draw_text_len(key, part):
    full = full_pick(key)
    key = jax.random.fold_in(key, 11)
    drawn = jax.random.randint(key, (SEQS,), 1, LEN + 1)
    return jnp.where(full, LEN, drawn).astype(jnp.int32)


def draw_mem_len(key, part):
    full = full_pick(key)
    key = jax.random.fold_in(key, 12)
    drawn = jax.random.randint(key, (SEQS,), 1, MEM + 1)
    return jnp.where(full, MEM, drawn).astype(jnp.int32)


def draw_image_flag(key, part):
    full = full_pick(key)
    key = jax.random.fold_in(key, 13)
    drawn = jax.random.randint(key, (SEQS,), 0, 2)
    return jnp.where(full, 1, drawn).astype(jnp.int32)


def shard_levels(stream_key, dims, shards, least, top_value):
    level, own = 1.0, jax.random.fold_in(stream_key, 6)
    for dim, blocks in shards:
        draws = jnp.exp(jax.random.uniform(jax.random.fold_in(own, dim), (blocks,), jnp.float32, least / len(shards), top_value / len(shards)))
        level = level * jnp.repeat(draws, dims[dim] // blocks).reshape([-1 if axis == dim else 1 for axis in range(len(dims))])
    return level


def bell_draw(own_key, extent, scale, limit, shards=(), kind=jnp.bfloat16):
    result = scale * jax.random.normal(own_key, extent, jnp.float32)
    if shards:
        result = result * shard_levels(own_key, extent, shards, -0.22, 0.18)
    return jnp.clip(result, -limit, limit).astype(kind)


def setup_inputs(seed: int = 0) -> dict:
    seeds = jax.random.split(jax.random.key(seed), 17)
    tokens = bell_draw(seeds[0], (SEQS, LEN, D), 1.0, 6.0, ((0, 16), (1, 2)))
    memory = bell_draw(seeds[1], (SEQS, MEM, D), 1.0, 6.0, ((0, 16), (1, 2)))
    cotangent = bell_draw(seeds[2], (SEQS, LEN, D), 1.0, 6.0, ((0, 16), (1, 2)))
    text_len = draw_text_len(jax.random.fold_in(seeds[16], 71), 0)
    mem_len = draw_mem_len(jax.random.fold_in(seeds[16], 71), 0)
    image_flag = draw_image_flag(jax.random.fold_in(seeds[16], 71), 0)
    self_qkv = bell_draw(seeds[6], (3, D, D), (D // 2) ** -0.5, 0.3125, ((1, 16),))
    self_out = bell_draw(seeds[7], (D, D), (D // 16) ** -0.5, 0.875, ((0, 16),))
    cross_qkv = bell_draw(seeds[8], (3, D, D), (D // 2) ** -0.5, 0.3125, ((1, 16),))
    cross_out = bell_draw(seeds[9], (D, D), (D // 8) ** -0.5, 0.625, ((0, 16),))
    w_in = bell_draw(seeds[10], (D, FF), D ** -0.5, 0.21875, ((0, 16),))
    w_out = bell_draw(seeds[11], (FF, D), FF ** -0.5, 0.109375, ((0, 16),))
    b_in = bell_draw(seeds[12], (FF,), 0.5, 3.0, ((0, 16),))
    b_out = bell_draw(seeds[13], (D,), 0.3, 2.0, ((0, 16),))
    norm_gain = jnp.clip(1.0 + 0.18 * jax.random.normal(seeds[14], (3, D), jnp.float32), 0.099609375, 1.8984375).astype(jnp.bfloat16)
    norm_bias = bell_draw(seeds[15], (3, D), 0.3, 2.0, ((1, 16),))
    return dict(tokens=tokens, memory=memory, cotangent=cotangent, text_len=text_len, mem_len=mem_len, image_flag=image_flag, self_qkv=self_qkv, self_out=self_out, cross_qkv=cross_qkv, cross_out=cross_out, w_in=w_in, w_out=w_out, b_in=b_in, b_out=b_out, norm_gain=norm_gain, norm_bias=norm_bias)


EPSILON = 1e-05
HIGH = lax.Precision.HIGHEST

@jax.custom_vjp
def low(v):
    return lax.optimization_barrier(v.astype(jnp.bfloat16)).astype(jnp.float32)

@jax.custom_vjp
def low_back(v):
    return v

def low_keep(v):
    return (low(v), None)

def low_pass(kept, grad):
    return (grad,)

def back_keep(v):
    return (v, None)

def back_low(kept, grad):
    return (low(grad),)
low.defvjp(low_keep, low_pass)
low_back.defvjp(back_keep, back_low)

def layer_norm(values, gain, shift):
    centre = values - lax.optimization_barrier(jnp.mean(values, -1, keepdims=True))
    spread = lax.optimization_barrier(jnp.mean(centre * centre, -1, keepdims=True))
    return centre * lax.rsqrt(spread + EPSILON) * gain + shift

def attention(query_matrix, key_matrix, values, allowed):
    batch = query_matrix.shape[0]
    rows = query_matrix.shape[1]
    q_heads = query_matrix.reshape(batch, rows, -1, HEAD_FEATURES)
    k_heads = key_matrix.reshape(batch, key_matrix.shape[1], -1, HEAD_FEATURES)
    v_heads = values.reshape(batch, values.shape[1], -1, HEAD_FEATURES)
    logit_scores = low_back(HEAD_FEATURES ** (-0.5) * jnp.einsum('bqhe,bkhe->bhqk', q_heads, k_heads, precision=HIGH))
    logit_scores = jnp.where(allowed[:, None], logit_scores, -1000000000.0)
    row_max = lax.optimization_barrier(jnp.max(logit_scores, -1, keepdims=True))
    expo = jnp.exp(logit_scores - row_max)
    probs = low(expo / lax.optimization_barrier(jnp.sum(expo, -1, keepdims=True)))
    mixed_heads = jnp.einsum('bhqk,bkhe->bqhe', probs, v_heads, precision=HIGH)
    return mixed_heads.reshape(batch, rows, -1)

def forward(x0, m0, params, self_mask, cross_mask, flag):
    self_w, self_proj, cross_w, cross_proj, inner_w, outer_w, inner_bias, outer_bias, gains, shifts = params
    h1 = low(layer_norm(x0, gains[0], shifts[0]))
    qkv = low_back(low(jnp.einsum('bld,kde->kble', h1, self_w, precision=HIGH)))
    attended = low_back(low(attention(qkv[0], qkv[1], qkv[2], self_mask)))
    x1 = x0 + low_back(jnp.einsum('bld,de->ble', attended, self_proj, precision=HIGH))
    h2 = low(layer_norm(x1, gains[1], shifts[1]))
    cross_q = low_back(low(jnp.einsum('bld,de->ble', h2, cross_w[0], precision=HIGH)))
    cross_kv = low_back(low(jnp.einsum('bnd,kde->kbne', m0, cross_w[1:], precision=HIGH)))
    crossed = low_back(low(attention(cross_q, cross_kv[0], cross_kv[1], cross_mask)))
    x2 = x1 + low_back(jnp.einsum('bld,de->ble', crossed, cross_proj, precision=HIGH)) * flag
    h3 = low(layer_norm(x2, gains[2], shifts[2]))
    pre = low_back(jnp.einsum('bld,df->blf', h3, inner_w, precision=HIGH) + inner_bias)
    act = low(jax.nn.gelu(pre, approximate=False))
    return x2 + low_back(jnp.einsum('blf,fd->bld', act, outer_w, precision=HIGH) + outer_bias)

def reference(tokens, memory, cotangent, text_len, mem_len, image_flag, self_qkv, self_out, cross_qkv, cross_out, w_in, w_out, b_in, b_out, norm_gain, norm_bias):
    params = tuple((item.astype(jnp.float32) for item in (self_qkv, self_out, cross_qkv, cross_out, w_in, w_out, b_in, b_out, norm_gain, norm_bias)))
    group = 4
    count = SEQS // group

    def shape_groups(value):
        return value.reshape((count, group) + value.shape[1:])
    inputs = (shape_groups(tokens), shape_groups(memory), shape_groups(cotangent), shape_groups(text_len), shape_groups(mem_len), shape_groups(image_flag))

    def step(carry, item):
        x_part, m_part, c_part, t_part, l_part, f_part = item
        position = jnp.arange(LEN, dtype=jnp.int32)
        self_mask = (position[None, None, :] <= position[None, :, None]) & (position[None, None, :] < t_part[:, None, None])
        mem_pos = jnp.arange(MEM, dtype=jnp.int32)
        cross_mask = jnp.broadcast_to(mem_pos[None, None, :] < l_part[:, None, None], (group, LEN, MEM))
        flag = f_part.astype(jnp.float32)[:, None, None]

        def run(x_val, m_val, p_val):
            return forward(x_val, m_val, p_val, self_mask, cross_mask, flag)
        attention_output, backward = jax.vjp(run, x_part.astype(jnp.float32), m_part.astype(jnp.float32), params)
        d_x, d_m, d_p = backward(c_part.astype(jnp.float32))
        carry = jax.tree.map(jnp.add, carry, d_p)
        return (carry, (attention_output.astype(jnp.bfloat16), d_x, d_m))
    initial = jax.tree.map(jnp.zeros_like, params)
    grads, (results, d_tokens, d_memory) = lax.scan(step, initial, inputs)
    return (results.reshape(tokens.shape), d_tokens.reshape(tokens.shape), d_memory.reshape(memory.shape), grads[0], grads[1], grads[2], grads[3], grads[4], grads[5], grads[6], grads[7], grads[8], grads[9])
```

```python
import jax
import jax.numpy as jnp
from jax import lax
from jax.experimental import pallas as pl
from jax.experimental.pallas import tpu as pltpu
from jax.sharding import PartitionSpec as P

F32 = jnp.float32
B16 = jnp.bfloat16
HEAD = 64
GROUP = 256
PER = GROUP // HEAD
EPSILON = 1e-05
NEG = -1000000000.0


def dot(a, b):
    return jnp.dot(a, b, preferred_element_type=F32)


def dot_nt(a, b):
    return lax.dot_general(a, b, (((1,), (1,)), ((), ())), preferred_element_type=F32)


def dot_tn(a, b):
    return lax.dot_general(a, b, (((0,), (0,)), ((), ())), preferred_element_type=F32)


def norm_parts(v):
    centre = v - jnp.mean(v, -1, keepdims=True)
    rs = lax.rsqrt(jnp.mean(centre * centre, -1, keepdims=True) + EPSILON)
    return centre * rs, rs


def norm_back(e, v, gain):
    n, rs = norm_parts(v)
    t = e * gain
    dx = rs * (t - jnp.mean(t, -1, keepdims=True) - n * jnp.mean(t * n, -1, keepdims=True))
    return dx, jnp.sum(e * n, 0, keepdims=True), jnp.sum(e, 0, keepdims=True)


def cols(g):
    return pl.ds(pl.multiple_of(g * GROUP, GROUP), GROUP)


def head_rows(h, rows, width):
    return lax.broadcasted_iota(jnp.int32, (rows, width), 0) // HEAD == h


def head_cols(h, rows, width):
    return lax.broadcasted_iota(jnp.int32, (rows, width), 1) // HEAD == h


def allowed_block(first_key, nk, first_query, nq, limit, causal):
    key = first_key + lax.broadcasted_iota(jnp.int32, (nk, nq), 0)
    ok = key < limit
    if causal:
        query = first_query + lax.broadcasted_iota(jnp.int32, (nk, nq), 1)
        ok = ok & (key <= query)
    return ok


def masked_scores(k_ref, kidx, qm, nk, q0, tq, limit, causal):
    s = dot(k_ref[kidx + (pl.ds(0, nk),)], qm)
    if causal and nk > tq:
        top = jnp.where(allowed_block(0, nk - tq, q0, tq, limit, False), s[: nk - tq], NEG)
        bottom = jnp.where(allowed_block(nk - tq, tq, q0, tq, limit, True), s[nk - tq :], NEG)
        return jnp.concatenate([top, bottom], 0)
    return jnp.where(allowed_block(nk - (tq if causal else nk), nk, q0, tq, limit, causal), s, NEG)


def attend_group(q_ref, k_ref, v_ref, qi_, ki_, vi_, out_ref, g, lse_ref, limit, causal, tq, qt, vt, ot):
    L = qt.shape[1]
    K = vt.shape[1]
    qt[...] = (q_ref[qi_].astype(F32) * HEAD**-0.5).T.astype(B16)
    vt[...] = v_ref[vi_].astype(F32).T.astype(B16)
    for i in range(L // tq):
        nk = (i + 1) * tq if causal else K
        for h in range(PER):
            block = qt[:, i * tq : (i + 1) * tq]
            qm = jnp.where(head_rows(h, GROUP, tq), block, jnp.zeros_like(block))
            s = masked_scores(k_ref, ki_, qm, nk, i * tq, tq, limit, causal)
            m = jnp.max(s, 0, keepdims=True)
            e = jnp.exp(s - m)
            total = jnp.sum(e, 0, keepdims=True)
            p = (e * (1.0 / total)).astype(B16)
            lse_ref[g, h : h + 1, i * tq : (i + 1) * tq] = m + jnp.log(total)
            o = dot(vt[h * HEAD : (h + 1) * HEAD, 0:nk], p)
            ot[h * HEAD : (h + 1) * HEAD, i * tq : (i + 1) * tq] = o.astype(B16)
    out_ref[:, cols(g)] = ot[...].astype(F32).T.astype(B16)


def attend_back_group(
    q_ref, k_ref, v_ref, qi_, ki_, vi_, a_ref, da_ref, g, lse_ref, limit, causal, tq,
    qt, kt, at, dat, ps, dss, qm_ref, dm_ref, dqt, dk_acc, dv_acc,
):
    L = qt.shape[1]
    K = kt.shape[1]
    scale = HEAD**-0.5
    qt[...] = (q_ref[qi_].astype(F32) * scale).T.astype(B16)
    kt[...] = (k_ref[ki_].astype(F32) * scale).T.astype(B16)
    at[...] = a_ref[:, cols(g)].astype(F32).T
    dat[...] = da_ref[:, cols(g)].astype(F32).T.astype(B16)
    if causal:
        dk_acc[...] = jnp.zeros_like(dk_acc)
        dv_acc[...] = jnp.zeros_like(dv_acc)
    for i in range(L // tq):
        nk = (i + 1) * tq if causal else K
        span = slice(i * tq, (i + 1) * tq)
        qn = q_ref[qi_ + (pl.ds(i * tq, tq),)] * jnp.asarray(scale, B16)
        dn = da_ref[pl.ds(i * tq, tq), cols(g)]
        for h in range(PER):
            hs = slice(h * HEAD, (h + 1) * HEAD)
            here = head_rows(h, GROUP, tq)
            block = qt[:, span]
            qm = jnp.where(here, block, jnp.zeros_like(block))
            block = dat[:, span]
            dm = jnp.where(here, block, jnp.zeros_like(block))
            delta = jnp.sum(at[hs, span] * dat[hs, span].astype(F32), 0, keepdims=True)
            s = masked_scores(k_ref, ki_, qm, nk, i * tq, tq, limit, causal)
            p = jnp.exp(s - lse_ref[g, h : h + 1, span])
            dp = dot(v_ref[vi_ + (pl.ds(0, nk),)], dm)
            ds = (p * (dp - delta)).astype(B16)
            ps[0:nk, h * tq : (h + 1) * tq] = p.astype(B16)
            dss[0:nk, h * tq : (h + 1) * tq] = ds
            dqt[hs, span] = dot(kt[hs, 0:nk], ds)
            mine = head_cols(h, tq, GROUP)
            qm_ref[h * tq : (h + 1) * tq] = jnp.where(mine, qn, jnp.zeros_like(qn))
            dm_ref[h * tq : (h + 1) * tq] = jnp.where(mine, dn, jnp.zeros_like(dn))
        dvi = dot(ps[0:nk], dm_ref[...])
        dki = dot(dss[0:nk], qm_ref[...])
        if causal:
            dv_acc[0:nk] += dvi
            dk_acc[0:nk] += dki
        elif i == 0:
            dv_acc[...] = dvi
            dk_acc[...] = dki
        else:
            dv_acc[...] += dvi
            dk_acc[...] += dki


ERFCX = (
    0.21161358920977177, 0.2106475215974073, 0.20533035663075158, 0.12143152976148842,
    0.27391662866419597, -0.22972237163936396, 0.432698311257476, -0.287490481514182,
    0.06157492612604076,
)


def gelu_parts(u):
    z = jnp.abs(u) * 0.7071067811865476
    t = 1.0 / (1.0 + 0.375 * z)
    poly = jnp.full_like(t, ERFCX[8])
    for c in ERFCX[7::-1]:
        poly = poly * t + c
    bell = jnp.exp(-0.5 * u * u)
    half = 0.5 * (poly * t) * bell
    cdf = jnp.where(u >= 0, 1.0 - half, half)
    return u * cdf, cdf + u * (bell * 0.3989422804014327)


ROWS = 256


def self_forward(tlen, tokens, gains, shifts, w, proj, h1, qkv, a, lse, x1, qt, vt, ot):
    L, D = tokens.shape
    for r in range(0, L, ROWS):
        rs = pl.ds(r, ROWS)
        n, _ = norm_parts(tokens[rs].astype(F32))
        h1[rs] = (n * gains[0:1] + shifts[0:1]).astype(B16)

    def group(g, _):
        for k in range(3):
            qkv[k, g] = dot(h1[...], w[k, :, cols(g)]).astype(B16)
        attend_group(qkv, qkv, qkv, (0, g), (1, g), (2, g), a, g, lse, tlen[0], True, 256, qt, vt, ot)
        return 0

    lax.fori_loop(0, D // GROUP, group, 0)
    for r in range(0, L, ROWS):
        rs = pl.ds(r, ROWS)
        x1[rs] = tokens[rs].astype(F32) + dot(a[rs], proj[...])


def cross_forward(mlen, flag, x1, mem, gains, shifts, w, proj, h2, cq, ckv, c, lse, x2, qt, vt, ot):
    L, D = x1.shape
    for r in range(0, L, ROWS):
        rs = pl.ds(r, ROWS)
        n, _ = norm_parts(x1[rs])
        h2[rs] = (n * gains[1:2] + shifts[1:2]).astype(B16)

    def group(g, _):
        cq[g] = dot(h2[...], w[0, :, cols(g)]).astype(B16)
        ckv[0, g] = dot(mem[...], w[1, :, cols(g)]).astype(B16)
        ckv[1, g] = dot(mem[...], w[2, :, cols(g)]).astype(B16)
        attend_group(cq, ckv, ckv, (g,), (0, g), (1, g), c, g, lse, mlen[0], False, 256, qt, vt, ot)
        return 0

    lax.fori_loop(0, D // GROUP, group, 0)
    f = flag[0].astype(F32)
    for r in range(0, L, ROWS):
        rs = pl.ds(r, ROWS)
        x2[rs] = x1[rs] + f * dot(c[rs], proj[...])


def feed_forward(x2, cot, gains, shifts, w_in, w_out, b_in, b_out, mixed, g2, gw_in, gw_out, gb_in, vecs,
                 h3, h3t, acc, dh3, act, dpre, tf=512):
    L, D = x2.shape
    FF = w_in.shape[1]
    gb_out = jnp.zeros((1, D), F32)
    for r in range(0, L, ROWS):
        rs = pl.ds(r, ROWS)
        n, _ = norm_parts(x2[rs])
        h = n * gains[2:3] + shifts[2:3]
        h3[rs] = h.astype(B16)
        h3t[:, r : r + ROWS] = h.T.astype(B16)
        acc[rs] = x2[rs] + b_out[...]
        dh3[rs] = jnp.zeros((ROWS, D), F32)
        gb_out += jnp.sum(cot[rs].astype(F32), 0, keepdims=True)
    vecs[2:3] = gb_out

    def tile(f, _):
        fs = pl.ds(pl.multiple_of(f * tf, tf), tf)
        gb = jnp.zeros((1, tf), F32)
        for r in range(0, L, ROWS):
            rs = pl.ds(r, ROWS)
            pre = dot(h3[rs], w_in[:, fs]) + b_in[:, fs]
            up, slope = gelu_parts(pre)
            act[rs] = up.astype(B16)
            acc[rs] += dot(act[rs], w_out[fs])
            d = (dot_nt(cot[rs], w_out[fs]) * slope).astype(B16)
            dpre[rs] = d
            gb += jnp.sum(d.astype(F32), 0, keepdims=True)
            dh3[rs] += dot_nt(d, w_in[:, fs])
        gb_in[:, fs] = gb
        gw_out[fs] = dot_tn(act[...], cot[...]).astype(B16)
        gw_in[:, fs] = dot(h3t[...], dpre[...]).astype(B16)
        return 0

    lax.fori_loop(0, FF // tf, tile, 0)
    sg = jnp.zeros((1, D), F32)
    sb = jnp.zeros((1, D), F32)
    for r in range(0, L, ROWS):
        rs = pl.ds(r, ROWS)
        mixed[rs] = acc[rs].astype(B16)
        dx, a, b = norm_back(dh3[rs], x2[rs], gains[2:3])
        g2[rs] = cot[rs].astype(F32) + dx
        sg += a
        sb += b
    vecs[0:1] = sg
    vecs[1:2] = sb


def cross_backward(mlen, flag, g2, x1, mem, gains, w, proj, h2, cq, ckv, c, lse,
                   g1, gmem, gw, gproj, vecs,
                   gc, dc, dcq, dck, dcv, dh2, qt, kt, at, dat, ps, dss, qm, dm, dqt, dk_acc, dv_acc):
    L, D = x1.shape
    f = flag[0].astype(F32)
    for r in range(0, L, ROWS):
        rs = pl.ds(r, ROWS)
        gcr = (f * g2[rs]).astype(B16)
        gc[rs] = gcr
        dc[rs] = dot_nt(gcr, proj[...]).astype(B16)
        dh2[rs] = jnp.zeros((ROWS, D), F32)
    gmem[...] = jnp.zeros_like(gmem)

    def gproj_tile(t, _):
        gproj[cols(t)] = dot_tn(c[:, cols(t)], gc[...]).astype(B16)
        return 0

    lax.fori_loop(0, D // GROUP, gproj_tile, 0)

    def group(g, _):
        attend_back_group(cq, ckv, ckv, (g,), (0, g), (1, g), c, dc, g, lse, mlen[0], False, 256,
                          qt, kt, at, dat, ps, dss, qm, dm, dqt, dk_acc, dv_acc)
        dcq[...] = dqt[...].T.astype(B16)
        dck[...] = dk_acc[...].astype(B16)
        dcv[...] = dv_acc[...].astype(B16)
        gw[0, :, cols(g)] = dot_tn(h2[...], dcq[...]).astype(B16)
        gw[1, :, cols(g)] = dot_tn(mem[...], dck[...]).astype(B16)
        gw[2, :, cols(g)] = dot_tn(mem[...], dcv[...]).astype(B16)
        dh2[...] += dot_nt(dcq[...], w[0, :, cols(g)])
        gmem[...] += dot_nt(dck[...], w[1, :, cols(g)]) + dot_nt(dcv[...], w[2, :, cols(g)])
        return 0

    lax.fori_loop(0, D // GROUP, group, 0)
    sg = jnp.zeros((1, D), F32)
    sb = jnp.zeros((1, D), F32)
    for r in range(0, L, ROWS):
        rs = pl.ds(r, ROWS)
        dx, a, b = norm_back(dh2[rs], x1[rs], gains[1:2])
        g1[rs] = g2[rs] + dx
        sg += a
        sb += b
    vecs[0:1] = sg
    vecs[1:2] = sb


def self_backward(tlen, g1, tokens, gains, w, proj, h1, qkv, a, lse,
                  gtok, gw, gproj, vecs,
                  ga, da, dq, dk, dv, dh1, qt, kt, at, dat, ps, dss, qm, dm, dqt, dk_acc, dv_acc):
    L, D = tokens.shape
    for r in range(0, L, ROWS):
        rs = pl.ds(r, ROWS)
        gar = g1[rs].astype(B16)
        ga[rs] = gar
        da[rs] = dot_nt(gar, proj[...]).astype(B16)
        dh1[rs] = jnp.zeros((ROWS, D), F32)

    def gproj_tile(t, _):
        gproj[cols(t)] = dot_tn(a[:, cols(t)], ga[...]).astype(B16)
        return 0

    lax.fori_loop(0, D // GROUP, gproj_tile, 0)

    def group(g, _):
        attend_back_group(qkv, qkv, qkv, (0, g), (1, g), (2, g), a, da, g, lse, tlen[0], True, 256,
                          qt, kt, at, dat, ps, dss, qm, dm, dqt, dk_acc, dv_acc)
        dq[...] = dqt[...].T.astype(B16)
        dk[...] = dk_acc[...].astype(B16)
        dv[...] = dv_acc[...].astype(B16)
        for k, d in enumerate((dq, dk, dv)):
            gw[k, :, cols(g)] = dot_tn(h1[...], d[...]).astype(B16)
            dh1[...] += dot_nt(d[...], w[k, :, cols(g)])
        return 0

    lax.fori_loop(0, D // GROUP, group, 0)
    sg = jnp.zeros((1, D), F32)
    sb = jnp.zeros((1, D), F32)
    for r in range(0, L, ROWS):
        rs = pl.ds(r, ROWS)
        dx, x, b = norm_back(dh1[rs], tokens[rs].astype(F32), gains[0:1])
        gtok[rs] = (g1[rs] + dx).astype(gtok.dtype)
        sg += x
        sb += b
    vecs[0:1] = sg
    vecs[1:2] = sb


VMEM = pltpu.VMEM
SMEM_SPEC = pl.BlockSpec(memory_space=pltpu.SMEM)
VMEM_SPEC = pl.BlockSpec(memory_space=pltpu.VMEM)


def call(kernel, scalars, arrays, outs, scratch, name):
    return pl.pallas_call(
        kernel,
        out_shape=[jax.ShapeDtypeStruct(s, d) for s, d in outs],
        in_specs=[SMEM_SPEC] * len(scalars) + [VMEM_SPEC] * len(arrays),
        out_specs=[VMEM_SPEC] * len(outs),
        scratch_shapes=[VMEM(s, d) for s, d in scratch],
        compiler_params=pltpu.CompilerParams(vmem_limit_bytes=60 * 1024 * 1024),
        name=name,
    )(*scalars, *arrays)


def back_scratch(L, K):
    return [
        ((GROUP, L), B16), ((GROUP, K), B16), ((GROUP, L), F32), ((GROUP, L), B16),
        ((K, PER * 256), B16), ((K, PER * 256), B16), ((PER * 256, GROUP), B16), ((PER * 256, GROUP), B16),
        ((GROUP, L), F32), ((K, GROUP), F32), ((K, GROUP), F32),
    ]


def layer(tokens, memory, cot, tlen, mlen, flag, self_w, self_proj, cross_w, cross_proj, w_in, w_out, b_in, b_out, gains, shifts):
    L, D = tokens.shape
    M = memory.shape[0]
    FF = w_in.shape[1]
    G = D // GROUP
    h1, qkv, a, lse, x1 = call(
        self_forward, (tlen,), (tokens, gains, shifts, self_w, self_proj),
        [((L, D), B16), ((3, G, L, GROUP), B16), ((L, D), B16), ((G, 8, L), F32), ((L, D), F32)],
        [((GROUP, L), B16)] * 3, "self_forward")
    h2, cq, ckv, c, clse, x2 = call(
        cross_forward, (mlen, flag), (x1, memory, gains, shifts, cross_w, cross_proj),
        [((L, D), B16), ((G, L, GROUP), B16), ((2, G, M, GROUP), B16), ((L, D), B16), ((G, 8, L), F32), ((L, D), F32)],
        [((GROUP, L), B16), ((GROUP, M), B16), ((GROUP, L), B16)], "cross_forward")
    mixed, g2, gw_in, gw_out, gb_in, v2 = call(
        feed_forward, (), (x2, cot, gains, shifts, w_in, w_out, b_in, b_out),
        [((L, D), B16), ((L, D), F32), ((D, FF), B16), ((FF, D), B16), ((1, FF), F32), ((8, D), F32)],
        [((L, D), B16), ((D, L), B16), ((L, D), F32), ((L, D), F32), ((L, 512), B16), ((L, 512), B16)], "feed_forward")
    g1, gmem, gcw, gcproj, v1 = call(
        cross_backward, (mlen, flag), (g2, x1, memory, gains, cross_w, cross_proj, h2, cq, ckv, c, clse),
        [((L, D), F32), ((M, D), F32), ((3, D, D), B16), ((D, D), B16), ((8, D), F32)],
        [((L, D), B16), ((L, D), B16), ((L, GROUP), B16), ((M, GROUP), B16), ((M, GROUP), B16), ((L, D), F32)]
        + back_scratch(L, M), "cross_backward")
    gtok, gsw, gsproj, v0 = call(
        self_backward, (tlen,), (g1, tokens, gains, self_w, self_proj, h1, qkv, a, lse),
        [((L, D), B16), ((3, D, D), B16), ((D, D), B16), ((8, D), F32)],
        [((L, D), B16), ((L, D), B16), ((L, GROUP), B16), ((L, GROUP), B16), ((L, GROUP), B16), ((L, D), F32)]
        + back_scratch(L, L), "self_backward")
    gain_grads = jnp.concatenate([v0[0:1], v1[0:1], v2[0:1]])
    shift_grads = jnp.concatenate([v0[1:2], v1[1:2], v2[1:2]])
    return mixed, gtok, gmem, gsw, gsproj, gcw, gcproj, gw_in, gw_out, gb_in, v2[2], gain_grads, shift_grads


def layer_norm(values, gain, shift):
    centre = values - jnp.mean(values, -1, keepdims=True)
    spread = jnp.mean(centre * centre, -1, keepdims=True)
    return centre * lax.rsqrt(spread + EPSILON) * gain + shift


def gelu_exact(values):
    return jax.nn.gelu(values, approximate=False)


def split_heads(values):
    return values.reshape(values.shape[0], values.shape[1], -1, HEAD).transpose(2, 0, 1, 3)


def merge_heads(values):
    return values.transpose(1, 2, 0, 3).reshape(values.shape[1], values.shape[2], -1)


def head_scores(query_matrix, key_matrix, allowed):
    logit_scores = jnp.einsum(
        "cti,cvi->ctv", query_matrix, key_matrix, preferred_element_type=jnp.float32
    ) * HEAD ** (-0.5)
    return jnp.where(allowed, logit_scores, -1000000000.0)


def attend(query_matrix, key_matrix, values, allowed):

    def one_head(parts):
        head_query_rows, head_key_rows, head_value_rows = parts
        logit_scores = head_scores(head_query_rows, head_key_rows, allowed)
        row_max = jnp.max(logit_scores, -1, keepdims=True)
        expo = jnp.exp(logit_scores - row_max)
        row_sum = jnp.sum(expo, -1, keepdims=True)
        reduced_probabilities = (expo / row_sum).astype(jnp.bfloat16)
        attention_output = jnp.einsum(
            "zqf,zfm->zqm",
            reduced_probabilities,
            head_value_rows,
            preferred_element_type=jnp.float32,
        )
        return (attention_output, row_max, row_sum)

    attention_output, row_max, row_sum = lax.map(
        one_head, (split_heads(query_matrix), split_heads(key_matrix), split_heads(values))
    )
    return (merge_heads(attention_output).astype(jnp.bfloat16), row_max, row_sum)


def attend_back(query_matrix, key_matrix, values, allowed, row_max, row_sum, grad_out):

    def one_head(parts):
        (
            head_query_rows,
            head_key_rows,
            head_value_rows,
            head_output_gradient,
            head_max,
            head_sum,
        ) = parts
        logit_scores = head_scores(head_query_rows, head_key_rows, allowed)
        probs = jnp.exp(logit_scores - head_max) / head_sum
        reduced_probabilities = probs.astype(jnp.bfloat16)
        probs_gradient = jnp.einsum(
            "cti,cvi->ctv",
            head_output_gradient,
            head_value_rows,
            preferred_element_type=jnp.float32,
        )
        delta_sum = jnp.sum(probs * probs_gradient, -1, keepdims=True)
        scores_gradient = (probs * (probs_gradient - delta_sum)).astype(jnp.bfloat16)
        d_query = jnp.einsum(
            "zqf,zfm->zqm", scores_gradient, head_key_rows, preferred_element_type=jnp.float32
        ) * HEAD ** (-0.5)
        d_keys = jnp.einsum(
            "pum,pug->pmg", scores_gradient, head_query_rows, preferred_element_type=jnp.float32
        ) * HEAD ** (-0.5)
        values_gradient = jnp.einsum(
            "pum,pug->pmg",
            reduced_probabilities,
            head_output_gradient,
            preferred_element_type=jnp.float32,
        )
        return (d_query, d_keys, values_gradient)

    d_query, d_keys, values_gradient = lax.map(
        one_head,
        (
            split_heads(query_matrix),
            split_heads(key_matrix),
            split_heads(values),
            split_heads(grad_out),
            row_max,
            row_sum,
        ),
    )
    return (merge_heads(d_query), merge_heads(d_keys), merge_heads(values_gradient))


def general_body(
    tokens,
    memory,
    cotangent,
    text_len,
    mem_len,
    image_flag,
    self_qkv,
    self_out,
    cross_qkv,
    cross_out,
    w_in,
    w_out,
    b_in,
    b_out,
    norm_gain,
    norm_bias,
):
    f32 = jnp.float32
    b16 = jnp.bfloat16
    seq_count, own_rows, width = tokens.shape
    offset = lax.axis_index("mem") * own_rows
    gathered = (
        lax.all_gather(self_qkv, "fsdp", axis=1, tiled=True),
        lax.all_gather(self_out, "fsdp", axis=0, tiled=True),
        lax.all_gather(cross_qkv, "fsdp", axis=1, tiled=True),
        lax.all_gather(cross_out, "fsdp", axis=0, tiled=True),
        lax.all_gather(w_in, "fsdp", axis=0, tiled=True),
        lax.all_gather(w_out, "fsdp", axis=0, tiled=True),
        lax.all_gather(b_in, "fsdp", axis=0, tiled=True),
        lax.all_gather(b_out, "fsdp", axis=0, tiled=True),
        lax.all_gather(norm_gain, "fsdp", axis=1, tiled=True),
        lax.all_gather(norm_bias, "fsdp", axis=1, tiled=True),
    )
    (
        self_w,
        self_proj,
        cross_w,
        cross_proj,
        inner_w,
        outer_w,
        inner_bias,
        outer_bias,
        gains,
        shifts,
    ) = gathered
    gains = gains.astype(f32)
    shifts = shifts.astype(f32)
    x0 = tokens.astype(f32)
    h1_full, norm0_back = jax.vjp(layer_norm, x0, gains[0], shifts[0])
    h1 = h1_full.astype(b16)
    qkv = jnp.einsum("srd,kde->ksre", h1, self_w, preferred_element_type=f32).astype(b16)
    keys_all, values_all = (
        lax.all_gather(qkv[1], "mem", axis=1, tiled=True),
        lax.all_gather(qkv[2], "mem", axis=1, tiled=True),
    )
    key_pos = jnp.arange(keys_all.shape[1], dtype=jnp.int32)
    query_pos = offset + jnp.arange(own_rows, dtype=jnp.int32)
    self_mask = (key_pos[None, None, :] <= query_pos[None, :, None]) & (
        key_pos[None, None, :] < text_len[:, None, None]
    )
    attended, self_max, self_sum = attend(qkv[0], keys_all, values_all, self_mask)
    x1 = x0 + jnp.einsum("srd,de->sre", attended, self_proj, preferred_element_type=f32)
    h2_full, norm1_back = jax.vjp(layer_norm, x1, gains[1], shifts[1])
    h2 = h2_full.astype(b16)
    cross_q = jnp.einsum("srd,de->sre", h2, cross_w[0], preferred_element_type=f32).astype(b16)
    memory_all = lax.all_gather(memory, "mem", axis=1, tiled=True)
    cross_kv = jnp.einsum(
        "snd,kde->ksne", memory_all, cross_w[1:], preferred_element_type=f32
    ).astype(b16)
    cross_keys, cross_values = (cross_kv[0], cross_kv[1])
    mem_pos = jnp.arange(cross_keys.shape[1], dtype=jnp.int32)
    cross_mask = mem_pos[None, None, :] < mem_len[:, None, None]
    crossed, cross_max, cross_sum = attend(cross_q, cross_keys, cross_values, cross_mask)
    flag = image_flag.astype(f32)[:, None, None]
    x2 = x1 + jnp.einsum("srd,de->sre", crossed, cross_proj, preferred_element_type=f32) * flag
    h3_full, norm2_back = jax.vjp(layer_norm, x2, gains[2], shifts[2])
    h3 = h3_full.astype(b16)
    pre = jnp.einsum("srd,df->srf", h3, inner_w, preferred_element_type=f32) + inner_bias.astype(
        f32
    )
    act_full, gelu_back = jax.vjp(gelu_exact, pre)
    act_low = act_full.astype(b16)
    attention_output = (
        x2
        + jnp.einsum("srf,fd->srd", act_low, outer_w, preferred_element_type=f32)
        + outer_bias.astype(f32)
    )
    mixed = attention_output.astype(b16)
    grad_top = cotangent.astype(f32)
    grad_low = grad_top.astype(b16)
    grad_outer_bias = jnp.sum(grad_low.astype(f32), (0, 1))
    grad_outer = jnp.einsum("srf,srd->fd", act_low, grad_low, preferred_element_type=f32)
    d_act = jnp.einsum("srd,fd->srf", grad_low, outer_w, preferred_element_type=f32)
    d_pre = gelu_back(d_act)[0].astype(b16)
    grad_inner_bias = jnp.sum(d_pre.astype(f32), (0, 1))
    grad_inner = jnp.einsum("srd,srf->df", h3, d_pre, preferred_element_type=f32)
    d_h3 = jnp.einsum("srf,df->srd", d_pre, inner_w, preferred_element_type=f32)
    d_x2, gain_two, shift_two = norm2_back(d_h3)
    grad_two = grad_top + d_x2
    grad_cross = (grad_two * flag).astype(b16)
    grad_cross_proj = jnp.einsum("srd,sre->de", crossed, grad_cross, preferred_element_type=f32)
    d_crossed = jnp.einsum(
        "sre,de->srd", grad_cross, cross_proj, preferred_element_type=f32
    ).astype(b16)
    d_cross_q, d_cross_k, d_cross_v = attend_back(
        cross_q, cross_keys, cross_values, cross_mask, cross_max, cross_sum, d_crossed
    )
    own_cross_k, own_cross_v = (
        lax.psum_scatter(
            d_cross_k.astype(jnp.bfloat16), "mem", scatter_dimension=1, tiled=True
        ).astype(jnp.float32),
        lax.psum_scatter(
            d_cross_v.astype(jnp.bfloat16), "mem", scatter_dimension=1, tiled=True
        ).astype(jnp.float32),
    )
    d_cross_kv = jnp.stack([own_cross_k, own_cross_v]).astype(b16)
    grad_cross_kv = jnp.einsum("snd,ksne->kde", memory, d_cross_kv, preferred_element_type=f32)
    grad_memory = jnp.einsum("ksne,kde->snd", d_cross_kv, cross_w[1:], preferred_element_type=f32)
    d_cross_low = d_cross_q.astype(b16)
    grad_cross_q = jnp.einsum("srd,sre->de", h2, d_cross_low, preferred_element_type=f32)
    d_h2 = jnp.einsum("sre,de->srd", d_cross_low, cross_w[0], preferred_element_type=f32)
    d_x1, gain_one, shift_one = norm1_back(d_h2)
    grad_one = grad_two + d_x1
    grad_cross_w = jnp.concatenate([grad_cross_q[None], grad_cross_kv], 0)
    grad_one_low = grad_one.astype(b16)
    grad_self_proj = jnp.einsum("srd,sre->de", attended, grad_one_low, preferred_element_type=f32)
    d_attended = jnp.einsum(
        "sre,de->srd", grad_one_low, self_proj, preferred_element_type=f32
    ).astype(b16)
    d_query, d_keys, values_gradient = attend_back(
        qkv[0], keys_all, values_all, self_mask, self_max, self_sum, d_attended
    )
    own_keys, own_values = (
        lax.psum_scatter(
            d_keys.astype(jnp.bfloat16), "mem", scatter_dimension=1, tiled=True
        ).astype(jnp.float32),
        lax.psum_scatter(
            values_gradient.astype(jnp.bfloat16), "mem", scatter_dimension=1, tiled=True
        ).astype(jnp.float32),
    )
    d_qkv = jnp.stack([d_query, own_keys, own_values]).astype(b16)
    grad_self_w = jnp.einsum("srd,ksre->kde", h1, d_qkv, preferred_element_type=f32)
    d_h1 = jnp.einsum("ksre,kde->srd", d_qkv, self_w, preferred_element_type=f32)
    d_x0, gain_zero, shift_zero = norm0_back(d_h1)
    grad_tokens = grad_one + d_x0
    gain_grads = jnp.stack([gain_zero, gain_one, gain_two])
    shift_grads = jnp.stack([shift_zero, shift_one, shift_two])
    full_grads = (
        grad_self_w,
        grad_self_proj,
        grad_cross_w,
        grad_cross_proj,
        grad_inner,
        grad_outer,
        grad_inner_bias,
        grad_outer_bias,
        gain_grads,
        shift_grads,
    )
    shards = (
        lax.psum_scatter(
            full_grads[0].astype(jnp.bfloat16), "fsdp", scatter_dimension=1, tiled=True
        ).astype(jnp.float32),
        lax.psum_scatter(
            full_grads[1].astype(jnp.bfloat16), "fsdp", scatter_dimension=0, tiled=True
        ).astype(jnp.float32),
        lax.psum_scatter(
            full_grads[2].astype(jnp.bfloat16), "fsdp", scatter_dimension=1, tiled=True
        ).astype(jnp.float32),
        lax.psum_scatter(
            full_grads[3].astype(jnp.bfloat16), "fsdp", scatter_dimension=0, tiled=True
        ).astype(jnp.float32),
        lax.psum_scatter(
            full_grads[4].astype(jnp.bfloat16), "fsdp", scatter_dimension=0, tiled=True
        ).astype(jnp.float32),
        lax.psum_scatter(
            full_grads[5].astype(jnp.bfloat16), "fsdp", scatter_dimension=0, tiled=True
        ).astype(jnp.float32),
        lax.psum_scatter(
            full_grads[6].astype(jnp.bfloat16), "fsdp", scatter_dimension=0, tiled=True
        ).astype(jnp.float32),
        lax.psum_scatter(
            full_grads[7].astype(jnp.bfloat16), "fsdp", scatter_dimension=0, tiled=True
        ).astype(jnp.float32),
        lax.psum_scatter(
            full_grads[8].astype(jnp.bfloat16), "fsdp", scatter_dimension=1, tiled=True
        ).astype(jnp.float32),
        lax.psum_scatter(
            full_grads[9].astype(jnp.bfloat16), "fsdp", scatter_dimension=1, tiled=True
        ).astype(jnp.float32),
    )
    totals = (
        lax.psum(shards[0].astype(jnp.bfloat16), "mem").astype(jnp.float32),
        lax.psum(shards[1].astype(jnp.bfloat16), "mem").astype(jnp.float32),
        lax.psum(shards[2].astype(jnp.bfloat16), "mem").astype(jnp.float32),
        lax.psum(shards[3].astype(jnp.bfloat16), "mem").astype(jnp.float32),
        lax.psum(shards[4].astype(jnp.bfloat16), "mem").astype(jnp.float32),
        lax.psum(shards[5].astype(jnp.bfloat16), "mem").astype(jnp.float32),
        lax.psum(shards[6].astype(jnp.bfloat16), "mem").astype(jnp.float32),
        lax.psum(shards[7].astype(jnp.bfloat16), "mem").astype(jnp.float32),
        lax.psum(shards[8].astype(jnp.bfloat16), "mem").astype(jnp.float32),
        lax.psum(shards[9].astype(jnp.bfloat16), "mem").astype(jnp.float32),
    )
    return (
        mixed,
        grad_tokens,
        grad_memory,
        totals[0],
        totals[1],
        totals[2],
        totals[3],
        totals[4],
        totals[5],
        totals[6],
        totals[7],
        totals[8],
        totals[9],
    )


def paired_body(tokens, memory, cotangent, text_len, mem_len, image_flag, self_qkv, self_out, cross_qkv, cross_out,
                w_in, w_out, b_in, b_out, norm_gain, norm_bias):
    me = lax.axis_index("mem")

    def whole(v):
        return lax.all_to_all(v, "mem", 0, 1, tiled=True)[0]

    def gather(v, axis=0):
        return lax.all_gather(v, "fsdp", axis=axis, tiled=True)

    def mine(v):
        return lax.dynamic_slice(v, (me,), (1,))

    outs = layer(
        whole(tokens), whole(memory), whole(cotangent), mine(text_len), mine(mem_len), mine(image_flag),
        gather(self_qkv, 1), gather(self_out), gather(cross_qkv, 1), gather(cross_out), gather(w_in), gather(w_out),
        gather(b_in).astype(F32)[None], gather(b_out).astype(F32)[None],
        gather(norm_gain, 1).astype(F32), gather(norm_bias, 1).astype(F32))
    mixed, gtok, gmem = outs[:3]

    def back(v):
        return lax.all_to_all(v[None], "mem", 1, 0, tiled=True)

    def scatter(v, axis=0):
        part = lax.psum_scatter(v.astype(B16), "fsdp", scatter_dimension=axis, tiled=True)
        return lax.psum(part, "mem").astype(F32)

    gsw, gsp, gcw, gcp, gwi, gwo, gbi, gbo, gg, gs = outs[3:]
    return (back(mixed), back(gtok).astype(F32), back(gmem.astype(B16)).astype(F32),
            scatter(gsw, 1), scatter(gsp), scatter(gcw, 1), scatter(gcp), scatter(gwi), scatter(gwo),
            scatter(gbi[0]), scatter(gbo), scatter(gg, 1), scatter(gs, 1))


def body(*args):
    tokens = args[0]
    if lax.axis_size("mem") == tokens.shape[0] and tokens.shape[1] % 256 == 0:
        return paired_body(*args)
    return general_body(*args)


def solution(mesh):
    placed = (
        P("fsdp", "mem", None),
        P("fsdp", "mem", None),
        P("fsdp", "mem", None),
        P("fsdp"),
        P("fsdp"),
        P("fsdp"),
        P(None, "fsdp", None),
        P("fsdp", None),
        P(None, "fsdp", None),
        P("fsdp", None),
        P("fsdp", None),
        P("fsdp", None),
        P("fsdp"),
        P("fsdp"),
        P(None, "fsdp"),
        P(None, "fsdp"),
    )
    return jax.shard_map(
        body,
        mesh=mesh,
        in_specs=placed,
        out_specs=(
            P("fsdp", "mem", None),
            P("fsdp", "mem", None),
            P("fsdp", "mem", None),
            P(None, "fsdp", None),
            P("fsdp", None),
            P(None, "fsdp", None),
            P("fsdp", None),
            P("fsdp", None),
            P("fsdp", None),
            P("fsdp"),
            P("fsdp"),
            P(None, "fsdp"),
            P(None, "fsdp"),
        ),
        check_vma=False,
    )
```

```python
import jax
import jax.numpy as jnp
from jax import lax
from jax.experimental import pallas as pl
from jax.experimental.pallas import tpu as pltpu
from jax.sharding import PartitionSpec as P

F32 = jnp.float32
B16 = jnp.bfloat16
HEAD = 64
GROUP = 256
PER = GROUP // HEAD
EPSILON = 1e-05
NEG = -1000000000.0


def dot(a, b):
    return jnp.dot(a, b, preferred_element_type=F32)


def dot_nt(a, b):
    return lax.dot_general(a, b, (((1,), (1,)), ((), ())), preferred_element_type=F32)


def dot_tn(a, b):
    return lax.dot_general(a, b, (((0,), (0,)), ((), ())), preferred_element_type=F32)


def norm_parts(v):
    centre = v - jnp.mean(v, -1, keepdims=True)
    rs = lax.rsqrt(jnp.mean(centre * centre, -1, keepdims=True) + EPSILON)
    return centre * rs, rs


def norm_back(e, v, gain):
    n, rs = norm_parts(v)
    t = e * gain
    dx = rs * (t - jnp.mean(t, -1, keepdims=True) - n * jnp.mean(t * n, -1, keepdims=True))
    return dx, jnp.sum(e * n, 0, keepdims=True), jnp.sum(e, 0, keepdims=True)


def cols(g):
    return pl.ds(pl.multiple_of(g * GROUP, GROUP), GROUP)


def head_rows(h, rows, width):
    return lax.broadcasted_iota(jnp.int32, (rows, width), 0) // HEAD == h


def head_cols(h, rows, width):
    return lax.broadcasted_iota(jnp.int32, (rows, width), 1) // HEAD == h


def allowed_block(first_key, nk, first_query, nq, limit, causal):
    key = first_key + lax.broadcasted_iota(jnp.int32, (nk, nq), 0)
    ok = key < limit
    if causal:
        query = first_query + lax.broadcasted_iota(jnp.int32, (nk, nq), 1)
        ok = ok & (key <= query)
    return ok


def masked_scores(k_ref, kidx, qm, nk, q0, tq, limit, causal):
    s = dot(k_ref[kidx + (pl.ds(0, nk),)], qm)
    if causal and nk > tq:
        top = jnp.where(allowed_block(0, nk - tq, q0, tq, limit, False), s[: nk - tq], NEG)
        bottom = jnp.where(allowed_block(nk - tq, tq, q0, tq, limit, True), s[nk - tq :], NEG)
        return jnp.concatenate([top, bottom], 0)
    return jnp.where(allowed_block(nk - (tq if causal else nk), nk, q0, tq, limit, causal), s, NEG)


def attend_group(q_ref, k_ref, v_ref, qi_, ki_, vi_, out_ref, g, lse_ref, limit, causal, tq, qt, vt, ot, step=None):
    L = qt.shape[1]
    K = vt.shape[1]
    qt[...] = (q_ref[qi_].astype(F32) * HEAD**-0.5).T.astype(B16)
    vt[...] = v_ref[vi_].astype(F32).T.astype(B16)
    for i in range(L // tq):
        nk = (i + 1) * tq if causal else K
        for h in range(PER):
            block = qt[:, i * tq : (i + 1) * tq]
            qm = jnp.where(head_rows(h, GROUP, tq), block, jnp.zeros_like(block))
            s = masked_scores(k_ref, ki_, qm, nk, i * tq, tq, limit, causal)
            m = jnp.max(s, 0, keepdims=True)
            e = jnp.exp(s - m)
            total = jnp.sum(e, 0, keepdims=True)
            p = (e * (1.0 / total)).astype(B16)
            lse_ref[g, h : h + 1, i * tq : (i + 1) * tq] = m + jnp.log(total)
            o = dot(vt[h * HEAD : (h + 1) * HEAD, 0:nk], p)
            ot[h * HEAD : (h + 1) * HEAD, i * tq : (i + 1) * tq] = o.astype(B16)
        if step is not None:
            step(i)
    out_ref[:, cols(g)] = ot[...].astype(F32).T.astype(B16)


def attend_back_group(
    q_ref, k_ref, v_ref, qi_, ki_, vi_, a_ref, da_ref, g, lse_ref, limit, causal, tq,
    qt, kt, at, dat, ps, dss, qm_ref, dm_ref, dqt, dk_acc, dv_acc, step=None,
):
    L = qt.shape[1]
    K = kt.shape[1]
    scale = HEAD**-0.5
    qt[...] = (q_ref[qi_].astype(F32) * scale).T.astype(B16)
    kt[...] = (k_ref[ki_].astype(F32) * scale).T.astype(B16)
    at[...] = a_ref[:, cols(g)].astype(F32).T.astype(B16)
    dat[...] = da_ref[:, cols(g)].astype(F32).T.astype(B16)
    if causal:
        dk_acc[...] = jnp.zeros_like(dk_acc)
        dv_acc[...] = jnp.zeros_like(dv_acc)
    for i in range(L // tq):
        nk = (i + 1) * tq if causal else K
        span = slice(i * tq, (i + 1) * tq)
        qn = q_ref[qi_ + (pl.ds(i * tq, tq),)] * jnp.asarray(scale, B16)
        dn = da_ref[pl.ds(i * tq, tq), cols(g)]
        for h in range(PER):
            hs = slice(h * HEAD, (h + 1) * HEAD)
            here = head_rows(h, GROUP, tq)
            block = qt[:, span]
            qm = jnp.where(here, block, jnp.zeros_like(block))
            block = dat[:, span]
            dm = jnp.where(here, block, jnp.zeros_like(block))
            delta = jnp.sum(at[hs, span].astype(F32) * dat[hs, span].astype(F32), 0, keepdims=True)
            s = masked_scores(k_ref, ki_, qm, nk, i * tq, tq, limit, causal)
            p = jnp.exp(s - lse_ref[g, h : h + 1, span])
            dp = dot(v_ref[vi_ + (pl.ds(0, nk),)], dm)
            ds = (p * (dp - delta)).astype(B16)
            ps[0:nk, h * tq : (h + 1) * tq] = p.astype(B16)
            dss[0:nk, h * tq : (h + 1) * tq] = ds
            dqt[hs, span] = dot(kt[hs, 0:nk], ds).astype(B16)
            mine = head_cols(h, tq, GROUP)
            qm_ref[h * tq : (h + 1) * tq] = jnp.where(mine, qn, jnp.zeros_like(qn))
            dm_ref[h * tq : (h + 1) * tq] = jnp.where(mine, dn, jnp.zeros_like(dn))
        dvi = dot(ps[0:nk], dm_ref[...])
        dki = dot(dss[0:nk], qm_ref[...])
        if causal:
            dv_acc[0:nk] += dvi
            dk_acc[0:nk] += dki
        elif i == 0:
            dv_acc[...] = dvi
            dk_acc[...] = dki
        else:
            dv_acc[...] += dvi
            dk_acc[...] += dki
        if step is not None:
            step(i)


ERFCX = (
    0.21161358920977177, 0.2106475215974073, 0.20533035663075158, 0.12143152976148842,
    0.27391662866419597, -0.22972237163936396, 0.432698311257476, -0.287490481514182,
    0.06157492612604076,
)


def gelu_parts(u):
    z = jnp.abs(u) * 0.7071067811865476
    t = 1.0 / (1.0 + 0.375 * z)
    poly = jnp.full_like(t, ERFCX[8])
    for c in ERFCX[7::-1]:
        poly = poly * t + c
    bell = jnp.exp(-0.5 * u * u)
    half = 0.5 * (poly * t) * bell
    cdf = jnp.where(u >= 0, 1.0 - half, half)
    return u * cdf, cdf + u * (bell * 0.3989422804014327)


ROWS = 256

VMEM = pltpu.VMEM
SMEM_SPEC = pl.BlockSpec(memory_space=pltpu.SMEM)


MESH = pl.DeviceIdType.MESH
NZ, NY, NC = 4, 2, 2
ANY_SPEC = pl.BlockSpec(memory_space=pl.ANY)
DMA = pltpu.SemaphoreType.DMA
SMALL = 16


class Place:
    def __init__(self):
        i = lax.axis_index("fsdp")
        self.x = lax.axis_index("mem")
        self.i = i
        self.z, self.y, self.c = i // (NY * NC), (i // NC) % NY, i % NC
        self.other_x, self.other_y, self.other_c = 1 - self.x, 1 - self.y, 1 - self.c

    def at_z(self, z):
        return (self.x, (z * NY + self.y) * NC + self.c)

    def ahead(self, r):
        return lax.rem(self.z + r, NZ)

    def behind(self, r):
        return lax.rem(self.z + NZ - r, NZ)

    def peer_y(self):
        return (self.x, (self.z * NY + self.other_y) * NC + self.c)

    def peer_c(self):
        return (self.x, (self.z * NY + self.y) * NC + self.other_c)

    def peer_x(self):
        return (self.other_x, self.i)

    def greet(self):
        barrier = pltpu.get_barrier_semaphore()
        peers = [self.at_z(self.ahead(r)) for r in (1, 2, 3)] + [self.peer_y(), self.peer_c(), self.peer_x()]
        for peer in peers:
            pl.semaphore_signal(barrier, inc=1, device_id=peer, device_id_type=MESH)
        pl.semaphore_wait(barrier, len(peers))


def remote(src, dst, sems, index, peer):
    return pltpu.make_async_remote_copy(
        src_ref=src, dst_ref=dst, send_sem=sems.at[(0,) + index], recv_sem=sems.at[(1,) + index],
        device_id=peer, device_id_type=MESH)


class Gather:
    def __init__(self, place, ref, zsem, ysem, csem):
        self.p, self.ref, self.zsem, self.ysem, self.csem = place, ref, zsem, ysem, csem

    def block(self, lead, z):
        return self.ref.at[lead + (z, self.p.y, self.p.c)]

    def z_send(self, lead, r):
        mine = self.block(lead, self.p.z)
        return remote(mine, mine, self.zsem, lead + (r - 1,), self.p.at_z(self.p.ahead(r)))

    def z_land(self, lead, r):
        slot = self.block(lead, self.p.behind(r))
        return remote(slot, slot, self.zsem, lead + (r - 1,), self.p.at_z(self.p.behind(r)))

    def column(self, lead, y, c):
        return self.ref.at[lead + (slice(None), y, c)]

    def y_copy(self, lead, y):
        part = self.column(lead, y, self.p.c)
        return remote(part, part, self.ysem, lead, self.p.peer_y())

    def c_copy(self, lead, k, y, c):
        part = self.column(lead, y, c)
        return remote(part, part, self.csem, lead + (k,), self.p.peer_c())

    def begin(self, lead):
        for r in (1, 2, 3):
            self.z_send(lead, r).start()

    def spread(self, lead):
        for r in (1, 2, 3):
            self.z_land(lead, r).wait_recv()
        self.y_copy(lead, self.p.y).start()
        self.c_copy(lead, 0, self.p.y, self.p.c).start()

    def finish(self, lead):
        self.y_copy(lead, self.p.other_y).wait_recv()
        self.c_copy(lead, 1, self.p.other_y, self.p.c).start()

    def ready(self, lead):
        self.c_copy(lead, 0, self.p.y, self.p.other_c).wait_recv()
        self.c_copy(lead, 1, self.p.other_y, self.p.other_c).wait_recv()

    def sent(self, lead):
        for r in (1, 2, 3):
            self.z_send(lead, r).wait_send()
        self.y_copy(lead, self.p.y).wait_send()
        self.c_copy(lead, 0, self.p.y, self.p.c).wait_send()
        self.c_copy(lead, 1, self.p.other_y, self.p.c).wait_send()


class GatherIn(Gather):
    def tile(self, z, r):
        return lax.rem(z + r, NZ)

    def begin(self, r):
        for d in (1, 2, 3):
            self.send(r, d).start()

    def send(self, r, d):
        to = self.p.ahead(d)
        mine = self.block((self.tile(to, r),), self.p.z)
        return remote(mine, mine, self.zsem, (r, d - 1), self.p.at_z(to))

    def lead(self, r):
        return (self.tile(self.p.z, r),)

    def y_in(self, r, y):
        part = self.column(self.lead(r), y, self.p.c)
        return remote(part, part, self.ysem, (r,), self.p.peer_y())

    def c_in(self, r, k, y, c):
        part = self.column(self.lead(r), y, c)
        return remote(part, part, self.csem, (r, k), self.p.peer_c())

    def spread(self, r):
        for d in (1, 2, 3):
            slot = self.block(self.lead(r), self.p.behind(d))
            remote(slot, slot, self.zsem, (r, d - 1), self.p.at_z(self.p.behind(d))).wait_recv()
        self.y_in(r, self.p.y).start()
        self.c_in(r, 0, self.p.y, self.p.c).start()

    def finish(self, r):
        self.y_in(r, self.p.other_y).wait_recv()
        self.c_in(r, 1, self.p.other_y, self.p.c).start()

    def ready(self, r):
        self.c_in(r, 0, self.p.y, self.p.other_c).wait_recv()
        self.c_in(r, 1, self.p.other_y, self.p.other_c).wait_recv()

    def sent(self, r):
        for d in (1, 2, 3):
            self.send(r, d).wait_send()
        self.y_in(r, self.p.y).wait_send()
        self.c_in(r, 0, self.p.y, self.p.c).wait_send()
        self.c_in(r, 1, self.p.other_y, self.p.c).wait_send()


class GatherOut(GatherIn):
    def begin(self, r):
        self.send(r).start()

    def send(self, r):
        mine = self.ref.at[self.p.z, self.p.y, self.p.c]
        return remote(mine, mine, self.zsem, (r,), self.p.at_z(self.p.behind(r)))

    def column(self, lead, y, c):
        return self.ref.at[lead + (y, c)]

    def spread(self, r, landed=True):
        if landed:
            slot = self.ref.at[self.p.ahead(r), self.p.y, self.p.c]
            remote(slot, slot, self.zsem, (r,), self.p.at_z(self.p.ahead(r))).wait_recv()
        self.y_in(r, self.p.y).start()
        self.c_in(r, 0, self.p.y, self.p.c).start()

    def sent(self, r, began=True):
        if began:
            self.send(r).wait_send()
        self.y_in(r, self.p.y).wait_send()
        self.c_in(r, 0, self.p.y, self.p.c).wait_send()
        self.c_in(r, 1, self.p.other_y, self.p.c).wait_send()


def unpack_small(v):
    n = NZ * NY * NC
    D = 48 * n
    total = jnp.zeros((8, D), F32)
    tiles = jnp.zeros((8, D), F32)
    lane = lax.broadcasted_iota(jnp.int32, (8, 256), 1)
    row = lax.broadcasted_iota(jnp.int32, (8, D), 0)
    for i in range(n):
        block = v[i // 4, (i // 2) % 2, i % 2]
        pad = jnp.zeros((8, D - 256), F32)
        total = total + roll_lanes(jnp.concatenate([jnp.where(lane < 48, block, 0.0), pad], 1), 48 * i)
        wide = roll_lanes(jnp.concatenate([jnp.where(lane < 192, block, 0.0), pad], 1), 192 * (i % 4))
        tiles = tiles + jnp.where(row == i // 4, jnp.broadcast_to(wide[7:8], wide.shape), 0.0)
    return jnp.concatenate([total, tiles], 0)


def roll_lanes(v, by):
    return pltpu.roll(v, by, 1) if by else v


def flat(v):
    return v.reshape(-1, v.shape[-1])


def forward_kernel(
    tlen, mlen, flag, tokens_h, memory_h, cot_h, sw_h, sp_h, cw_h, cp_h, wi_h, wo_h, small_h,
    mixed_h, tok_h, h1_h, qkv_h, a_h, lse_h, x1_h, mem_h, h2_h, cq_h, ckv_h, c_h, clse_h, g2_h, w_h, s1i_h, s1o_h, vecs_h, gbi_h, gains_h,
    W, WI, WO, V, tok, mem, cot, vec, h1, qkv, a, lse, x1, h2, ckv, clse, x2, h3t, acc, dh3, gwi, gwo, rci, rco,
    qt, vt, vtc, ot, gbi, vout,
    wz, wy, wc, iz, iy, ic, oz, oy, oc, vz, vy, vc, xs, rs_sem, loc, spill_sem,
):
    p = Place()
    L, D = tok.shape
    half = L // 2
    M = mem.shape[0]
    FT = WI.shape[-1]
    local = []

    def fetch(src, dst):
        cp = pltpu.make_async_copy(src, dst, loc.at[len(local)])
        cp.start()
        local.append(cp)
        return cp

    me = (p.z, p.y, p.c)
    small_cp = fetch(small_h, V.at[me])
    pieces = [[] for _ in range(8)]
    for g in range(3):
        for k in range(3):
            pieces[g].append(fetch(sw_h.at[k, :, pl.ds(g * GROUP, GROUP)], W.at[(g,) + me + (slice(None), pl.ds(k * GROUP, GROUP))]))
    tok_cp = fetch(tokens_h.at[p.x], tok.at[pl.ds(pl.multiple_of(p.x * half, half), half)])
    pieces[3].append(fetch(sp_h, W.at[(3,) + me]))
    for g in range(3):
        for k in range(3):
            pieces[4 + g].append(fetch(cw_h.at[k, :, pl.ds(g * GROUP, GROUP)], W.at[(4 + g,) + me + (slice(None), pl.ds(k * GROUP, GROUP))]))
    pieces[7].append(fetch(cp_h, W.at[(7,) + me]))
    mem_cp = fetch(memory_h.at[p.x], mem.at[pl.ds(pl.multiple_of(p.x * (M // 2), M // 2), M // 2)])
    in_cp = [fetch(wi_h.at[:, pl.ds(t * FT, FT)], WI.at[(t,) + me]) for t in range(NZ)]
    out_cp = fetch(wo_h, WO.at[me])
    cot_cp = fetch(cot_h.at[p.x], cot.at[pl.ds(pl.multiple_of(p.x * half, half), half)])

    p.greet()
    gw = Gather(p, W, wz, wy, wc)
    gi = GatherIn(p, WI, iz, iy, ic)
    go = GatherOut(p, WO, oz, oy, oc)
    gv = Gather(p, V, vz, vy, vc)

    def x_part(src_h, dst, rows, k):
        send = remote(src_h.at[p.other_x], dst.at[pl.ds(pl.multiple_of(p.x * rows, rows), rows)], xs, (k,), p.peer_x())
        land = dst.at[pl.ds(pl.multiple_of(p.other_x * rows, rows), rows)]
        return send, remote(src_h.at[p.other_x], land, xs, (k,), p.peer_x())

    tok_send, tok_land = x_part(tokens_h, tok, half, 0)
    mem_send, mem_land = x_part(memory_h, mem, M // 2, 1)
    cot_send, cot_land = x_part(cot_h, cot, half, 2)
    small_cp.wait()
    gv.begin(())
    tok_send.start()
    for n in range(8):
        for cp in pieces[n]:
            cp.wait()
        if n < 2:
            gw.begin((n,))
    gv.spread(())
    gv.finish(())
    gv.ready(())
    vec[...] = unpack_small(V)
    gains, shifts = vec, vec
    GAIN, SHIFT, BOUT, BIN = 0, 3, 6, 8

    def norm_rows(src, dst, k, start, count):
        for r in range(0, count, ROWS):
            rs = pl.ds(pl.multiple_of(start + r, ROWS), ROWS)
            n, _ = norm_parts(src[rs].astype(F32))
            dst[rs] = (n * gains[GAIN + k : GAIN + k + 1] + shifts[SHIFT + k : SHIFT + k + 1]).astype(B16)

    tok_cp.wait()
    norm_rows(tok, h1, 0, p.x * half, half)
    gw.spread((0,))
    gw.begin((2,))
    mem_cp.wait()
    tok_land.wait_recv()
    mem_send.start()
    norm_rows(tok, h1, 0, p.other_x * half, half)
    gw.spread((1,))
    gw.begin((3,))
    gw.finish((0,))
    for cp in in_cp + [out_cp, cot_cp]:
        cp.wait()

    spills = []

    def spill(src, dst):
        cp = pltpu.make_async_copy(src, dst, spill_sem.at[len(spills)])
        cp.start()
        spills.append(cp)
        return cp

    tok_spill = spill(tok, tok_h)
    h1_spill = spill(h1, h1_h)

    def tick(n):
        gw.spread((n,))

        @pl.when(n + 2 < 8)
        def _():
            gw.begin((n + 2,))

        gw.finish((n - 1,))

    def self_group(g, _):
        gw.ready((g,))
        for r in range(0, L, ROWS):
            rs = pl.ds(r, ROWS)
            out = dot(h1[rs], flat(W[g])).astype(B16)
            for k in range(3):
                qkv[k, g, rs] = out[:, k * GROUP : (k + 1) * GROUP]

        def step(i):
            if i in (1, 3):
                tick(2 + 2 * g + i // 2)

        attend_group(qkv, qkv, qkv, (0, g), (1, g), (2, g), a, g, lse, tlen[p.x], True, 256, qt, vt, ot, step)
        return 0

    lax.fori_loop(0, 3, self_group, 0)
    gi.begin(0)
    qkv_spill = spill(qkv, qkv_h)
    a_spill = spill(a, a_h)
    spill(lse, lse_h)
    mem_land.wait_recv()
    spill(mem, mem_h)
    cot_send.start()
    gw.ready((3,))
    for r in range(0, L, ROWS):
        rs = pl.ds(r, ROWS)
        x1[rs] = tok[rs].astype(F32) + dot(a[rs], flat(W[3]))
        norm_rows(x1, h2, 1, r, ROWS)
    spill(x1, x1_h)
    h2_spill = spill(h2, h2_h)
    gw.finish((7,))
    gi.spread(0)
    go.spread(0, False)
    gi.begin(1)
    go.begin(1)

    tok_spill.wait()
    qkv_spill.wait()
    c = tok
    cq = qkv.at[0]

    def cross_group(g, _):
        gw.ready((4 + g,))
        for r in range(0, L, ROWS):
            rs = pl.ds(r, ROWS)
            cq[g, rs] = dot(h2[rs], flat(W[4 + g, :, :, :, :, 0:GROUP])).astype(B16)
        kv = dot(mem[...], flat(W[4 + g, :, :, :, :, GROUP : 3 * GROUP])).astype(B16)
        ckv[0, g] = kv[:, :GROUP]
        ckv[1, g] = kv[:, GROUP:]

        def step(i):
            pass

        attend_group(cq, ckv, ckv, (g,), (0, g), (1, g), c, g, clse, mlen[p.x], False, 256, qt, vtc, ot, step)
        return 0

    lax.fori_loop(0, 3, cross_group, 0)
    gi.finish(0)
    go.finish(0)
    spill(cq, cq_h)
    spill(ckv, ckv_h)
    spill(c, c_h)
    spill(clse, clse_h)
    gw.ready((7,))
    f = flag[p.x].astype(F32)
    h1_spill.wait()
    a_spill.wait()
    h2_spill.wait()
    h3, act, dpre = h1, h2, a
    for r in range(0, L, ROWS):
        rs = pl.ds(r, ROWS)
        x2[rs] = x1[rs] + f * dot(c[rs], flat(W[7]))
        n, _ = norm_parts(x2[rs])
        h = n * gains[GAIN + 2 : GAIN + 3] + shifts[SHIFT + 2 : SHIFT + 3]
        h3[rs] = h.astype(B16)
        h3t[:, r : r + ROWS] = h.T.astype(B16)
        acc[rs] = x2[rs] + vec[BOUT : BOUT + 1]
        dh3[rs] = jnp.zeros((ROWS, D), F32)
    spill(W, w_h)
    cot_land.wait_recv()
    gb_out = jnp.zeros((1, D), F32)
    for r in range(0, L, ROWS):
        gb_out += jnp.sum(cot[pl.ds(r, ROWS)].astype(F32), 0, keepdims=True)
    vout[2:3] = gb_out

    def reduce_copy(r, which):
        b = lax.rem(r, 2)
        if which == 0:
            return remote(gwi.at[b, :, :, p.other_c], rci.at[r], rs_sem, (r, 0), p.peer_c())
        return remote(gwo.at[b, :, p.other_c], rco.at[r], rs_sem, (r, 1), p.peer_c())

    def reduce_add(r):
        b = lax.rem(r, 2)
        reduce_copy(r, 0).wait()
        for k in range(NZ):
            rci[r, k] = (rci[r, k].astype(F32) + gwi[b, k, :, p.c].astype(F32)).astype(B16)
        reduce_copy(r, 1).wait()
        for k in range(NY):
            rco[r, k] = (rco[r, k].astype(F32) + gwo[b, k, p.c].astype(F32)).astype(B16)

    def ffn_round(r, _):
        t = p.ahead(r)
        gi.ready(r)
        go.ready(r)
        b_in = vec[pl.ds(BIN + t, 1)]
        gb = jnp.zeros((1, FT), F32)
        for q in range(0, L, ROWS):
            rs = pl.ds(q, ROWS)
            pre = dot(h3[rs], flat(WI[t])) + b_in
            up, slope = gelu_parts(pre)
            act[rs] = up.astype(B16)
            acc[rs] += dot(act[rs], flat(WO[t]))
            d = (dot_nt(cot[rs], flat(WO[t])) * slope).astype(B16)
            dpre[rs] = d
            gb += jnp.sum(d.astype(F32), 0, keepdims=True)
            dh3[rs] += dot_nt(d, flat(WI[t]))
            if q == ROWS:

                @pl.when(r < NZ - 1)
                def _():
                    gi.spread(r + 1)
                    go.spread(r + 1)

                @pl.when(r < NZ - 2)
                def _():
                    gi.begin(r + 2)
                    go.begin(r + 2)

        gbi[t] = jnp.broadcast_to(gb, (8, FT))

        @pl.when(r > 0)
        def _():
            reduce_add(r - 1)

        b = lax.rem(r, 2)
        for j in range(0, D, GROUP):
            part = dot_tn(act[...], cot[:, j : j + GROUP]).astype(B16)
            gwo[b, :, :, :, j : j + GROUP] = part.reshape(gwo.shape[1:4] + (GROUP,))
        reduce_copy(r, 1).start()
        for j in range(0, FT, GROUP):
            part = dot(h3t[...], dpre[:, j : j + GROUP]).astype(B16)
            gwi[b, :, :, :, :, j : j + GROUP] = part.reshape(gwi.shape[1:5] + (GROUP,))
        reduce_copy(r, 0).start()

        @pl.when(r < NZ - 1)
        def _():
            gi.finish(r + 1)
            go.finish(r + 1)

        return 0

    lax.fori_loop(0, NZ, ffn_round, 0)
    mixed = act
    sg = jnp.zeros((1, D), F32)
    sb = jnp.zeros((1, D), F32)
    for r in range(0, L, ROWS):
        mixed[pl.ds(r, ROWS)] = acc[pl.ds(r, ROWS)].astype(B16)
    theirs = pl.ds(pl.multiple_of(p.other_x * half, half), half)
    mix_send = remote(mixed.at[theirs], mixed_h.at[p.x], xs, (3,), p.peer_x())
    mix_land = remote(mixed.at[theirs], mixed_h.at[p.other_x], xs, (3,), p.peer_x())
    mix_send.start()
    spill(mixed.at[pl.ds(pl.multiple_of(p.x * half, half), half)], mixed_h.at[p.x])
    for r in range(0, L, ROWS):
        rs = pl.ds(r, ROWS)
        dx, s, b = norm_back(dh3[rs], x2[rs], gains[GAIN + 2 : GAIN + 3])
        acc[rs] = cot[rs].astype(F32) + dx
        sg += s
        sb += b
    vout[0:1] = sg
    vout[1:2] = sb
    spill(acc, g2_h)
    spill(vout, vecs_h)
    spill(gbi, gbi_h)
    spill(vec, gains_h)
    reduce_add(NZ - 1)
    spill(rci, s1i_h)
    spill(rco, s1o_h)

    gv.sent(())
    for n in range(8):
        gw.sent((n,))
    for r in range(NZ):
        gi.sent(r)
        go.sent(r, r > 0)
    for cp in (tok_send, mem_send, cot_send, mix_send):
        cp.wait_send()
    mix_land.wait_recv()
    freed = (tok_spill, qkv_spill, h1_spill, a_spill, h2_spill)
    for cp in spills:
        if not any(cp is q for q in freed):
            cp.wait()


def forward_call(tlen, mlen, flag, tokens, memory, cot, sw, sp, cw, cp, wi, wo, small):
    _, half, D = tokens.shape
    L = 2 * half
    M = 2 * memory.shape[1]
    G = D // GROUP
    S = D // (NZ * NY * NC)
    FT = wi.shape[1] // NZ
    R = wo.shape[0]
    outs = [
        ((2, half, D), B16), ((L, D), B16), ((L, D), B16), ((3, G, L, GROUP), B16), ((L, D), B16), ((G, 8, L), F32),
        ((L, D), F32), ((M, D), B16), ((L, D), B16), ((G, L, GROUP), B16), ((2, G, M, GROUP), B16), ((L, D), B16),
        ((G, 8, L), F32), ((L, D), F32), ((8, NZ, NY, NC, S, D), B16), ((NZ, NZ, NY, S, FT), B16), ((NZ, NY, R, D), B16),
        ((8, D), F32), ((NZ, 8, FT), F32), ((SMALL, D), F32),
    ]
    scratch = [
        ((8, NZ, NY, NC, S, D), B16), ((NZ, NZ, NY, NC, S, FT), B16), ((NZ, NY, NC, R, D), B16), ((NZ, NY, NC, 8, 256), F32),
        ((L, D), B16), ((M, D), B16), ((L, D), B16), ((SMALL, D), F32), ((L, D), B16), ((3, G, L, GROUP), B16), ((L, D), B16),
        ((G, 8, L), F32), ((L, D), F32), ((L, D), B16), ((2, G, M, GROUP), B16), ((G, 8, L), F32),
        ((L, D), F32), ((D, L), B16), ((L, D), F32), ((L, D), F32),
        ((2, NZ, NY, NC, S, FT), B16), ((2, NY, NC, R, D), B16), ((NZ, NZ, NY, S, FT), B16), ((NZ, NY, R, D), B16),
        ((GROUP, L), B16), ((GROUP, L), B16), ((GROUP, M), B16), ((GROUP, L), B16), ((NZ, 8, FT), F32), ((8, D), F32),
    ]
    sems = [(2, 8, 3), (2, 8), (2, 8, 2), (2, 4, 3), (2, 4), (2, 4, 2), (2, 4), (2, 4), (2, 4, 2), (2, 3), (2,), (2, 2), (2, 4), (2, 4, 2), (40,), (24,)]
    return pl.pallas_call(
        forward_kernel,
        out_shape=[jax.ShapeDtypeStruct(s, d) for s, d in outs],
        in_specs=[SMEM_SPEC] * 3 + [ANY_SPEC] * 10,
        out_specs=[ANY_SPEC] * len(outs),
        scratch_shapes=[VMEM(s, d) for s, d in scratch] + [DMA(s) for s in sems],
        compiler_params=pltpu.CompilerParams(vmem_limit_bytes=62 * 1024 * 1024, collective_id=0, has_side_effects=True),
        name="forward",
    )(tlen, mlen, flag, tokens, memory, cot, sw, sp, cw, cp, wi, wo, small)


def pack_small(norm_gain, norm_bias, b_out, b_in):
    s = norm_gain.shape[1]
    rows = jnp.concatenate([norm_gain, norm_bias, b_out[None]], 0).astype(F32)
    rows = jnp.pad(rows, ((0, 0), (0, 256 - s)))
    return jnp.concatenate([rows, jnp.pad(b_in.astype(F32), (0, 256 - b_in.shape[0]))[None]], 0)


def quarter(n):
    return n % 4 if isinstance(n, int) else lax.rem(n, 4)


class Reduce:
    def __init__(self, place, G, rc, ry, rz, tot_h, rx_h, csem, ysem, zsem, xsem, lsem):
        self.p, self.G, self.rc, self.ry, self.rz, self.tot_h, self.rx_h = place, G, rc, ry, rz, tot_h, rx_h
        self.csem, self.ysem, self.zsem, self.xsem, self.lsem = csem, ysem, zsem, xsem, lsem

    def c_copy(self, n):
        return remote(self.G.at[quarter(n), :, :, self.p.other_c], self.rc.at[n], self.csem, (n,), self.p.peer_c())

    def y_copy(self, n):
        return remote(self.rc.at[n, :, self.p.other_y], self.ry.at[n], self.ysem, (n,), self.p.peer_y())

    def z_copy(self, n, r):
        to = self.p.ahead(r)
        return remote(self.ry.at[n, to], self.rz.at[n, r - 1], self.zsem, (n, r - 1), self.p.at_z(to))

    def x_copy(self, n):
        return remote(self.ry.at[n, self.p.z], self.rx_h.at[n], self.xsem, (n,), self.p.peer_x())

    def own_copy(self, n):
        return pltpu.make_async_copy(self.ry.at[n, self.p.z], self.tot_h.at[n], self.lsem.at[n])

    def over_c(self, n):
        self.c_copy(n).start()

    def over_y(self, n):
        self.c_copy(n).wait()
        for k in range(NZ):
            self.rc[n, k] = (self.rc[n, k].astype(F32) + self.G[quarter(n), k, :, self.p.c].astype(F32)).astype(B16)
        self.y_copy(n).start()

    def over_z(self, n):
        self.y_copy(n).wait_recv()
        for k in range(NZ):
            self.ry[n, k] = (self.ry[n, k].astype(F32) + self.rc[n, k, self.p.y].astype(F32)).astype(B16)
        for r in (1, 2, 3):
            self.z_copy(n, r).start()

    def over_x(self, n):
        for r in (1, 2, 3):
            self.z_copy(n, r).wait_recv()
        total = self.ry[n, self.p.z].astype(F32)
        for r in range(3):
            total = total + self.rz[n, r].astype(F32)
        self.ry[n, self.p.z] = total.astype(B16)
        self.x_copy(n).start()
        self.own_copy(n).start()

    def done(self, n):
        self.y_copy(n).wait_send()
        for r in (1, 2, 3):
            self.z_copy(n, r).wait_send()
        self.x_copy(n).wait()
        self.own_copy(n).wait()


class ReduceTiles:
    def __init__(self, place, s1i, s1o, owni, owno, ryi, ryo, rzi, rzo, toti_h, rxi_h, toto_h, rxo_h, yi, yo, zi, zo, xi, xo, lsem):
        self.p, self.s1i, self.s1o, self.owni, self.owno = place, s1i, s1o, owni, owno
        self.ryi, self.ryo, self.rzi, self.rzo = ryi, ryo, rzi, rzo
        self.toti_h, self.rxi_h, self.toto_h, self.rxo_h = toti_h, rxi_h, toto_h, rxo_h
        self.yi, self.yo, self.zi, self.zo, self.xi, self.xo, self.lsem = yi, yo, zi, zo, xi, xo, lsem

    def y_in(self, r):
        return remote(self.s1i.at[r, :, self.p.other_y], self.ryi.at[r], self.yi, (r,), self.p.peer_y())

    def y_out(self, r):
        return remote(self.s1o.at[r, self.p.other_y], self.ryo.at[r], self.yo, (r,), self.p.peer_y())

    def load_in(self, r):
        return pltpu.make_async_copy(self.s1i.at[r, :, self.p.y], self.owni.at[r], self.lsem.at[0, r])

    def load_out(self, r):
        return pltpu.make_async_copy(self.s1o.at[r, self.p.y], self.owno.at[r], self.lsem.at[1, r])

    def z_in(self, r, d):
        to, t = self.p.ahead(d), self.p.ahead(r)
        return remote(self.ryi.at[r, to], self.rzi.at[t, d - 1], self.zi, (t, d - 1), self.p.at_z(to))

    def z_out(self, r):
        return remote(self.ryo.at[r], self.rzo.at[r - 1], self.zo, (r - 1,), self.p.at_z(self.p.ahead(r)))

    def x_in(self, t, r):
        return remote(self.ryi.at[r, self.p.z], self.rxi_h.at[t], self.xi, (t,), self.p.peer_x())

    def x_out(self):
        return remote(self.ryo.at[0], self.rxo_h, self.xo, (0,), self.p.peer_x())

    def own_in(self, t, r):
        return pltpu.make_async_copy(self.ryi.at[r, self.p.z], self.toti_h.at[t], self.lsem.at[2, t])

    def own_out(self):
        return pltpu.make_async_copy(self.ryo.at[0], self.toto_h, self.lsem.at[3, 0])

    def over_y(self, r):
        self.y_in(r).start()
        self.y_out(r).start()
        self.load_in(r).start()
        self.load_out(r).start()

    def over_z(self, r):
        self.load_in(r).wait()
        self.y_in(r).wait_recv()
        for k in range(NZ):
            self.ryi[r, k] = (self.ryi[r, k].astype(F32) + self.owni[r, k].astype(F32)).astype(B16)
        for d in (1, 2, 3):
            self.z_in(r, d).start()
        self.load_out(r).wait()
        self.y_out(r).wait_recv()
        self.ryo[r] = (self.ryo[r].astype(F32) + self.owno[r].astype(F32)).astype(B16)
        if r > 0:
            self.z_out(r).start()

    def over_x(self):
        for t in range(NZ):
            r = lax.rem(t + NZ - self.p.z, NZ)
            total = self.ryi[r, self.p.z].astype(F32)
            for d in (1, 2, 3):
                slot = self.rzi.at[t, d - 1]
                remote(slot, slot, self.zi, (t, d - 1), self.p.at_z(self.p.behind(d))).wait_recv()
                total = total + self.rzi[t, d - 1].astype(F32)
            self.ryi[r, self.p.z] = total.astype(B16)
            self.x_in(t, r).start()
            self.own_in(t, r).start()
        total = self.ryo[0].astype(F32)
        for r in (1, 2, 3):
            self.z_out(r).wait_recv()
            total = total + self.rzo[r - 1].astype(F32)
        self.ryo[0] = total.astype(B16)
        self.x_out().start()
        self.own_out().start()

    def done(self):
        for r in range(NZ):
            self.y_in(r).wait_send()
            self.y_out(r).wait_send()
            for d in (1, 2, 3):
                self.z_in(r, d).wait_send()
            if r:
                self.z_out(r).wait_send()
            t = self.p.ahead(r)
            self.x_in(t, r).wait()
            self.own_in(t, r).wait()
        self.x_out().wait()
        self.own_out().wait()


class SumAll:
    def __init__(self, place, v, land, sems):
        self.p, self.v, self.land, self.sems = place, v, land, sems

    def copy(self, k, peer):
        return remote(self.v.at[k], self.land.at[k], self.sems, (k,), peer)

    def begin(self):
        self.copy(0, self.p.peer_c()).start()

    def over_y(self):
        self.copy(0, self.p.peer_c()).wait_recv()
        self.v[1] = self.v[0] + self.land[0]
        self.copy(1, self.p.peer_y()).start()

    def z_copy(self, r, to):
        return remote(self.v.at[2], self.land.at[1 + r], self.sems, (1 + r,), self.p.at_z(to))

    def over_z(self):
        self.copy(1, self.p.peer_y()).wait_recv()
        self.v[2] = self.v[1] + self.land[1]
        for r in (1, 2, 3):
            self.z_copy(r, self.p.ahead(r)).start()

    def over_x(self):
        for r in (1, 2, 3):
            self.z_copy(r, self.p.ahead(r)).wait_recv()
        total = jnp.zeros_like(self.v[2])
        for z in range(NZ):
            r = lax.rem(self.p.z + NZ - z, NZ)
            part = self.v[2]
            for d in (1, 2, 3):
                part = jnp.where(r == d, self.land[1 + d], part)
            total = total + part
        self.v[3] = total
        remote(self.v.at[3], self.land.at[5], self.sems, (5,), self.p.peer_x()).start()

    def done(self):
        for k, peer in ((0, self.p.peer_c()), (1, self.p.peer_y())):
            self.copy(k, peer).wait_send()
        for r in (1, 2, 3):
            self.z_copy(r, self.p.ahead(r)).wait_send()
        remote(self.v.at[3], self.land.at[5], self.sems, (5,), self.p.peer_x()).wait()
        self.v[0] = self.v[3] + self.land[5]


def backward_kernel(
    tlen, mlen, flag, tok_h, h1_h, qkv_h, a_h, lse_h, x1_h, mem_h, h2_h, cq_h, ckv_h, c_h, clse_h, g2_h, w_h, s1i_h, s1o_h, vecs_h, gbi_h, gains_h,
    gtok_h, gmem_h, tot_h, rx_h, toti_h, rxi_h, toto_h, rxo_h, vec_h,
    W, G, rc, ry, rz, owni, owno, ryi, ryo, rzi, rzo, sv, sland,
    h, att, qkv, ckv, lse, clse, x1, mem, g2, gb, db, dh, gm, gmb, vec, vin, gbi,
    qt, kt, ktc, at, dat, ps, dss, qm, dm, dqt, dk_acc, dv_acc, dkc_acc, dvc_acc, dq, dk, dv, dck, dcv,
    csem, ysem, zsem, xsem, lsem, yi, yo, zi, zo, xi, xo, tlsem, vsem, gsem, loc,
):
    p = Place()
    L, D = h.shape
    M = mem.shape[0]
    half = L // 2
    count = []

    def fetch(src, dst):
        cp = pltpu.make_async_copy(src, dst, loc.at[len(count)])
        cp.start()
        count.append(cp)
        return cp

    vec_cp = [fetch(gains_h, vec), fetch(vecs_h, vin), fetch(gbi_h, gbi)]
    g2_cp = fetch(g2_h, g2)
    w_cp = [None] * 4
    w_cp[3] = fetch(w_h.at[7], W.at[3])
    c_cp = fetch(c_h, att)
    cross_cp = [fetch(cq_h, qkv.at[0]), fetch(ckv_h, ckv), fetch(clse_h, clse), fetch(h2_h, h), fetch(mem_h, mem)]
    for g in range(3):
        w_cp[g] = fetch(w_h.at[4 + g], W.at[g])
    x1_cp = fetch(x1_h, x1)
    kv_cp = [fetch(qkv_h.at[1], qkv.at[1]), fetch(qkv_h.at[2], qkv.at[2]), fetch(lse_h, lse)]
    p.greet()
    rs_ = Reduce(p, G, rc, ry, rz, tot_h, rx_h, csem, ysem, zsem, xsem, lsem)
    tiles = ReduceTiles(p, s1i_h, s1o_h, owni, owno, ryi, ryo, rzi, rzo, toti_h, rxi_h, toto_h, rxo_h, yi, yo, zi, zo, xi, xo, tlsem)
    small = SumAll(p, sv, sland, vsem)
    for r in range(NZ):
        tiles.over_y(r)

    f = flag[p.x].astype(F32)
    for cp in vec_cp:
        cp.wait()
    g2_cp.wait()
    w_cp[3].wait()
    for r in range(0, L, ROWS):
        rs = pl.ds(r, ROWS)
        gcr = (f * g2[rs]).astype(B16)
        gb[rs] = gcr
        db[rs] = dot_nt(gcr, flat(W[3])).astype(B16)
        dh[rs] = jnp.zeros((ROWS, D), F32)
    gm[...] = jnp.zeros_like(gm)

    def put(n, lo, hi, value):
        G[quarter(n), :, :, :, :, lo:hi] = value.astype(B16).reshape(G.shape[1:5] + (hi - lo,))

    def out_projection(n):
        for j in range(0, D, GROUP):
            put(n, j, j + GROUP, dot_tn(att[...], gb[:, j : j + GROUP]))

    c_cp.wait()
    out_projection(3)
    rs_.over_c(3)
    for cp in cross_cp:
        cp.wait()
    for g in range(3):
        w_cp[g].wait()

    def wpart(n, k):
        return flat(W[n, :, :, :, :, k * GROUP : (k + 1) * GROUP])

    def cross_group(g, _):
        attend_back_group(qkv, ckv, ckv, (0, g), (0, g), (1, g), att, db, g, clse, mlen[p.x], False, 256,
                          qt, ktc, at, dat, ps, dss, qm, dm, dqt, dkc_acc, dvc_acc)
        dq[...] = dqt[...].astype(F32).T.astype(B16)
        dck[...] = dkc_acc[...].astype(B16)
        dcv[...] = dvc_acc[...].astype(B16)
        put(g, 0, GROUP, dot_tn(h[...], dq[...]))
        put(g, GROUP, 2 * GROUP, dot_tn(mem[...], dck[...]))
        put(g, 2 * GROUP, 3 * GROUP, dot_tn(mem[...], dcv[...]))
        rs_.over_c(g)
        for r in range(0, L, ROWS):
            rs = pl.ds(r, ROWS)
            dh[rs] += dot_nt(dq[rs], wpart(g, 0))
        gm[...] += dot_nt(dck[...], wpart(g, 1)) + dot_nt(dcv[...], wpart(g, 2))

        @pl.when(g == 0)
        def _():
            rs_.over_y(3)

        @pl.when(g > 0)
        def _():
            rs_.over_y(g - 1)

        return 0

    lax.fori_loop(0, 3, cross_group, 0)
    tiles.over_z(0)
    self_cp = [fetch(w_h.at[3], W.at[3]), fetch(a_h, att), fetch(h1_h, h), fetch(qkv_h.at[0], qkv.at[0])]
    for g in range(3):
        self_cp.append(fetch(w_h.at[g], W.at[g]))
    gmb[...] = gm[...].astype(B16)
    mhalf = M // 2
    gm_send = remote(gmb.at[pl.ds(pl.multiple_of(p.other_x * mhalf, mhalf), mhalf)], gmem_h.at[p.x], gsem, (0,), p.peer_x())
    gm_land = remote(gmb.at[pl.ds(0, mhalf)], gmem_h.at[p.other_x], gsem, (0,), p.peer_x())
    gm_send.start()
    gm_own = fetch(gmb.at[pl.ds(pl.multiple_of(p.x * mhalf, mhalf), mhalf)], gmem_h.at[p.x])
    x1_cp.wait()
    sg = jnp.zeros((1, D), F32)
    sb = jnp.zeros((1, D), F32)
    for r in range(0, L, ROWS):
        rs = pl.ds(r, ROWS)
        dx, s, b = norm_back(dh[rs], x1[rs], vec[1:2])
        g1 = g2[rs] + dx
        g2[rs] = g1
        gb[rs] = g1.astype(B16)
        sg += s
        sb += b
    sv[0, 1:2] = sg
    sv[0, 4:5] = sb
    sv[0, 2:3] = vin[0:1]
    sv[0, 5:6] = vin[1:2]
    sv[0, 6:7] = vin[2:3]
    sv[0, 7:8] = jnp.zeros((1, D), F32)
    for t in range(NZ):
        sv[0, 8 + t : 9 + t] = gbi[t, 0:1]
    sv[0, 12:16] = jnp.zeros((4, D), F32)
    rs_.over_y(2)
    tiles.over_z(1)
    self_cp[0].wait()
    for r in range(0, L, ROWS):
        rs = pl.ds(r, ROWS)
        db[rs] = dot_nt(gb[rs], flat(W[3])).astype(B16)
        dh[rs] = jnp.zeros((ROWS, D), F32)
    self_cp[1].wait()
    out_projection(7)
    rs_.over_c(7)
    tok = gb
    tok_cp = fetch(tok_h, tok)
    for cp in self_cp[2:] + kv_cp:
        cp.wait()

    def self_group(g, _):
        def step(i):
            if i == 1:

                @pl.when(g == 0)
                def _():
                    rs_.over_y(7)
                    tiles.over_z(2)

                @pl.when(g == 1)
                def _():
                    rs_.over_z(3)
                    rs_.over_z(0)

                @pl.when(g == 2)
                def _():
                    rs_.over_z(7)
                    tiles.over_x()
            if i == 3:

                @pl.when(g == 0)
                def _():
                    tiles.over_z(3)

                @pl.when(g == 1)
                def _():
                    rs_.over_z(1)
                    rs_.over_z(2)

                @pl.when(g == 2)
                def _():
                    rs_.over_x(3)
                    rs_.over_x(0)

        attend_back_group(qkv, qkv, qkv, (0, g), (1, g), (2, g), att, db, g, lse, tlen[p.x], True, 256,
                          qt, kt, at, dat, ps, dss, qm, dm, dqt, dk_acc, dv_acc, step)
        dq[...] = dqt[...].astype(F32).T.astype(B16)
        dk[...] = dk_acc[...].astype(B16)
        dv[...] = dv_acc[...].astype(B16)
        for k, d in enumerate((dq, dk, dv)):
            put(4 + g, k * GROUP, (k + 1) * GROUP, dot_tn(h[...], d[...]))
        rs_.over_c(4 + g)
        for r in range(0, L, ROWS):
            rs = pl.ds(r, ROWS)
            dh[rs] += dot_nt(dq[rs], wpart(g, 0)) + dot_nt(dk[rs], wpart(g, 1)) + dot_nt(dv[rs], wpart(g, 2))
        rs_.over_y(4 + g)
        return 0

    lax.fori_loop(0, 3, self_group, 0)
    rs_.over_z(4)
    rs_.over_z(5)
    tok_cp.wait()
    sg = jnp.zeros((1, D), F32)
    sb = jnp.zeros((1, D), F32)
    gt = db
    for r in range(0, L, ROWS):
        rs = pl.ds(r, ROWS)
        dx, s, b = norm_back(dh[rs], tok[rs].astype(F32), vec[0:1])
        gt[rs] = (g2[rs] + dx).astype(B16)
        sg += s
        sb += b
    sv[0, 0:1] = sg
    sv[0, 3:4] = sb
    small.begin()
    gt_send = remote(gt.at[pl.ds(pl.multiple_of(p.other_x * half, half), half)], gtok_h.at[p.x], gsem, (1,), p.peer_x())
    gt_land = remote(gt.at[pl.ds(0, half)], gtok_h.at[p.other_x], gsem, (1,), p.peer_x())
    gt_send.start()
    gt_own = fetch(gt.at[pl.ds(pl.multiple_of(p.x * half, half), half)], gtok_h.at[p.x])
    rs_.over_z(6)
    small.over_y()
    for n in (1, 2, 7, 4, 5):
        rs_.over_x(n)
    small.over_z()
    rs_.over_x(6)
    small.over_x()
    for n in range(8):
        rs_.done(n)
    tiles.done()
    small.done()
    vec_out = fetch(sv.at[0], vec_h)
    for cp in (gm_send, gt_send):
        cp.wait_send()
    for cp in (gm_land, gt_land):
        cp.wait_recv()
    for cp in (gm_own, gt_own, vec_out):
        cp.wait()


def backward_call(tlen, mlen, flag, arrays):
    tok, h1, qkv, a, lse, x1, mem, h2, cq, ckv, c, clse, g2, w, s1i, s1o, vecs, gbi, gains = arrays
    L, D = tok.shape
    M = mem.shape[0]
    G = D // GROUP
    S = w.shape[4]
    R = s1o.shape[2]
    outs = [((2, L // 2, D), B16), ((2, M // 2, D), B16), ((8, S, D), B16), ((8, S, D), B16), ((NZ, S, D), B16), ((NZ, S, D), B16),
            ((R, D), B16), ((R, D), B16), ((SMALL, D), F32)]
    scratch = [
        ((4, NZ, NY, NC, S, D), B16), ((4, NZ, NY, NC, S, D), B16), ((8, NZ, NY, S, D), B16), ((8, NZ, S, D), B16), ((8, 3, S, D), B16),
        ((NZ, NZ, S, D), B16), ((NZ, R, D), B16), ((NZ, NZ, S, D), B16), ((NZ, R, D), B16), ((NZ, 3, S, D), B16), ((3, R, D), B16),
        ((4, SMALL, D), F32), ((6, SMALL, D), F32),
        ((L, D), B16), ((L, D), B16), ((3, G, L, GROUP), B16), ((2, G, M, GROUP), B16), ((G, 8, L), F32), ((G, 8, L), F32), ((L, D), F32),
        ((M, D), B16), ((L, D), F32), ((L, D), B16), ((L, D), B16), ((L, D), F32), ((M, D), F32), ((M, D), B16), ((SMALL, D), F32), ((8, D), F32),
        ((NZ, 8, D), F32),
        ((GROUP, L), B16), ((GROUP, L), B16), ((GROUP, M), B16), ((GROUP, L), B16), ((GROUP, L), B16),
        ((L, PER * 256), B16), ((L, PER * 256), B16), ((PER * 256, GROUP), B16), ((PER * 256, GROUP), B16),
        ((GROUP, L), B16), ((L, GROUP), F32), ((L, GROUP), F32), ((M, GROUP), F32), ((M, GROUP), F32),
        ((L, GROUP), B16), ((L, GROUP), B16), ((L, GROUP), B16), ((M, GROUP), B16), ((M, GROUP), B16),
    ]
    sems = [(2, 8), (2, 8), (2, 8, 3), (2, 8), (8,), (2, 4), (2, 4), (2, 4, 3), (2, 3), (2, 4), (2, 1), (4, 4), (2, 6), (2, 2), (40,)]
    return pl.pallas_call(
        backward_kernel,
        out_shape=[jax.ShapeDtypeStruct(s, d) for s, d in outs],
        in_specs=[SMEM_SPEC] * 3 + [ANY_SPEC] * 19,
        out_specs=[ANY_SPEC] * len(outs),
        scratch_shapes=[VMEM(s, d) for s, d in scratch] + [DMA(s) for s in sems],
        compiler_params=pltpu.CompilerParams(vmem_limit_bytes=63 * 1024 * 1024, collective_id=1, has_side_effects=True),
        name="backward",
    )(tlen, mlen, flag, *arrays)


def paired_body(tokens, memory, cotangent, text_len, mem_len, image_flag, self_qkv, self_out, cross_qkv, cross_out,
                w_in, w_out, b_in, b_out, norm_gain, norm_bias):
    fw = forward_call(text_len, mem_len, image_flag, tokens, memory, cotangent, self_qkv, self_out, cross_qkv, cross_out,
                      w_in, w_out, pack_small(norm_gain, norm_bias, b_out, b_in))
    gtok, gmem, tot, rx, toti, rxi, toto, rxo, vec = backward_call(text_len, mem_len, image_flag, fw[1:])
    i = lax.axis_index("fsdp")
    S = self_out.shape[0]
    pieces = tot.astype(F32) + rx.astype(F32)
    ins = toti.astype(F32) + rxi.astype(F32)

    def qkv(v):
        return v.reshape(3, S, 3, GROUP).transpose(2, 1, 0, 3).reshape(3, S, -1)

    mine = lax.dynamic_slice(vec, (0, i * S), (8, S))
    R = w_out.shape[0]
    tile = lax.dynamic_slice(vec, (8 + i // 4, (i % 4) * R), (1, R))
    return (fw[0], gtok.astype(F32), gmem.astype(F32), qkv(pieces[4:7]), pieces[7], qkv(pieces[0:3]), pieces[3],
            ins.transpose(1, 0, 2).reshape(S, -1), toto.astype(F32) + rxo.astype(F32), tile[0], mine[6], mine[0:3], mine[3:6])


def layer_norm(values, gain, shift):
    centre = values - jnp.mean(values, -1, keepdims=True)
    spread = jnp.mean(centre * centre, -1, keepdims=True)
    return centre * lax.rsqrt(spread + EPSILON) * gain + shift


def gelu_exact(values):
    return jax.nn.gelu(values, approximate=False)


def split_heads(values):
    return values.reshape(values.shape[0], values.shape[1], -1, HEAD).transpose(2, 0, 1, 3)


def merge_heads(values):
    return values.transpose(1, 2, 0, 3).reshape(values.shape[1], values.shape[2], -1)


def head_scores(query_matrix, key_matrix, allowed):
    logit_scores = jnp.einsum(
        "cti,cvi->ctv", query_matrix, key_matrix, preferred_element_type=jnp.float32
    ) * HEAD ** (-0.5)
    return jnp.where(allowed, logit_scores, -1000000000.0)


def attend(query_matrix, key_matrix, values, allowed):

    def one_head(parts):
        head_query_rows, head_key_rows, head_value_rows = parts
        logit_scores = head_scores(head_query_rows, head_key_rows, allowed)
        row_max = jnp.max(logit_scores, -1, keepdims=True)
        expo = jnp.exp(logit_scores - row_max)
        row_sum = jnp.sum(expo, -1, keepdims=True)
        reduced_probabilities = (expo / row_sum).astype(jnp.bfloat16)
        attention_output = jnp.einsum(
            "zqf,zfm->zqm",
            reduced_probabilities,
            head_value_rows,
            preferred_element_type=jnp.float32,
        )
        return (attention_output, row_max, row_sum)

    attention_output, row_max, row_sum = lax.map(
        one_head, (split_heads(query_matrix), split_heads(key_matrix), split_heads(values))
    )
    return (merge_heads(attention_output).astype(jnp.bfloat16), row_max, row_sum)


def attend_back(query_matrix, key_matrix, values, allowed, row_max, row_sum, grad_out):

    def one_head(parts):
        (
            head_query_rows,
            head_key_rows,
            head_value_rows,
            head_output_gradient,
            head_max,
            head_sum,
        ) = parts
        logit_scores = head_scores(head_query_rows, head_key_rows, allowed)
        probs = jnp.exp(logit_scores - head_max) / head_sum
        reduced_probabilities = probs.astype(jnp.bfloat16)
        probs_gradient = jnp.einsum(
            "cti,cvi->ctv",
            head_output_gradient,
            head_value_rows,
            preferred_element_type=jnp.float32,
        )
        delta_sum = jnp.sum(probs * probs_gradient, -1, keepdims=True)
        scores_gradient = (probs * (probs_gradient - delta_sum)).astype(jnp.bfloat16)
        d_query = jnp.einsum(
            "zqf,zfm->zqm", scores_gradient, head_key_rows, preferred_element_type=jnp.float32
        ) * HEAD ** (-0.5)
        d_keys = jnp.einsum(
            "pum,pug->pmg", scores_gradient, head_query_rows, preferred_element_type=jnp.float32
        ) * HEAD ** (-0.5)
        values_gradient = jnp.einsum(
            "pum,pug->pmg",
            reduced_probabilities,
            head_output_gradient,
            preferred_element_type=jnp.float32,
        )
        return (d_query, d_keys, values_gradient)

    d_query, d_keys, values_gradient = lax.map(
        one_head,
        (
            split_heads(query_matrix),
            split_heads(key_matrix),
            split_heads(values),
            split_heads(grad_out),
            row_max,
            row_sum,
        ),
    )
    return (merge_heads(d_query), merge_heads(d_keys), merge_heads(values_gradient))


def general_body(
    tokens,
    memory,
    cotangent,
    text_len,
    mem_len,
    image_flag,
    self_qkv,
    self_out,
    cross_qkv,
    cross_out,
    w_in,
    w_out,
    b_in,
    b_out,
    norm_gain,
    norm_bias,
):
    f32 = jnp.float32
    b16 = jnp.bfloat16
    seq_count, own_rows, width = tokens.shape
    offset = lax.axis_index("mem") * own_rows
    gathered = (
        lax.all_gather(self_qkv, "fsdp", axis=1, tiled=True),
        lax.all_gather(self_out, "fsdp", axis=0, tiled=True),
        lax.all_gather(cross_qkv, "fsdp", axis=1, tiled=True),
        lax.all_gather(cross_out, "fsdp", axis=0, tiled=True),
        lax.all_gather(w_in, "fsdp", axis=0, tiled=True),
        lax.all_gather(w_out, "fsdp", axis=0, tiled=True),
        lax.all_gather(b_in, "fsdp", axis=0, tiled=True),
        lax.all_gather(b_out, "fsdp", axis=0, tiled=True),
        lax.all_gather(norm_gain, "fsdp", axis=1, tiled=True),
        lax.all_gather(norm_bias, "fsdp", axis=1, tiled=True),
    )
    (
        self_w,
        self_proj,
        cross_w,
        cross_proj,
        inner_w,
        outer_w,
        inner_bias,
        outer_bias,
        gains,
        shifts,
    ) = gathered
    gains = gains.astype(f32)
    shifts = shifts.astype(f32)
    x0 = tokens.astype(f32)
    h1_full, norm0_back = jax.vjp(layer_norm, x0, gains[0], shifts[0])
    h1 = h1_full.astype(b16)
    qkv = jnp.einsum("srd,kde->ksre", h1, self_w, preferred_element_type=f32).astype(b16)
    keys_all, values_all = (
        lax.all_gather(qkv[1], "mem", axis=1, tiled=True),
        lax.all_gather(qkv[2], "mem", axis=1, tiled=True),
    )
    key_pos = jnp.arange(keys_all.shape[1], dtype=jnp.int32)
    query_pos = offset + jnp.arange(own_rows, dtype=jnp.int32)
    self_mask = (key_pos[None, None, :] <= query_pos[None, :, None]) & (
        key_pos[None, None, :] < text_len[:, None, None]
    )
    attended, self_max, self_sum = attend(qkv[0], keys_all, values_all, self_mask)
    x1 = x0 + jnp.einsum("srd,de->sre", attended, self_proj, preferred_element_type=f32)
    h2_full, norm1_back = jax.vjp(layer_norm, x1, gains[1], shifts[1])
    h2 = h2_full.astype(b16)
    cross_q = jnp.einsum("srd,de->sre", h2, cross_w[0], preferred_element_type=f32).astype(b16)
    memory_all = lax.all_gather(memory, "mem", axis=1, tiled=True)
    cross_kv = jnp.einsum(
        "snd,kde->ksne", memory_all, cross_w[1:], preferred_element_type=f32
    ).astype(b16)
    cross_keys, cross_values = (cross_kv[0], cross_kv[1])
    mem_pos = jnp.arange(cross_keys.shape[1], dtype=jnp.int32)
    cross_mask = mem_pos[None, None, :] < mem_len[:, None, None]
    crossed, cross_max, cross_sum = attend(cross_q, cross_keys, cross_values, cross_mask)
    flag = image_flag.astype(f32)[:, None, None]
    x2 = x1 + jnp.einsum("srd,de->sre", crossed, cross_proj, preferred_element_type=f32) * flag
    h3_full, norm2_back = jax.vjp(layer_norm, x2, gains[2], shifts[2])
    h3 = h3_full.astype(b16)
    pre = jnp.einsum("srd,df->srf", h3, inner_w, preferred_element_type=f32) + inner_bias.astype(
        f32
    )
    act_full, gelu_back = jax.vjp(gelu_exact, pre)
    act_low = act_full.astype(b16)
    attention_output = (
        x2
        + jnp.einsum("srf,fd->srd", act_low, outer_w, preferred_element_type=f32)
        + outer_bias.astype(f32)
    )
    mixed = attention_output.astype(b16)
    grad_top = cotangent.astype(f32)
    grad_low = grad_top.astype(b16)
    grad_outer_bias = jnp.sum(grad_low.astype(f32), (0, 1))
    grad_outer = jnp.einsum("srf,srd->fd", act_low, grad_low, preferred_element_type=f32)
    d_act = jnp.einsum("srd,fd->srf", grad_low, outer_w, preferred_element_type=f32)
    d_pre = gelu_back(d_act)[0].astype(b16)
    grad_inner_bias = jnp.sum(d_pre.astype(f32), (0, 1))
    grad_inner = jnp.einsum("srd,srf->df", h3, d_pre, preferred_element_type=f32)
    d_h3 = jnp.einsum("srf,df->srd", d_pre, inner_w, preferred_element_type=f32)
    d_x2, gain_two, shift_two = norm2_back(d_h3)
    grad_two = grad_top + d_x2
    grad_cross = (grad_two * flag).astype(b16)
    grad_cross_proj = jnp.einsum("srd,sre->de", crossed, grad_cross, preferred_element_type=f32)
    d_crossed = jnp.einsum(
        "sre,de->srd", grad_cross, cross_proj, preferred_element_type=f32
    ).astype(b16)
    d_cross_q, d_cross_k, d_cross_v = attend_back(
        cross_q, cross_keys, cross_values, cross_mask, cross_max, cross_sum, d_crossed
    )
    own_cross_k, own_cross_v = (
        lax.psum_scatter(
            d_cross_k.astype(jnp.bfloat16), "mem", scatter_dimension=1, tiled=True
        ).astype(jnp.float32),
        lax.psum_scatter(
            d_cross_v.astype(jnp.bfloat16), "mem", scatter_dimension=1, tiled=True
        ).astype(jnp.float32),
    )
    d_cross_kv = jnp.stack([own_cross_k, own_cross_v]).astype(b16)
    grad_cross_kv = jnp.einsum("snd,ksne->kde", memory, d_cross_kv, preferred_element_type=f32)
    grad_memory = jnp.einsum("ksne,kde->snd", d_cross_kv, cross_w[1:], preferred_element_type=f32)
    d_cross_low = d_cross_q.astype(b16)
    grad_cross_q = jnp.einsum("srd,sre->de", h2, d_cross_low, preferred_element_type=f32)
    d_h2 = jnp.einsum("sre,de->srd", d_cross_low, cross_w[0], preferred_element_type=f32)
    d_x1, gain_one, shift_one = norm1_back(d_h2)
    grad_one = grad_two + d_x1
    grad_cross_w = jnp.concatenate([grad_cross_q[None], grad_cross_kv], 0)
    grad_one_low = grad_one.astype(b16)
    grad_self_proj = jnp.einsum("srd,sre->de", attended, grad_one_low, preferred_element_type=f32)
    d_attended = jnp.einsum(
        "sre,de->srd", grad_one_low, self_proj, preferred_element_type=f32
    ).astype(b16)
    d_query, d_keys, values_gradient = attend_back(
        qkv[0], keys_all, values_all, self_mask, self_max, self_sum, d_attended
    )
    own_keys, own_values = (
        lax.psum_scatter(
            d_keys.astype(jnp.bfloat16), "mem", scatter_dimension=1, tiled=True
        ).astype(jnp.float32),
        lax.psum_scatter(
            values_gradient.astype(jnp.bfloat16), "mem", scatter_dimension=1, tiled=True
        ).astype(jnp.float32),
    )
    d_qkv = jnp.stack([d_query, own_keys, own_values]).astype(b16)
    grad_self_w = jnp.einsum("srd,ksre->kde", h1, d_qkv, preferred_element_type=f32)
    d_h1 = jnp.einsum("ksre,kde->srd", d_qkv, self_w, preferred_element_type=f32)
    d_x0, gain_zero, shift_zero = norm0_back(d_h1)
    grad_tokens = grad_one + d_x0
    gain_grads = jnp.stack([gain_zero, gain_one, gain_two])
    shift_grads = jnp.stack([shift_zero, shift_one, shift_two])
    full_grads = (
        grad_self_w,
        grad_self_proj,
        grad_cross_w,
        grad_cross_proj,
        grad_inner,
        grad_outer,
        grad_inner_bias,
        grad_outer_bias,
        gain_grads,
        shift_grads,
    )
    shards = (
        lax.psum_scatter(
            full_grads[0].astype(jnp.bfloat16), "fsdp", scatter_dimension=1, tiled=True
        ).astype(jnp.float32),
        lax.psum_scatter(
            full_grads[1].astype(jnp.bfloat16), "fsdp", scatter_dimension=0, tiled=True
        ).astype(jnp.float32),
        lax.psum_scatter(
            full_grads[2].astype(jnp.bfloat16), "fsdp", scatter_dimension=1, tiled=True
        ).astype(jnp.float32),
        lax.psum_scatter(
            full_grads[3].astype(jnp.bfloat16), "fsdp", scatter_dimension=0, tiled=True
        ).astype(jnp.float32),
        lax.psum_scatter(
            full_grads[4].astype(jnp.bfloat16), "fsdp", scatter_dimension=0, tiled=True
        ).astype(jnp.float32),
        lax.psum_scatter(
            full_grads[5].astype(jnp.bfloat16), "fsdp", scatter_dimension=0, tiled=True
        ).astype(jnp.float32),
        lax.psum_scatter(
            full_grads[6].astype(jnp.bfloat16), "fsdp", scatter_dimension=0, tiled=True
        ).astype(jnp.float32),
        lax.psum_scatter(
            full_grads[7].astype(jnp.bfloat16), "fsdp", scatter_dimension=0, tiled=True
        ).astype(jnp.float32),
        lax.psum_scatter(
            full_grads[8].astype(jnp.bfloat16), "fsdp", scatter_dimension=1, tiled=True
        ).astype(jnp.float32),
        lax.psum_scatter(
            full_grads[9].astype(jnp.bfloat16), "fsdp", scatter_dimension=1, tiled=True
        ).astype(jnp.float32),
    )
    totals = (
        lax.psum(shards[0].astype(jnp.bfloat16), "mem").astype(jnp.float32),
        lax.psum(shards[1].astype(jnp.bfloat16), "mem").astype(jnp.float32),
        lax.psum(shards[2].astype(jnp.bfloat16), "mem").astype(jnp.float32),
        lax.psum(shards[3].astype(jnp.bfloat16), "mem").astype(jnp.float32),
        lax.psum(shards[4].astype(jnp.bfloat16), "mem").astype(jnp.float32),
        lax.psum(shards[5].astype(jnp.bfloat16), "mem").astype(jnp.float32),
        lax.psum(shards[6].astype(jnp.bfloat16), "mem").astype(jnp.float32),
        lax.psum(shards[7].astype(jnp.bfloat16), "mem").astype(jnp.float32),
        lax.psum(shards[8].astype(jnp.bfloat16), "mem").astype(jnp.float32),
        lax.psum(shards[9].astype(jnp.bfloat16), "mem").astype(jnp.float32),
    )
    return (
        mixed,
        grad_tokens,
        grad_memory,
        totals[0],
        totals[1],
        totals[2],
        totals[3],
        totals[4],
        totals[5],
        totals[6],
        totals[7],
        totals[8],
        totals[9],
    )


def body(*args):
    if lax.axis_size("mem") == 2 and lax.axis_size("fsdp") == NZ * NY * NC:
        return paired_body(*args)
    return general_body(*args)


def solution(mesh):
    placed = (
        P("fsdp", "mem", None),
        P("fsdp", "mem", None),
        P("fsdp", "mem", None),
        P("fsdp"),
        P("fsdp"),
        P("fsdp"),
        P(None, "fsdp", None),
        P("fsdp", None),
        P(None, "fsdp", None),
        P("fsdp", None),
        P("fsdp", None),
        P("fsdp", None),
        P("fsdp"),
        P("fsdp"),
        P(None, "fsdp"),
        P(None, "fsdp"),
    )
    return jax.shard_map(
        body,
        mesh=mesh,
        in_specs=placed,
        out_specs=(
            P("fsdp", "mem", None),
            P("fsdp", "mem", None),
            P("fsdp", "mem", None),
            P(None, "fsdp", None),
            P("fsdp", None),
            P(None, "fsdp", None),
            P("fsdp", None),
            P("fsdp", None),
            P("fsdp", None),
            P("fsdp"),
            P("fsdp"),
            P(None, "fsdp"),
            P(None, "fsdp"),
        ),
        check_vma=False,
    )
```

```python
import jax
import jax.numpy as jnp
from jax import lax
from jax.experimental import pallas as pl
from jax.experimental.pallas import tpu as pltpu
from jax.sharding import PartitionSpec as P

F32 = jnp.float32
B16 = jnp.bfloat16
HEAD = 64
GROUP = 256
PER = GROUP // HEAD
EPSILON = 1e-05
NEG = -1000000000.0


def dot(a, b):
    return jnp.dot(a, b, preferred_element_type=F32)


def dot_nt(a, b):
    return lax.dot_general(a, b, (((1,), (1,)), ((), ())), preferred_element_type=F32)


def dot_tn(a, b):
    return lax.dot_general(a, b, (((0,), (0,)), ((), ())), preferred_element_type=F32)


def norm_parts(v):
    centre = v - jnp.mean(v, -1, keepdims=True)
    rs = lax.rsqrt(jnp.mean(centre * centre, -1, keepdims=True) + EPSILON)
    return centre * rs, rs


def norm_back(e, v, gain):
    n, rs = norm_parts(v)
    t = e * gain
    dx = rs * (t - jnp.mean(t, -1, keepdims=True) - n * jnp.mean(t * n, -1, keepdims=True))
    return dx, jnp.sum(e * n, 0, keepdims=True), jnp.sum(e, 0, keepdims=True)


def cols(g):
    return pl.ds(pl.multiple_of(g * GROUP, GROUP), GROUP)


def head_rows(h, rows, width):
    return lax.broadcasted_iota(jnp.int32, (rows, width), 0) // HEAD == h


def head_cols(h, rows, width):
    return lax.broadcasted_iota(jnp.int32, (rows, width), 1) // HEAD == h


def allowed_block(first_key, nk, first_query, nq, limit, causal):
    key = first_key + lax.broadcasted_iota(jnp.int32, (nk, nq), 0)
    ok = key < limit
    if causal:
        query = first_query + lax.broadcasted_iota(jnp.int32, (nk, nq), 1)
        ok = ok & (key <= query)
    return ok


def attend_back_group(
    q_ref, k_ref, v_ref, qi_, ki_, vi_, a_ref, da_ref, g, lse_ref, limit, causal, tq,
    qt, kt, at, dat, ps, dss, qm_ref, dm_ref, dqt, dk_acc, dv_acc, step=None,
):
    L = qt.shape[1]
    K = kt.shape[1]
    scale = HEAD**-0.5
    qt[...] = (q_ref[qi_].astype(F32) * scale).T.astype(B16)
    kt[...] = (k_ref[ki_].astype(F32) * scale).T.astype(B16)
    at[...] = a_ref[:, cols(g)].astype(F32).T.astype(B16)
    dat[...] = da_ref[:, cols(g)].astype(F32).T.astype(B16)

    def keys(i):
        return (i + 1) * tq if causal else K

    def front(i, h):
        nk, span = keys(i), slice(i * tq, (i + 1) * tq)
        here = head_rows(h, GROUP, tq)
        block = qt[:, span]
        s = dot(k_ref[ki_ + (pl.ds(0, nk),)], jnp.where(here, block, jnp.zeros_like(block)))
        block = dat[:, span]
        dp = dot(v_ref[vi_ + (pl.ds(0, nk),)], jnp.where(here, block, jnp.zeros_like(block)))
        return s, dp

    def middle(i, h, s, dp):
        nk, span = keys(i), slice(i * tq, (i + 1) * tq)
        hs = slice(h * HEAD, (h + 1) * HEAD)
        delta = jnp.sum(at[hs, span].astype(F32) * dat[hs, span].astype(F32), 0, keepdims=True)
        s = mask_scores(s, nk, i * tq, tq, limit, causal)
        p = jnp.exp(s - lse_ref[g, h : h + 1, span])
        ds = (p * (dp - delta)).astype(B16)
        ps[0:nk, h * tq : (h + 1) * tq] = p.astype(B16)
        dss[0:nk, h * tq : (h + 1) * tq] = ds
        mine = head_cols(h, tq, GROUP)
        qn = q_ref[qi_ + (pl.ds(i * tq, tq),)] * jnp.asarray(scale, B16)
        dn = da_ref[pl.ds(i * tq, tq), cols(g)]
        qm_ref[h * tq : (h + 1) * tq] = jnp.where(mine, qn, jnp.zeros_like(qn))
        dm_ref[h * tq : (h + 1) * tq] = jnp.where(mine, dn, jnp.zeros_like(dn))
        return ds

    def back(i, h, ds):
        nk, span = keys(i), slice(i * tq, (i + 1) * tq)
        hs = slice(h * HEAD, (h + 1) * HEAD)
        dqt[hs, span] = dot(kt[hs, 0:nk], ds).astype(B16)

    def close(i):
        nk = keys(i)
        dvi = dot(ps[0:nk], dm_ref[...])
        dki = dot(dss[0:nk], qm_ref[...])
        if i == tiles[0]:
            dv_acc[0:nk] = dvi
            dk_acc[0:nk] = dki
        else:
            dv_acc[0:nk] += dvi
            dk_acc[0:nk] += dki

    tiles = list(range(L // tq))[::-1]
    order = [(i, h) for i in tiles for h in range(PER)]
    ahead = front(*order[0])
    late = None
    for n, (i, h) in enumerate(order):
        now = ahead
        if h < PER - 1:
            ahead = front(*order[n + 1])
        ds = middle(i, h, *now)
        if late is not None:
            back(*late)
        late = (i, h, ds)
        if h == PER - 1:
            if n + 1 < len(order):
                ahead = front(*order[n + 1])
            back(*late)
            late = None
            close(i)
            if step is not None:
                step(tiles.index(i))


def mask_scores(s, nk, q0, tq, limit, causal):
    if causal and nk > tq:
        top = jnp.where(allowed_block(0, nk - tq, q0, tq, limit, False), s[: nk - tq], NEG)
        bottom = jnp.where(allowed_block(nk - tq, tq, q0, tq, limit, True), s[nk - tq :], NEG)
        return jnp.concatenate([top, bottom], 0)
    return jnp.where(allowed_block(0, nk, q0, tq, limit, causal), s, NEG)


def attend_group(q_ref, k_ref, v_ref, qi_, ki_, vi_, out_ref, g, lse_ref, limit, causal, tq, qt, vt, ot, step=None):
    L = qt.shape[1]
    K = vt.shape[1]
    qt[...] = (q_ref[qi_].astype(F32) * HEAD**-0.5).T.astype(B16)
    vt[...] = v_ref[vi_].astype(F32).T.astype(B16)

    def keys(i):
        return (i + 1) * tq if causal else K

    def front(i, h):
        block = qt[:, i * tq : (i + 1) * tq]
        qm = jnp.where(head_rows(h, GROUP, tq), block, jnp.zeros_like(block))
        return dot(k_ref[ki_ + (pl.ds(0, keys(i)),)], qm)

    def middle(i, h, s):
        s = mask_scores(s, keys(i), i * tq, tq, limit, causal)
        m = jnp.max(s, 0, keepdims=True)
        e = jnp.exp(s - m)
        total = jnp.sum(e, 0, keepdims=True)
        lse_ref[g, h : h + 1, i * tq : (i + 1) * tq] = m + jnp.log(total)
        return (e * (1.0 / total)).astype(B16)

    def back(i, h, p):
        hs = slice(h * HEAD, (h + 1) * HEAD)
        ot[hs, i * tq : (i + 1) * tq] = dot(vt[hs, 0 : keys(i)], p).astype(B16)

    order = [(i, h) for i in range(L // tq) for h in range(PER)]
    ahead = front(*order[0])
    late = None
    for n, (i, h) in enumerate(order):
        now = ahead
        if n + 1 < len(order):
            ahead = front(*order[n + 1])
        p = middle(i, h, now)
        if late is not None:
            back(*late)
        late = (i, h, p)
        if step is not None and h == PER - 1:
            step(i)
    back(*late)
    out_ref[:, cols(g)] = ot[...].astype(F32).T.astype(B16)


ERFCX = (
    0.21161358920977177, 0.2106475215974073, 0.20533035663075158, 0.12143152976148842,
    0.27391662866419597, -0.22972237163936396, 0.432698311257476, -0.287490481514182,
    0.06157492612604076,
)


def gelu_parts(u):
    t = 1.0 / (1.0 + (0.375 * 0.7071067811865476) * jnp.abs(u))
    poly = jnp.full_like(t, 0.5 * ERFCX[8])
    for c in ERFCX[7::-1]:
        poly = poly * t + 0.5 * c
    bell = jnp.exp(u * (-0.5 * u))
    half = (poly * t) * bell
    cdf = jnp.where(u >= 0, 1.0 - half, half)
    return u * cdf, cdf + u * (bell * 0.3989422804014327)


ROWS = 256

VMEM = pltpu.VMEM
SMEM_SPEC = pl.BlockSpec(memory_space=pltpu.SMEM)


MESH = pl.DeviceIdType.MESH
NZ, NY, NC = 4, 2, 2
ANY_SPEC = pl.BlockSpec(memory_space=pl.ANY)
HBM_SPEC = pl.BlockSpec(memory_space=pltpu.HBM)
DMA = pltpu.SemaphoreType.DMA
SMALL = 16


class Place:
    def __init__(self):
        i = lax.axis_index("fsdp")
        self.x = lax.axis_index("mem")
        self.i = i
        self.z, self.y, self.c = i // (NY * NC), (i // NC) % NY, i % NC
        self.other_x, self.other_y, self.other_c = 1 - self.x, 1 - self.y, 1 - self.c

    def at_z(self, z):
        return (self.x, (z * NY + self.y) * NC + self.c)

    def ahead(self, r):
        return lax.rem(self.z + r, NZ)

    def behind(self, r):
        return lax.rem(self.z + NZ - r, NZ)

    def peer_y(self):
        return (self.x, (self.z * NY + self.other_y) * NC + self.c)

    def peer_c(self):
        return (self.x, (self.z * NY + self.y) * NC + self.other_c)

    def peer_x(self):
        return (self.other_x, self.i)

    def greet(self):
        barrier = pltpu.get_barrier_semaphore()
        peers = [self.at_z(self.ahead(r)) for r in (1, 2, 3)] + [self.peer_y(), self.peer_c(), self.peer_x()]
        for peer in peers:
            pl.semaphore_signal(barrier, inc=1, device_id=peer, device_id_type=MESH)
        pl.semaphore_wait(barrier, len(peers))


def remote(src, dst, sems, index, peer):
    return pltpu.make_async_remote_copy(
        src_ref=src, dst_ref=dst, send_sem=sems.at[(0,) + index], recv_sem=sems.at[(1,) + index],
        device_id=peer, device_id_type=MESH)


class Gather:
    def __init__(self, place, ref, zsem, ysem, csem):
        self.p, self.ref, self.zsem, self.ysem, self.csem = place, ref, zsem, ysem, csem

    def block(self, lead, z):
        return self.ref.at[lead + (z, self.p.y, self.p.c)]

    def z_send(self, lead, r):
        mine = self.block(lead, self.p.z)
        return remote(mine, mine, self.zsem, lead + (r - 1,), self.p.at_z(self.p.ahead(r)))

    def z_land(self, lead, r):
        slot = self.block(lead, self.p.behind(r))
        return remote(slot, slot, self.zsem, lead + (r - 1,), self.p.at_z(self.p.behind(r)))

    def column(self, lead, y, c):
        return self.ref.at[lead + (slice(None), y, c)]

    def y_copy(self, lead, y):
        part = self.column(lead, y, self.p.c)
        return remote(part, part, self.ysem, lead, self.p.peer_y())

    def c_copy(self, lead, k, y, c):
        part = self.column(lead, y, c)
        return remote(part, part, self.csem, lead + (k,), self.p.peer_c())

    def begin(self, lead):
        for r in (1, 2, 3):
            self.z_send(lead, r).start()

    def spread(self, lead):
        for r in (1, 2, 3):
            self.z_land(lead, r).wait_recv()
        self.y_copy(lead, self.p.y).start()
        self.c_copy(lead, 0, self.p.y, self.p.c).start()

    def finish(self, lead):
        self.y_copy(lead, self.p.other_y).wait_recv()
        self.c_copy(lead, 1, self.p.other_y, self.p.c).start()

    def ready(self, lead):
        self.c_copy(lead, 0, self.p.y, self.p.other_c).wait_recv()
        self.c_copy(lead, 1, self.p.other_y, self.p.other_c).wait_recv()

    def sent(self, lead):
        for r in (1, 2, 3):
            self.z_send(lead, r).wait_send()
        self.y_copy(lead, self.p.y).wait_send()
        self.c_copy(lead, 0, self.p.y, self.p.c).wait_send()
        self.c_copy(lead, 1, self.p.other_y, self.p.c).wait_send()


class GatherIn(Gather):
    def tile(self, z, r):
        return lax.rem(z + r, NZ)

    def begin(self, r):
        for d in (1, 2, 3):
            self.send(r, d).start()

    def send(self, r, d):
        to = self.p.ahead(d)
        mine = self.block((self.tile(to, r),), self.p.z)
        return remote(mine, mine, self.zsem, (r, d - 1), self.p.at_z(to))

    def lead(self, r):
        return (self.tile(self.p.z, r),)

    def y_in(self, r, y):
        part = self.column(self.lead(r), y, self.p.c)
        return remote(part, part, self.ysem, (r,), self.p.peer_y())

    def c_in(self, r, k, y, c):
        part = self.column(self.lead(r), y, c)
        return remote(part, part, self.csem, (r, k), self.p.peer_c())

    def spread(self, r):
        for d in (1, 2, 3):
            slot = self.block(self.lead(r), self.p.behind(d))
            remote(slot, slot, self.zsem, (r, d - 1), self.p.at_z(self.p.behind(d))).wait_recv()
        self.y_in(r, self.p.y).start()
        self.c_in(r, 0, self.p.y, self.p.c).start()

    def finish(self, r):
        self.y_in(r, self.p.other_y).wait_recv()
        self.c_in(r, 1, self.p.other_y, self.p.c).start()

    def ready(self, r):
        self.c_in(r, 0, self.p.y, self.p.other_c).wait_recv()
        self.c_in(r, 1, self.p.other_y, self.p.other_c).wait_recv()

    def sent(self, r):
        for d in (1, 2, 3):
            self.send(r, d).wait_send()
        self.y_in(r, self.p.y).wait_send()
        self.c_in(r, 0, self.p.y, self.p.c).wait_send()
        self.c_in(r, 1, self.p.other_y, self.p.c).wait_send()


class GatherHalves(Gather):
    def __init__(self, place, ref, first, zsem, ysem, xsem, csem):
        super().__init__(place, ref, zsem, ysem, csem)
        self.first, self.xsem = first, xsem
        half = ref.shape[-1] // 2
        self.mine = pl.ds(pl.multiple_of(place.x * half, half), half)
        self.theirs = pl.ds(pl.multiple_of(place.other_x * half, half), half)

    def z_send(self, n, r):
        part = self.ref.at[n, self.p.z, self.p.y, self.p.c, :, self.mine]
        return remote(part, part, self.zsem, (n - self.first, r - 1), self.p.at_z(self.p.ahead(r)))

    def z_land(self, n, r):
        part = self.ref.at[n, self.p.behind(r), self.p.y, self.p.c, :, self.mine]
        return remote(part, part, self.zsem, (n - self.first, r - 1), self.p.at_z(self.p.behind(r)))

    def part(self, n, y, c, columns):
        return self.ref.at[n, :, y, c, :, columns]

    def y_half(self, n, y):
        part = self.part(n, y, self.p.c, self.mine)
        return remote(part, part, self.ysem, (n - self.first,), self.p.peer_y())

    def x_half(self, n, k, y, columns):
        part = self.part(n, y, self.p.c, columns)
        return remote(part, part, self.xsem, (n - self.first, k), self.p.peer_x())

    def c_half(self, n, k, y, c, columns):
        part = self.part(n, y, c, columns)
        return remote(part, part, self.csem, (n - self.first, k), self.p.peer_c())

    def quarters(self):
        return ((0, self.p.y, self.mine), (1, self.p.other_y, self.mine), (2, self.p.y, self.theirs), (3, self.p.other_y, self.theirs))

    def spread(self, n):
        for r in (1, 2, 3):
            self.z_land(n, r).wait_recv()
        self.x_half(n, 0, self.p.y, self.mine).start()
        self.y_half(n, self.p.y).start()
        self.c_half(n, 0, self.p.y, self.p.c, self.mine).start()

    def finish(self, n):
        self.y_half(n, self.p.other_y).wait_recv()
        self.x_half(n, 1, self.p.other_y, self.mine).start()
        self.c_half(n, 1, self.p.other_y, self.p.c, self.mine).start()

    def relay(self, n):
        for k, y in ((0, self.p.y), (1, self.p.other_y)):
            self.x_half(n, k, y, self.theirs).wait_recv()
            self.c_half(n, 2 + k, y, self.p.c, self.theirs).start()

    def ready(self, n):
        for k, y, columns in self.quarters():
            self.c_half(n, k, y, self.p.other_c, columns).wait_recv()

    def sent(self, n):
        for r in (1, 2, 3):
            self.z_send(n, r).wait_send()
        self.y_half(n, self.p.y).wait_send()
        for k, y in ((0, self.p.y), (1, self.p.other_y)):
            self.x_half(n, k, y, self.mine).wait_send()
        for k, y, columns in self.quarters():
            self.c_half(n, k, y, self.p.c, columns).wait_send()


class GatherOut:
    def __init__(self, place, ref, zsem, ysem, xsem, csem):
        self.p, self.ref, self.zsem, self.ysem, self.xsem, self.csem = place, ref, zsem, ysem, xsem, csem
        half = ref.shape[-1] // 2
        self.mine = pl.ds(pl.multiple_of(place.x * half, half), half)
        self.theirs = pl.ds(pl.multiple_of(place.other_x * half, half), half)

    def block(self, z, y, c, columns):
        return self.ref.at[z, y, c, :, columns]

    def z_copy(self, r, src_z, to):
        part = self.block(src_z, self.p.y, self.p.c, self.mine)
        return remote(part, part, self.zsem, (r,), self.p.at_z(to))

    def y_copy(self, r, y):
        part = self.block(self.p.ahead(r), y, self.p.c, self.mine)
        return remote(part, part, self.ysem, (r,), self.p.peer_y())

    def x_copy(self, r, k, y, columns):
        part = self.block(self.p.ahead(r), y, self.p.c, columns)
        return remote(part, part, self.xsem, (r, k), self.p.peer_x())

    def c_copy(self, r, k, y, c, columns):
        part = self.block(self.p.ahead(r), y, c, columns)
        return remote(part, part, self.csem, (r, k), self.p.peer_c())

    def begin(self, r):
        self.z_copy(r, self.p.z, self.p.behind(r)).start()

    def spread(self, r, landed=True):
        if landed:
            self.z_copy(r, self.p.ahead(r), self.p.ahead(r)).wait_recv()
        if r:
            self.x_copy(r, 0, self.p.y, self.mine).start()
        self.y_copy(r, self.p.y).start()
        self.c_copy(r, 0, self.p.y, self.p.c, self.mine).start()

    def finish(self, r):
        self.y_copy(r, self.p.other_y).wait_recv()
        self.x_copy(r, 1, self.p.other_y, self.mine).start()
        self.c_copy(r, 1, self.p.other_y, self.p.c, self.mine).start()

    def relay(self, r):
        for k, y in ((0, self.p.y), (1, self.p.other_y)):
            if r or k:
                self.x_copy(r, k, y, self.theirs).wait_recv()
            self.c_copy(r, 2 + k, y, self.p.c, self.theirs).start()

    def ready(self, r):
        for k, y, columns in ((0, self.p.y, self.mine), (1, self.p.other_y, self.mine), (2, self.p.y, self.theirs), (3, self.p.other_y, self.theirs)):
            self.c_copy(r, k, y, self.p.other_c, columns).wait_recv()

    def sent(self, r, began=True):
        if began:
            self.z_copy(r, self.p.z, self.p.behind(r)).wait_send()
        self.y_copy(r, self.p.y).wait_send()
        for k, y in ((0, self.p.y), (1, self.p.other_y)):
            if r or k:
                self.x_copy(r, k, y, self.mine).wait_send()
        for k, y, columns in ((0, self.p.y, self.mine), (1, self.p.other_y, self.mine), (2, self.p.y, self.theirs), (3, self.p.other_y, self.theirs)):
            self.c_copy(r, k, y, self.p.c, columns).wait_send()


def unpack_small(v):
    n = NZ * NY * NC
    D = 48 * n
    total = jnp.zeros((8, D), F32)
    tiles = jnp.zeros((8, D), F32)
    lane = lax.broadcasted_iota(jnp.int32, (8, 256), 1)
    row = lax.broadcasted_iota(jnp.int32, (8, D), 0)
    for i in range(n):
        block = v[i // 4, (i // 2) % 2, i % 2]
        pad = jnp.zeros((8, D - 256), F32)
        total = total + roll_lanes(jnp.concatenate([jnp.where(lane < 48, block, 0.0), pad], 1), 48 * i)
        wide = roll_lanes(jnp.concatenate([jnp.where(lane < 192, block, 0.0), pad], 1), 192 * (i % 4))
        tiles = tiles + jnp.where(row == i // 4, jnp.broadcast_to(wide[7:8], wide.shape), 0.0)
    return jnp.concatenate([total, tiles], 0)


def roll_lanes(v, by):
    return pltpu.roll(v, by, 1) if by else v


def flat(v):
    return v.reshape(-1, v.shape[-1])


PRE, SELF, NEXT, CROSS, FEED, LATE, TAIL = range(7)
BP, SP, FP, LP, RP, BI, SI, FI, BO, SO, FO, LO, TE, RA, XB, XA, PY, PZ, PX, TX, TY, TZ, TF, ME, SY, SZ, SX = range(27)
SPLIT = (5, 6, 7)
FORWARD_PLAN = {
    (PRE, 0, 0): ((TE, 0), (SO, 0), (BP, 0), (BP, 1),),
    (PRE, 1, 0): ((SP, 0), (BP, 5), (BP, 6), (SP, 1), (TE, 1),),
    (PRE, 2, 0): ((TE, 2), (BP, 2),),
    (PRE, 3, 0): ((SP, 5), (FP, 0), (SP, 6),),
    (SELF, 0, 0): ((BP, 3),),
    (SELF, 0, 1): ((BP, 4),),
    (SELF, 0, 2): ((BP, 7),),
    (SELF, 0, 3): ((SP, 2), (FP, 1), (BI, 0),),
    (SELF, 1, 0): ((SP, 3),),
    (SELF, 1, 1): ((FP, 5),),
    (SELF, 1, 2): ((FP, 6), (FP, 2), (BO, 1), (BO, 2),),
    (SELF, 1, 3): ((BI, 1),),
    (SELF, 2, 0): ((SP, 4),),
    (SELF, 2, 2): ((FP, 3), (SP, 7),),
    (NEXT, 1, 0): ((FP, 4), (SI, 0),),
    (CROSS, 0, 0): ((LP, 5),),
    (CROSS, 0, 1): ((FP, 7),),
    (CROSS, 0, 2): ((FO, 0),),
    (CROSS, 0, 3): ((SO, 1),),
    (CROSS, 1, 0): ((BI, 2),),
    (CROSS, 1, 1): ((LP, 6),),
    (CROSS, 1, 3): ((SO, 2), (FI, 0),),
    (CROSS, 2, 0): ((LP, 7),),
    (CROSS, 2, 1): ((FO, 1),),
    (CROSS, 2, 2): ((BO, 3), (SI, 1),),
    (CROSS, 2, 3): ((BI, 3), (LO, 0),),
    (FEED, 0, 0): ((SI, 2),),
    (FEED, 0, 1): ((SO, 3), (LO, 1), (FO, 2),),
    (FEED, 0, 2): ((FI, 1),),
    (FEED, 1, 0): ((SI, 3),),
    (FEED, 1, 1): ((FO, 3),),
    (FEED, 1, 2): ((RA, 0), (LO, 2), (FI, 2),),
    (FEED, 1, 3): ((XB, 0),),
    (FEED, 2, 1): ((FI, 3),),
    (FEED, 2, 2): ((RA, 1), (LO, 3),),
    (FEED, 3, 1): ((RA, 2),),
    (TAIL, 0, 0): ((XA, 0), (RA, 3),),
}


def run_plan(plan, steps, point):
    for kind, n in plan.get(point, ()):
        steps[kind](n)


def run_plan_at(plan, steps, prefix, index, count, i):
    for at in range(count):
        point = (prefix, at, i)
        if point in plan:

            @pl.when(index == at)
            def _(point=point):
                run_plan(plan, steps, point)


def forward_kernel(
    tlen, mlen, flag, tokens_h, memory_h, cot_h, sw_h, sp_h, cw_h, cp_h, wi_h, wo_h, small_h,
    mixed_h, tok_h, h1_h, qkv_h, a_h, lse_h, x1_h, mem_h, h2_h, cq_h, ckv_h, c_h, clse_h, g2_h, w_h, s1i_h, s1o_h, s2i_h, s2o_h, vecs_h, gbi_h, gains_h,
    W, WI, WO, V, tok, mem, cot, vec, h1, qkv, a, lse, x1, h2, ckv, clse, x2, h3t, acc, dh3, gwi, gwo, rci, rco, rxi, rxo,
    qt, vt, vtc, ot, gbi, vout,
    wz, wy, wc, iz, iy, ic, oz, oy, ox, oc, hz, hy, hx, hc, vz, vy, vc, xs, rs_sem, rx_sem, loc, spill_sem,
):
    p = Place()
    L, D = tok.shape
    half = L // 2
    M = mem.shape[0]
    FT = WI.shape[-1]
    local = []

    def fetch(src, dst):
        cp = pltpu.make_async_copy(src, dst, loc.at[len(local)])
        cp.start()
        local.append(cp)
        return cp

    me = (p.z, p.y, p.c)
    pieces = [[] for _ in range(8)]
    for n in SPLIT:
        if n < 7:
            g = n - 4
            for k in range(3):
                pieces[n].append(fetch(cw_h.at[k, :, pl.ds(g * GROUP, GROUP)], W.at[(n,) + me + (slice(None), pl.ds(k * GROUP, GROUP))]))
    pieces[7].append(fetch(cp_h, W.at[(7,) + me]))
    small_cp = fetch(small_h, V.at[me])
    for g in range(3):
        for k in range(3):
            pieces[g].append(fetch(sw_h.at[k, :, pl.ds(g * GROUP, GROUP)], W.at[(g,) + me + (slice(None), pl.ds(k * GROUP, GROUP))]))
    tok_cp = fetch(tokens_h.at[p.x], tok.at[pl.ds(pl.multiple_of(p.x * half, half), half)])
    pieces[3].append(fetch(sp_h, W.at[(3,) + me]))
    for g in range(3):
        for k in range(3):
            if 4 + g not in SPLIT:
                pieces[4 + g].append(fetch(cw_h.at[k, :, pl.ds(g * GROUP, GROUP)], W.at[(4 + g,) + me + (slice(None), pl.ds(k * GROUP, GROUP))]))
    mem_cp = fetch(memory_h.at[p.x], mem.at[pl.ds(pl.multiple_of(p.x * (M // 2), M // 2), M // 2)])
    in_cp = [fetch(wi_h.at[:, pl.ds(t * FT, FT)], WI.at[(t,) + me]) for t in range(NZ)]
    out_cp = fetch(wo_h, WO.at[me])
    cot_cp = fetch(cot_h.at[p.x], cot.at[pl.ds(pl.multiple_of(p.x * half, half), half)])

    for n in SPLIT:
        for cp in pieces[n]:
            cp.wait()
    p.greet()
    gw = Gather(p, W, wz, wy, wc)
    gh = GatherHalves(p, W, SPLIT[0], hz, hy, hx, hc)
    gi = GatherIn(p, WI, iz, iy, ic)
    go = GatherOut(p, WO, oz, oy, ox, oc)
    gv = Gather(p, V, vz, vy, vc)

    def x_part(src_h, dst, rows, k):
        send = remote(src_h.at[p.other_x], dst.at[pl.ds(pl.multiple_of(p.x * rows, rows), rows)], xs, (k,), p.peer_x())
        land = dst.at[pl.ds(pl.multiple_of(p.other_x * rows, rows), rows)]
        return send, remote(src_h.at[p.other_x], land, xs, (k,), p.peer_x())

    tok_send, tok_land = x_part(tokens_h, tok, half, 0)
    mem_send, mem_land = x_part(memory_h, mem, M // 2, 1)
    cot_send, cot_land = x_part(cot_h, cot, half, 2)
    small_cp.wait()
    gv.begin(())

    def piece(method, halves):
        def step(n):
            if n in SPLIT:
                getattr(gh, halves)(n)
            else:
                getattr(gw, method)((n,))

        return step

    steps = {
        BP: piece("begin", "begin"), SP: piece("spread", "spread"), FP: piece("finish", "finish"), LP: gh.relay,
        RP: piece("ready", "ready"), BI: gi.begin, SI: gi.spread, FI: gi.finish,
        BO: go.begin, SO: lambda r: go.spread(r, r > 0), FO: go.finish, LO: go.relay,
        TE: lambda k: (tok_send, mem_send, cot_send)[k].start(),
    }
    for n, cps in enumerate(pieces):
        for cp in cps:
            if n not in SPLIT:
                cp.wait()
    for cp in in_cp + [out_cp, mem_cp, cot_cp]:
        cp.wait()

    def point(name):
        run_plan(FORWARD_PLAN, steps, name)

    point((PRE, 0, 0))
    gv.spread(())
    gv.finish(())
    gv.ready(())
    vec[...] = unpack_small(V)
    gains, shifts = vec, vec
    GAIN, SHIFT, BOUT, BIN = 0, 3, 6, 8

    def norm_rows(src, dst, k, start, count):
        for r in range(0, count, ROWS):
            rs = pl.ds(pl.multiple_of(start + r, ROWS), ROWS)
            n, _ = norm_parts(src[rs].astype(F32))
            dst[rs] = (n * gains[GAIN + k : GAIN + k + 1] + shifts[SHIFT + k : SHIFT + k + 1]).astype(B16)

    point((PRE, 1, 0))
    tok_cp.wait()
    norm_rows(tok, h1, 0, p.x * half, half)
    point((PRE, 2, 0))
    tok_land.wait_recv()
    norm_rows(tok, h1, 0, p.other_x * half, half)
    point((PRE, 3, 0))

    spills = []

    def spill(src, dst):
        cp = pltpu.make_async_copy(src, dst, spill_sem.at[len(spills)])
        cp.start()
        spills.append(cp)
        return cp

    tok_spill = spill(tok, tok_h)
    h1_spill = spill(h1, h1_h)

    def self_group(g, _):
        gw.ready((g,))
        for r in range(0, L, ROWS):
            rs = pl.ds(r, ROWS)
            out = dot(h1[rs], flat(W[g])).astype(B16)
            for k in range(3):
                qkv[k, g, rs] = out[:, k * GROUP : (k + 1) * GROUP]

        def step(i):
            run_plan_at(FORWARD_PLAN, steps, SELF, g, 3, i)

        attend_group(qkv, qkv, qkv, (0, g), (1, g), (2, g), a, g, lse, tlen[p.x], True, 256, qt, vt, ot, step)
        return 0

    lax.fori_loop(0, 3, self_group, 0)
    qkv_spill = spill(qkv, qkv_h)
    a_spill = spill(a, a_h)
    spill(lse, lse_h)
    steps[RP](3)
    for r in range(0, L, ROWS):
        rs = pl.ds(r, ROWS)
        x1[rs] = tok[rs].astype(F32) + dot(a[rs], flat(W[3]))
        norm_rows(x1, h2, 1, r, ROWS)
    point((NEXT, 1, 0))
    mem_land.wait_recv()
    spill(mem, mem_h)
    spill(x1, x1_h)
    h2_spill = spill(h2, h2_h)
    tok_spill.wait()
    qkv_spill.wait()
    c = tok
    cq = qkv.at[0]

    def cross_group(g, _):
        for k in range(3):

            @pl.when(g == k)
            def _(k=k):
                steps[RP](4 + k)

        for r in range(0, L, ROWS):
            rs = pl.ds(r, ROWS)
            cq[g, rs] = dot(h2[rs], flat(W[4 + g, :, :, :, :, 0:GROUP])).astype(B16)
        kv = dot(mem[...], flat(W[4 + g, :, :, :, :, GROUP : 3 * GROUP])).astype(B16)
        ckv[0, g] = kv[:, :GROUP]
        ckv[1, g] = kv[:, GROUP:]

        def step(i):
            run_plan_at(FORWARD_PLAN, steps, CROSS, g, 3, i)

        attend_group(cq, ckv, ckv, (g,), (0, g), (1, g), c, g, clse, mlen[p.x], False, 256, qt, vtc, ot, step)
        return 0

    lax.fori_loop(0, 3, cross_group, 0)
    spill(cq, cq_h)
    spill(ckv, ckv_h)
    spill(c, c_h)
    spill(clse, clse_h)
    steps[RP](7)
    f = flag[p.x].astype(F32)
    h1_spill.wait()
    a_spill.wait()
    h2_spill.wait()
    h3, act, dpre = h1, h2, a
    for r in range(0, L, ROWS):
        rs = pl.ds(r, ROWS)
        x2[rs] = x1[rs] + f * dot(c[rs], flat(W[7]))
        n, _ = norm_parts(x2[rs])
        h = n * gains[GAIN + 2 : GAIN + 3] + shifts[SHIFT + 2 : SHIFT + 3]
        h3[rs] = h.astype(B16)
        h3t[:, r : r + ROWS] = h.T.astype(B16)
        acc[rs] = x2[rs] + vec[BOUT : BOUT + 1]
        dh3[rs] = jnp.zeros((ROWS, D), F32)
    point((NEXT, 2, 0))
    spill(W, w_h)
    cot_land.wait_recv()
    gb_out = jnp.zeros((1, D), F32)
    for r in range(0, L, ROWS):
        gb_out += jnp.sum(cot[pl.ds(r, ROWS)].astype(F32), 0, keepdims=True)
    vout[2:3] = gb_out

    def reduce_copy(r, which):
        if which == 0:
            return remote(gwi.at[:, :, p.other_c], rci.at[r], rs_sem, (r, 0), p.peer_c())
        return remote(gwo.at[:, p.other_c], rco.at[r], rs_sem, (r, 1), p.peer_c())

    def reduce_add(r):
        reduce_copy(r, 0).wait()
        for k in range(NZ):
            rci[r, k] = (rci[r, k].astype(F32) + gwi[k, :, p.c].astype(F32)).astype(B16)
        reduce_copy(r, 1).wait()
        for k in range(NY):
            rco[r, k] = (rco[r, k].astype(F32) + gwo[k, p.c].astype(F32)).astype(B16)

    def x_copy(r, which):
        if which == 0:
            return remote(rci.at[r, :, :, :, go.theirs], rxi, rx_sem, (0,), p.peer_x())
        return remote(rco.at[r, :, :, go.theirs], rxo, rx_sem, (1,), p.peer_x())

    def x_begin(r):
        x_copy(r, 0).start()
        x_copy(r, 1).start()

    def x_add(r):
        x_copy(r, 0).wait()
        for k in range(NZ):
            rxi[k] = (rxi[k].astype(F32) + rci[r, k, :, :, go.mine].astype(F32)).astype(B16)
        x_copy(r, 1).wait()
        for k in range(NY):
            rxo[k] = (rxo[k].astype(F32) + rco[r, k, :, go.mine].astype(F32)).astype(B16)

    steps.update({RA: reduce_add, XB: x_begin, XA: x_add})

    def out_rows(t, j):
        return flat(WO[t])[j * GROUP : (j + 1) * GROUP]

    def ffn_round(r, _):
        t = p.ahead(r)
        gi.ready(r)
        go.ready(r)
        b_in = vec[pl.ds(BIN + t, 1)]
        sums = [jnp.zeros((1, GROUP), F32) for _ in range(0, FT, GROUP)]

        def front(q, j):
            rs, js = pl.ds(q, ROWS), slice(j * GROUP, (j + 1) * GROUP)
            w = flat(WI[t, :, :, :, :, js])
            return dot(h3[rs], w) + b_in[:, js], dot_nt(cot[rs], out_rows(t, j))

        def middle(q, j, pre, d_act):
            rs, js = pl.ds(q, ROWS), slice(j * GROUP, (j + 1) * GROUP)
            up, slope = gelu_parts(pre)
            act[rs, js] = up.astype(B16)
            d = (d_act * slope).astype(B16)
            dpre[rs, js] = d
            sums[j] = sums[j] + jnp.sum(d.astype(F32), 0, keepdims=True)

        def back(q):
            rs = pl.ds(q, ROWS)
            acc[rs] += dot(act[rs], flat(WO[t]))
            dh3[rs] += dot_nt(dpre[rs], flat(WI[t]))

        order = [(q, j) for q in range(0, L, ROWS) for j in range(FT // GROUP)]
        ahead = front(*order[0])
        for n, (q, j) in enumerate(order):
            now = ahead
            if n + 1 < len(order):
                ahead = front(*order[n + 1])
            middle(q, j, *now)
            if j == FT // GROUP - 1:
                back(q)
            if n in (4, 8):
                run_plan_at(FORWARD_PLAN, steps, FEED, r, NZ, n // 4 - 1)

        for j in range(FT // GROUP):
            gbi[t, :, j * GROUP : (j + 1) * GROUP] = jnp.broadcast_to(sums[j], (8, GROUP))

        run_plan_at(FORWARD_PLAN, steps, FEED, r, NZ, 2)
        for j in range(0, D, GROUP):
            part = dot_tn(act[...], cot[:, j : j + GROUP]).astype(B16)
            gwo[:, :, :, j : j + GROUP] = part.reshape(gwo.shape[:3] + (GROUP,))
        reduce_copy(r, 1).start()
        run_plan_at(FORWARD_PLAN, steps, FEED, r, NZ, 3)
        for j in range(0, FT, GROUP):
            part = dot(h3t[...], dpre[:, j : j + GROUP]).astype(B16)
            gwi[:, :, :, :, j : j + GROUP] = part.reshape(gwi.shape[:4] + (GROUP,))
        reduce_copy(r, 0).start()

        run_plan_at(FORWARD_PLAN, steps, FEED, r, NZ, 4)
        return 0

    lax.fori_loop(0, NZ, ffn_round, 0)
    mixed = act
    sg = jnp.zeros((1, D), F32)
    sb = jnp.zeros((1, D), F32)
    for r in range(0, L, ROWS):
        mixed[pl.ds(r, ROWS)] = acc[pl.ds(r, ROWS)].astype(B16)
    spill(mixed, mixed_h)
    for r in range(0, L, ROWS):
        rs = pl.ds(r, ROWS)
        dx, s, b = norm_back(dh3[rs], x2[rs], gains[GAIN + 2 : GAIN + 3])
        acc[rs] = cot[rs].astype(F32) + dx
        sg += s
        sb += b
    vout[0:1] = sg
    vout[1:2] = sb
    spill(acc, g2_h)
    spill(vout, vecs_h)
    spill(gbi, gbi_h)
    spill(vec, gains_h)
    point((TAIL, 0, 0))
    spill(rxi, s2i_h)
    spill(rxo, s2o_h)
    spill(rci.at[pl.ds(1, 3)], s1i_h)
    spill(rco.at[pl.ds(1, 3)], s1o_h)

    gv.sent(())
    for n in range(8):
        piece("sent", "sent")(n)
    for r in range(NZ):
        gi.sent(r)
        go.sent(r, r > 0)
    for cp in (tok_send, mem_send, cot_send):
        cp.wait_send()
    freed = (tok_spill, qkv_spill, h1_spill, a_spill, h2_spill)
    for cp in spills:
        if not any(cp is q for q in freed):
            cp.wait()


def forward_call(tlen, mlen, flag, tokens, memory, cot, sw, sp, cw, cp, wi, wo, small):
    _, half, D = tokens.shape
    L = 2 * half
    M = 2 * memory.shape[1]
    G = D // GROUP
    S = D // (NZ * NY * NC)
    FT = wi.shape[1] // NZ
    R = wo.shape[0]
    H = len(SPLIT)
    outs = [
        ((L, D), B16), ((L, D), B16), ((L, D), B16), ((3, G, L, GROUP), B16), ((L, D), B16), ((G, 8, L), F32),
        ((L, D), F32), ((M, D), B16), ((L, D), B16), ((G, L, GROUP), B16), ((2, G, M, GROUP), B16), ((L, D), B16),
        ((G, 8, L), F32), ((L, D), F32), ((8, NZ, NY, NC, S, D), B16), ((3, NZ, NY, S, FT), B16), ((3, NY, R, D), B16),
        ((NZ, NY, S, FT // 2), B16), ((NY, R, D // 2), B16), ((8, D), F32), ((NZ, 8, FT), F32), ((SMALL, D), F32),
    ]
    scratch = [
        ((8, NZ, NY, NC, S, D), B16), ((NZ, NZ, NY, NC, S, FT), B16), ((NZ, NY, NC, R, D), B16), ((NZ, NY, NC, 8, 256), F32),
        ((L, D), B16), ((M, D), B16), ((L, D), B16), ((SMALL, D), F32), ((L, D), B16), ((3, G, L, GROUP), B16), ((L, D), B16),
        ((G, 8, L), F32), ((L, D), F32), ((L, D), B16), ((2, G, M, GROUP), B16), ((G, 8, L), F32),
        ((L, D), F32), ((D, L), B16), ((L, D), F32), ((L, D), F32),
        ((NZ, NY, NC, S, FT), B16), ((NY, NC, R, D), B16), ((NZ, NZ, NY, S, FT), B16), ((NZ, NY, R, D), B16),
        ((NZ, NY, S, FT // 2), B16), ((NY, R, D // 2), B16),
        ((GROUP, L), B16), ((GROUP, L), B16), ((GROUP, M), B16), ((GROUP, L), B16), ((NZ, 8, FT), F32), ((8, D), F32),
    ]
    sems = [(2, 8, 3), (2, 8), (2, 8, 2), (2, 4, 3), (2, 4), (2, 4, 2), (2, 4), (2, 4), (2, 4, 2), (2, 4, 4), (2, H, 3), (2, H), (2, H, 2), (2, H, 4), (2, 3), (2,), (2, 2), (2, 4), (2, 4, 2), (2, 2), (40,), (24,)]
    return pl.pallas_call(
        forward_kernel,
        out_shape=[jax.ShapeDtypeStruct(s, d) for s, d in outs],
        in_specs=[SMEM_SPEC] * 3 + [ANY_SPEC] * 10,
        out_specs=[ANY_SPEC] * len(outs),
        scratch_shapes=[VMEM(s, d) for s, d in scratch] + [DMA(s) for s in sems],
        compiler_params=pltpu.CompilerParams(vmem_limit_bytes=63 * 1024 * 1024, collective_id=0, has_side_effects=True),
        name="forward",
    )(tlen, mlen, flag, tokens, memory, cot, sw, sp, cw, cp, wi, wo, small)


def pack_small(norm_gain, norm_bias, b_out, b_in):
    s = norm_gain.shape[1]
    rows = jnp.concatenate([norm_gain, norm_bias, b_out[None]], 0).astype(F32)
    rows = jnp.pad(rows, ((0, 0), (0, 256 - s)))
    return jnp.concatenate([rows, jnp.pad(b_in.astype(F32), (0, 256 - b_in.shape[0]))[None]], 0)


def quarter(n):
    return n % 4 if isinstance(n, int) else lax.rem(n, 4)


class Reduce:
    def __init__(self, place, G, rc, ry, rz, tot_h, rx_h, csem, ysem, zsem, xsem, lsem):
        self.p, self.G, self.rc, self.ry, self.rz, self.tot_h, self.rx_h = place, G, rc, ry, rz, tot_h, rx_h
        self.csem, self.ysem, self.zsem, self.xsem, self.lsem = csem, ysem, zsem, xsem, lsem

    def c_copy(self, n):
        return remote(self.G.at[quarter(n), :, :, self.p.other_c], self.rc.at[n], self.csem, (n,), self.p.peer_c())

    def y_copy(self, n):
        return remote(self.rc.at[n, :, self.p.other_y], self.ry.at[n], self.ysem, (n,), self.p.peer_y())

    def z_copy(self, n, r):
        to = self.p.ahead(r)
        return remote(self.ry.at[n, to], self.rz.at[n, r - 1], self.zsem, (n, r - 1), self.p.at_z(to))

    def x_copy(self, n):
        return remote(self.ry.at[n, self.p.z], self.rx_h.at[n], self.xsem, (n,), self.p.peer_x())

    def own_copy(self, n):
        return pltpu.make_async_copy(self.ry.at[n, self.p.z], self.tot_h.at[n], self.lsem.at[n])

    def over_c(self, n):
        self.c_copy(n).start()

    def over_y(self, n):
        self.c_copy(n).wait()
        for k in range(NZ):
            self.rc[n, k] = (self.rc[n, k].astype(F32) + self.G[quarter(n), k, :, self.p.c].astype(F32)).astype(B16)
        self.y_copy(n).start()

    def over_z(self, n):
        self.y_copy(n).wait_recv()
        for k in range(NZ):
            self.ry[n, k] = (self.ry[n, k].astype(F32) + self.rc[n, k, self.p.y].astype(F32)).astype(B16)
        for r in (1, 2, 3):
            self.z_copy(n, r).start()

    def over_x(self, n):
        for r in (1, 2, 3):
            self.z_copy(n, r).wait_recv()
        total = self.ry[n, self.p.z].astype(F32)
        for r in range(3):
            total = total + self.rz[n, r].astype(F32)
        self.ry[n, self.p.z] = total.astype(B16)
        self.x_copy(n).start()
        self.own_copy(n).start()

    def done(self, n):
        self.y_copy(n).wait_send()
        for r in (1, 2, 3):
            self.z_copy(n, r).wait_send()
        self.x_copy(n).wait()
        self.own_copy(n).wait()


class ReduceTiles:
    def __init__(self, place, s1i, s1o, s2i, s2o, own, land, outs, sems):
        self.p = place
        self.s1, self.s2 = (s1i, s1o), (s2i, s2o)
        self.own = own
        self.xi, self.xo, self.yi, self.yo, self.zi, self.zo = land
        self.outi_h, self.outo_h = outs
        self.xs, self.ys, self.zi_s, self.zo_s, self.fi, self.fo, self.lsem = sems
        half = s2i.shape[-1]
        self.mine = pl.ds(pl.multiple_of(place.x * half, half), half)
        self.theirs = pl.ds(pl.multiple_of(place.other_x * half, half), half)

    def full(self, r, which, columns):
        return self.s1[0].at[r - 1, :, :, :, columns] if which == 0 else self.s1[1].at[r - 1, :, :, columns]

    def x_copy(self, r, which):
        return remote(self.full(r, which, self.theirs), (self.xi, self.xo)[which].at[r - 1], self.xs, (r - 1, which), self.p.peer_x())

    def x_load(self, r, which):
        return pltpu.make_async_copy(self.full(r, which, self.mine), self.own[which].at[r - 1], self.lsem.at[which, r])

    def side(self, r, which, y):
        if which == 0:
            return self.xi.at[r - 1, :, y] if r else self.s2[0].at[:, y]
        return self.xo.at[r - 1, y] if r else self.s2[1].at[y]

    def y_copy(self, r, which):
        return remote(self.side(r, which, self.p.other_y), (self.yi, self.yo)[which].at[r], self.ys, (r, which), self.p.peer_y())

    def y_load(self, r, which):
        return pltpu.make_async_copy(self.side(r, which, self.p.y), self.own[2 + which], self.lsem.at[which, r])

    def z_in(self, r, d):
        to, t = self.p.ahead(d), self.p.ahead(r)
        return remote(self.yi.at[r, to], self.zi.at[t, d - 1], self.zi_s, (t, d - 1), self.p.at_z(to))

    def z_out(self, r):
        return remote(self.yo.at[r], self.zo.at[r - 1], self.zo_s, (r - 1,), self.p.at_z(self.p.ahead(r)))

    def last(self, t, r, columns):
        return remote(self.yi.at[r, self.p.z], self.outi_h.at[t, :, columns], self.fi, (t,), self.p.peer_x())

    def last_out(self, columns):
        return remote(self.yo.at[0], self.outo_h.at[:, columns], self.fo, (0,), self.p.peer_x())

    def keep(self, t, r):
        return pltpu.make_async_copy(self.yi.at[r, self.p.z], self.outi_h.at[t, :, self.mine], self.lsem.at[2, t])

    def keep_out(self):
        return pltpu.make_async_copy(self.yo.at[0], self.outo_h.at[:, self.mine], self.lsem.at[3, 0])

    def over_x(self, r):
        for which in range(2):
            self.x_copy(r, which).start()
            self.x_load(r, which).start()

    def over_y(self, r):
        for which in range(2):
            if r:
                self.x_copy(r, which).wait()
                self.x_load(r, which).wait()
                here, own = (self.xi, self.xo)[which], self.own[which]
                for k in range(here.shape[1]):
                    here[r - 1, k] = (here[r - 1, k].astype(F32) + own[r - 1, k].astype(F32)).astype(B16)
            else:
                self.y_load(r, which).start()
            self.y_copy(r, which).start()

    def over_z(self, r):
        if not r:
            self.y_load(r, 0).wait()
        self.y_copy(r, 0).wait_recv()
        for k in range(NZ):
            own = self.xi[r - 1, k, self.p.y] if r else self.own[2][k]
            self.yi[r, k] = (self.yi[r, k].astype(F32) + own.astype(F32)).astype(B16)
        for d in (1, 2, 3):
            self.z_in(r, d).start()
        if not r:
            self.y_load(r, 1).wait()
        self.y_copy(r, 1).wait_recv()
        own = self.xo[r - 1, self.p.y] if r else self.own[3][...]
        self.yo[r] = (self.yo[r].astype(F32) + own.astype(F32)).astype(B16)
        if r:
            self.z_out(r).start()

    def finish(self):
        for t in range(NZ):
            r = lax.rem(t + NZ - self.p.z, NZ)
            total = self.yi[r, self.p.z].astype(F32)
            for d in (1, 2, 3):
                slot = self.zi.at[t, d - 1]
                remote(slot, slot, self.zi_s, (t, d - 1), self.p.at_z(self.p.behind(d))).wait_recv()
                total = total + self.zi[t, d - 1].astype(F32)
            self.yi[r, self.p.z] = total.astype(B16)
            self.last(t, r, self.mine).start()
            self.keep(t, r).start()
        total = self.yo[0].astype(F32)
        for r in (1, 2, 3):
            self.z_out(r).wait_recv()
            total = total + self.zo[r - 1].astype(F32)
        self.yo[0] = total.astype(B16)
        self.last_out(self.mine).start()
        self.keep_out().start()

    def done(self):
        for r in range(NZ):
            for which in range(2):
                self.y_copy(r, which).wait_send()
            for d in (1, 2, 3):
                self.z_in(r, d).wait_send()
            if r:
                self.z_out(r).wait_send()
            t = self.p.ahead(r)
            self.last(t, r, self.mine).wait_send()
            self.last(t, r, self.theirs).wait_recv()
            self.keep(t, r).wait()
        self.last_out(self.mine).wait_send()
        self.last_out(self.theirs).wait_recv()
        self.keep_out().wait()


class SumAll:
    def __init__(self, place, v, land, sems):
        self.p, self.v, self.land, self.sems = place, v, land, sems

    def copy(self, k, peer):
        return remote(self.v.at[k], self.land.at[k], self.sems, (k,), peer)

    def begin(self):
        self.copy(0, self.p.peer_c()).start()

    def over_y(self):
        self.copy(0, self.p.peer_c()).wait_recv()
        self.v[1] = self.v[0] + self.land[0]
        self.copy(1, self.p.peer_y()).start()

    def z_copy(self, r, to):
        return remote(self.v.at[2], self.land.at[1 + r], self.sems, (1 + r,), self.p.at_z(to))

    def over_z(self):
        self.copy(1, self.p.peer_y()).wait_recv()
        self.v[2] = self.v[1] + self.land[1]
        for r in (1, 2, 3):
            self.z_copy(r, self.p.ahead(r)).start()

    def over_x(self):
        for r in (1, 2, 3):
            self.z_copy(r, self.p.ahead(r)).wait_recv()
        total = jnp.zeros_like(self.v[2])
        for z in range(NZ):
            r = lax.rem(self.p.z + NZ - z, NZ)
            part = self.v[2]
            for d in (1, 2, 3):
                part = jnp.where(r == d, self.land[1 + d], part)
            total = total + part
        self.v[3] = total
        remote(self.v.at[3], self.land.at[5], self.sems, (5,), self.p.peer_x()).start()

    def done(self):
        for k, peer in ((0, self.p.peer_c()), (1, self.p.peer_y())):
            self.copy(k, peer).wait_send()
        for r in (1, 2, 3):
            self.z_copy(r, self.p.ahead(r)).wait_send()
        remote(self.v.at[3], self.land.at[5], self.sems, (5,), self.p.peer_x()).wait()
        self.v[0] = self.v[3] + self.land[5]


BACKWARD_PLAN = {
    (PRE, 0, 0): ((TX, 1), (TY, 0),),
    (CROSS, 0, 1): ((PY, 3),),
    (CROSS, 0, 3): ((TX, 2),),
    (CROSS, 1, 0): ((TZ, 0), (TX, 3), (PY, 0),),
    (CROSS, 1, 2): ((PZ, 3),),
    (CROSS, 1, 3): ((TY, 1),),
    (CROSS, 1, 4): ((ME, 0),),
    (CROSS, 2, 1): ((PY, 1), (PZ, 0),),
    (LATE, 1, 0): ((TY, 2),),
    (LATE, 2, 0): ((TZ, 1),),
    (SELF, 0, 0): ((PZ, 1),),
    (SELF, 0, 2): ((PX, 3), (TY, 3), (TZ, 2),),
    (SELF, 0, 4): ((PY, 2),),
    (SELF, 1, 1): ((PX, 0), (TZ, 3),),
    (SELF, 1, 2): ((PY, 4),),
    (SELF, 1, 4): ((PZ, 2),),
    (SELF, 2, 0): ((PY, 5), (TF, 0),),
    (SELF, 2, 1): ((PZ, 4), (PX, 1),),
    (SELF, 2, 3): ((PY, 7),),
    (SELF, 2, 4): ((PX, 2), (PZ, 5),),
    (TAIL, 1, 0): ((PY, 6), (PX, 4), (SY, 0), (PZ, 7), (PZ, 6), (SZ, 0), (PX, 5), (PX, 7), (PX, 6), (SX, 0),),
}


def backward_kernel(
    tlen, mlen, flag, mix_h, tok_h, h1_h, qkv_h, a_h, lse_h, x1_h, mem_h, h2_h, cq_h, ckv_h, c_h, clse_h, g2_h, w_h, s1i_h, s1o_h, s2i_h, s2o_h,
    vecs_h, gbi_h, gains_h,
    mixed_h, gtok_h, gmem_h, tot_h, rx_h, outi_h, outo_h, vec_h,
    W, G, rc, ry, rz, ownxi, ownxo, ownyi, ownyo, rxi, rxo, ryi, ryo, rzi, rzo, sv, sland,
    h, att, qkv, ckv, lse, clse, x1, mem, g2, gb, db, dh, gm, gmb, vec, vin, gbi,
    qt, kt, ktc, at, dat, ps, dss, qm, dm, dqt, dk_acc, dv_acc, dkc_acc, dvc_acc, dq, dk, dv, dck, dcv,
    csem, ysem, zsem, xsem, lsem, txs, tys, tzi, tzo, tfi, tfo, tlsem, vsem, gsem, loc,
):
    p = Place()
    L, D = h.shape
    M = mem.shape[0]
    half = L // 2
    count = []

    def fetch(src, dst):
        cp = pltpu.make_async_copy(src, dst, loc.at[len(count)])
        cp.start()
        count.append(cp)
        return cp

    vec_cp = [fetch(gains_h, vec), fetch(vecs_h, vin), fetch(gbi_h, gbi)]
    g2_cp = fetch(g2_h, g2)
    w_cp = [None] * 4
    w_cp[3] = fetch(w_h.at[7], W.at[3])
    c_cp = fetch(c_h, att)
    cross_cp = [fetch(cq_h, qkv.at[0]), fetch(ckv_h, ckv), fetch(clse_h, clse), fetch(h2_h, h), fetch(mem_h, mem)]
    for g in range(3):
        w_cp[g] = fetch(w_h.at[4 + g], W.at[g])
    x1_cp = fetch(x1_h, x1)
    kv_cp = [fetch(qkv_h.at[1], qkv.at[1]), fetch(qkv_h.at[2], qkv.at[2]), fetch(lse_h, lse)]
    p.greet()
    rs_ = Reduce(p, G, rc, ry, rz, tot_h, rx_h, csem, ysem, zsem, xsem, lsem)
    tiles = ReduceTiles(p, s1i_h, s1o_h, s2i_h, s2o_h, (ownxi, ownxo, ownyi, ownyo), (rxi, rxo, ryi, ryo, rzi, rzo), (outi_h, outo_h),
                        (txs, tys, tzi, tzo, tfi, tfo, tlsem))
    small = SumAll(p, sv, sland, vsem)
    theirs = pl.ds(pl.multiple_of(p.other_x * half, half), half)
    ours = pl.ds(pl.multiple_of(p.x * half, half), half)
    mix_send = remote(mix_h.at[theirs], mixed_h.at[p.x], gsem, (2,), p.peer_x())
    mix_land = remote(mix_h.at[theirs], mixed_h.at[p.other_x], gsem, (2,), p.peer_x())
    steps = {
        PY: rs_.over_y, PZ: rs_.over_z, PX: rs_.over_x, TX: tiles.over_x, TY: tiles.over_y, TZ: tiles.over_z,
        TF: lambda _: tiles.finish(), ME: lambda _: mix_send.start(),
        SY: lambda _: small.over_y(), SZ: lambda _: small.over_z(), SX: lambda _: small.over_x(),
    }

    def point(name):
        run_plan(BACKWARD_PLAN, steps, name)

    point((PRE, 0, 0))
    f = flag[p.x].astype(F32)
    for cp in vec_cp:
        cp.wait()
    g2_cp.wait()
    w_cp[3].wait()
    for r in range(0, L, ROWS):
        rs = pl.ds(r, ROWS)
        gcr = (f * g2[rs]).astype(B16)
        gb[rs] = gcr
        db[rs] = dot_nt(gcr, flat(W[3])).astype(B16)
        dh[rs] = jnp.zeros((ROWS, D), F32)
    gm[...] = jnp.zeros_like(gm)
    point((PRE, 1, 0))

    def put(n, lo, hi, value):
        G[quarter(n), :, :, :, :, lo:hi] = value.astype(B16).reshape(G.shape[1:5] + (hi - lo,))

    def out_projection(n):
        for j in range(0, D, GROUP):
            put(n, j, j + GROUP, dot_tn(att[...], gb[:, j : j + GROUP]))

    c_cp.wait()
    out_projection(3)
    rs_.over_c(3)
    for cp in cross_cp:
        cp.wait()
    for g in range(3):
        w_cp[g].wait()

    def wpart(n, k):
        return flat(W[n, :, :, :, :, k * GROUP : (k + 1) * GROUP])

    def cross_group(g, _):
        def step(i):
            run_plan_at(BACKWARD_PLAN, steps, CROSS, g, 3, i)

        attend_back_group(qkv, ckv, ckv, (0, g), (0, g), (1, g), att, db, g, clse, mlen[p.x], False, 256,
                          qt, ktc, at, dat, ps, dss, qm, dm, dqt, dkc_acc, dvc_acc, step)
        dq[...] = dqt[...].astype(F32).T.astype(B16)
        dck[...] = dkc_acc[...].astype(B16)
        dcv[...] = dvc_acc[...].astype(B16)
        put(g, 0, GROUP, dot_tn(h[...], dq[...]))
        put(g, GROUP, 2 * GROUP, dot_tn(mem[...], dck[...]))
        put(g, 2 * GROUP, 3 * GROUP, dot_tn(mem[...], dcv[...]))
        rs_.over_c(g)
        for r in range(0, L, ROWS):
            rs = pl.ds(r, ROWS)
            dh[rs] += dot_nt(dq[rs], wpart(g, 0))
        gm[...] += dot_nt(dck[...], wpart(g, 1)) + dot_nt(dcv[...], wpart(g, 2))

        step(4)
        return 0

    lax.fori_loop(0, 3, cross_group, 0)
    self_cp = [fetch(w_h.at[3], W.at[3]), fetch(a_h, att), fetch(h1_h, h), fetch(qkv_h.at[0], qkv.at[0])]
    for g in range(3):
        self_cp.append(fetch(w_h.at[g], W.at[g]))
    gmb[...] = gm[...].astype(B16)
    mhalf = M // 2
    gm_send = remote(gmb.at[pl.ds(pl.multiple_of(p.other_x * mhalf, mhalf), mhalf)], gmem_h.at[p.x], gsem, (0,), p.peer_x())
    gm_land = remote(gmb.at[pl.ds(0, mhalf)], gmem_h.at[p.other_x], gsem, (0,), p.peer_x())
    gm_send.start()
    gm_own = fetch(gmb.at[pl.ds(pl.multiple_of(p.x * mhalf, mhalf), mhalf)], gmem_h.at[p.x])
    point((LATE, 0, 0))
    x1_cp.wait()
    sg = jnp.zeros((1, D), F32)
    sb = jnp.zeros((1, D), F32)
    for r in range(0, L, ROWS):
        rs = pl.ds(r, ROWS)
        dx, s, b = norm_back(dh[rs], x1[rs], vec[1:2])
        g1 = g2[rs] + dx
        g2[rs] = g1
        gb[rs] = g1.astype(B16)
        sg += s
        sb += b
    sv[0, 1:2] = sg
    sv[0, 4:5] = sb
    sv[0, 2:3] = vin[0:1]
    sv[0, 5:6] = vin[1:2]
    sv[0, 6:7] = vin[2:3]
    sv[0, 7:8] = jnp.zeros((1, D), F32)
    for t in range(NZ):
        sv[0, 8 + t : 9 + t] = gbi[t, 0:1]
    sv[0, 12:16] = jnp.zeros((4, D), F32)
    point((LATE, 1, 0))
    self_cp[0].wait()
    for r in range(0, L, ROWS):
        rs = pl.ds(r, ROWS)
        db[rs] = dot_nt(gb[rs], flat(W[3])).astype(B16)
        dh[rs] = jnp.zeros((ROWS, D), F32)
    point((LATE, 2, 0))
    self_cp[1].wait()
    out_projection(7)
    rs_.over_c(7)
    tok = gb
    tok_cp = fetch(tok_h, tok)
    for cp in self_cp[2:] + kv_cp:
        cp.wait()

    def self_group(g, _):
        def step(i):
            run_plan_at(BACKWARD_PLAN, steps, SELF, g, 3, i)

        attend_back_group(qkv, qkv, qkv, (0, g), (1, g), (2, g), att, db, g, lse, tlen[p.x], True, 256,
                          qt, kt, at, dat, ps, dss, qm, dm, dqt, dk_acc, dv_acc, step)
        dq[...] = dqt[...].astype(F32).T.astype(B16)
        dk[...] = dk_acc[...].astype(B16)
        dv[...] = dv_acc[...].astype(B16)
        for k, d in enumerate((dq, dk, dv)):
            put(4 + g, k * GROUP, (k + 1) * GROUP, dot_tn(h[...], d[...]))
        rs_.over_c(4 + g)
        for r in range(0, L, ROWS):
            rs = pl.ds(r, ROWS)
            dh[rs] += dot_nt(dq[rs], wpart(g, 0)) + dot_nt(dk[rs], wpart(g, 1)) + dot_nt(dv[rs], wpart(g, 2))
        step(4)
        return 0

    lax.fori_loop(0, 3, self_group, 0)
    tok_cp.wait()
    sg = jnp.zeros((1, D), F32)
    sb = jnp.zeros((1, D), F32)
    gt = db
    sent = False
    gt_send = remote(gt.at[theirs], gtok_h.at[p.x], gsem, (1,), p.peer_x())
    gt_land = remote(gt.at[theirs], gtok_h.at[p.other_x], gsem, (1,), p.peer_x())
    for start in (p.other_x * half, p.x * half):
        for r in range(0, half, ROWS):
            rs = pl.ds(pl.multiple_of(start + r, ROWS), ROWS)
            dx, s, b = norm_back(dh[rs], tok[rs].astype(F32), vec[0:1])
            gt[rs] = (g2[rs] + dx).astype(B16)
            sg += s
            sb += b
        if not sent:
            gt_send.start()
            point((TAIL, 0, 0))
        sent = True
    sv[0, 0:1] = sg
    sv[0, 3:4] = sb
    small.begin()
    gt_own = fetch(gt.at[ours], gtok_h.at[p.x])
    point((TAIL, 1, 0))
    for n in range(8):
        rs_.done(n)
    tiles.done()
    small.done()
    vec_out = fetch(sv.at[0], vec_h)
    for cp in (mix_send, gm_send, gt_send):
        cp.wait_send()
    for cp in (mix_land, gm_land, gt_land):
        cp.wait_recv()
    for cp in (gm_own, gt_own, vec_out):
        cp.wait()


def backward_call(tlen, mlen, flag, arrays):
    mix, tok, h1, qkv, a, lse, x1, mem, h2, cq, ckv, c, clse, g2, w, s1i, s1o, s2i, s2o, vecs, gbi, gains = arrays
    L, D = tok.shape
    M = mem.shape[0]
    G = D // GROUP
    S = w.shape[4]
    R = s1o.shape[2]
    H = D // 2
    outs = [((2, L // 2, D), B16), ((2, L // 2, D), B16), ((2, M // 2, D), B16), ((8, S, D), B16), ((8, S, D), B16), ((NZ, S, D), B16),
            ((R, D), B16), ((SMALL, D), F32)]
    scratch = [
        ((4, NZ, NY, NC, S, D), B16), ((4, NZ, NY, NC, S, D), B16), ((8, NZ, NY, S, D), B16), ((8, NZ, S, D), B16), ((8, 3, S, D), B16),
        ((3, NZ, NY, S, H), B16), ((3, NY, R, H), B16), ((NZ, S, H), B16), ((R, H), B16),
        ((3, NZ, NY, S, H), B16), ((3, NY, R, H), B16), ((NZ, NZ, S, H), B16), ((NZ, R, H), B16), ((NZ, 3, S, H), B16), ((3, R, H), B16),
        ((4, SMALL, D), F32), ((6, SMALL, D), F32),
        ((L, D), B16), ((L, D), B16), ((3, G, L, GROUP), B16), ((2, G, M, GROUP), B16), ((G, 8, L), F32), ((G, 8, L), F32), ((L, D), F32),
        ((M, D), B16), ((L, D), F32), ((L, D), B16), ((L, D), B16), ((L, D), F32), ((M, D), F32), ((M, D), B16), ((SMALL, D), F32), ((8, D), F32),
        ((NZ, 8, D), F32),
        ((GROUP, L), B16), ((GROUP, L), B16), ((GROUP, M), B16), ((GROUP, L), B16), ((GROUP, L), B16),
        ((L, PER * 256), B16), ((L, PER * 256), B16), ((PER * 256, GROUP), B16), ((PER * 256, GROUP), B16),
        ((GROUP, L), B16), ((L, GROUP), F32), ((L, GROUP), F32), ((M, GROUP), F32), ((M, GROUP), F32),
        ((L, GROUP), B16), ((L, GROUP), B16), ((L, GROUP), B16), ((M, GROUP), B16), ((M, GROUP), B16),
    ]
    sems = [(2, 8), (2, 8), (2, 8, 3), (2, 8), (8,), (2, 3, 2), (2, 4, 2), (2, 4, 3), (2, 3), (2, 4), (2, 1), (4, 4), (2, 6), (2, 3), (40,)]
    return pl.pallas_call(
        backward_kernel,
        out_shape=[jax.ShapeDtypeStruct(s, d) for s, d in outs],
        in_specs=[SMEM_SPEC] * 3 + [ANY_SPEC] * len(arrays),
        out_specs=[ANY_SPEC] * len(outs),
        scratch_shapes=[VMEM(s, d) for s, d in scratch] + [DMA(s) for s in sems],
        compiler_params=pltpu.CompilerParams(vmem_limit_bytes=63 * 1024 * 1024, collective_id=1, has_side_effects=True),
        name="backward",
    )(tlen, mlen, flag, *arrays)


def finish_kernel(
    mix_i, mixed_i, gtok_i, gmem_i, tot_i, rx_i, ins_i, out_i, vec_i,
    mixed, gtok, gmem, gsw, gsp, gcw, gcp, gwi, gwo, gbi, gbo, gg, gs,
    mix_v, tok_v, mem_v, tot_v, rx_v, ins_v, out_v, vec_v, tok_f, mem_f, sw_f, sp_f, cw_f, cp_f, wi_f, wo_f, bi_f, bo_f, g_f, s_f, sems,
):
    count = []

    def copy(src, dst):
        cp = pltpu.make_async_copy(src, dst, sems.at[len(count)])
        cp.start()
        count.append(cp)
        return cp

    S = gsp.shape[0]
    halves = [copy(gtok_i.at[k], tok_v.at[k]) for k in range(2)]
    rest = [copy(a, b) for a, b in ((tot_i, tot_v), (rx_i, rx_v), (ins_i, ins_v), (out_i, out_v), (gmem_i, mem_v), (vec_i, vec_v))]
    x = lax.axis_index("mem")
    half = mixed.shape[1]
    both = [copy(mix_i.at[pl.ds(pl.multiple_of(x * half, half), half)], mix_v.at[0]), copy(mixed_i.at[1 - x], mix_v.at[1])]
    outs = []
    for k in range(2):
        halves[k].wait()
        tok_f[k] = tok_v[k].astype(F32)
        outs.append(copy(tok_f.at[k], gtok.at[k]))
    for k, cp in enumerate(both):
        cp.wait()
        outs.append(copy(mix_v.at[k], mixed.at[1 - x if k else x]))
    for cp in rest:
        cp.wait()
    for first, dst in ((0, cw_f), (4, sw_f)):
        for g in range(3):
            v = tot_v[first + g].astype(F32) + rx_v[first + g].astype(F32)
            for k in range(3):
                dst[k, :, g * GROUP : (g + 1) * GROUP] = v[:, k * GROUP : (k + 1) * GROUP]
    cp_f[...] = tot_v[3].astype(F32) + rx_v[3].astype(F32)
    sp_f[...] = tot_v[7].astype(F32) + rx_v[7].astype(F32)
    D = sp_f.shape[1]
    for t in range(NZ):
        wi_f[:, t * D : (t + 1) * D] = ins_v[t].astype(F32)
    wo_f[...] = out_v[...].astype(F32)
    mem_f[...] = mem_v[...].astype(F32)
    i = lax.axis_index("fsdp")
    R = wo_f.shape[0]
    mine = pltpu.roll(vec_v[0:8], lax.rem(D - i * S, D), 1)
    g_f[...] = mine[0:3, :S]
    s_f[...] = mine[3:6, :S]
    bo_f[...] = mine[6:7, :S]
    row = lax.broadcasted_iota(jnp.int32, (8, D), 0)
    tile = jnp.sum(jnp.where(row == i // (NY * NC), vec_v[8:16], 0.0), 0, keepdims=True)
    tile = pltpu.roll(jnp.broadcast_to(tile, (8, D)), lax.rem(D - lax.rem(i, NY * NC) * R, D), 1)
    bi_f[...] = tile[0:1, :R]
    for a, b in ((mem_f, gmem), (sw_f, gsw), (sp_f, gsp), (cw_f, gcw), (cp_f, gcp), (wi_f, gwi), (wo_f, gwo), (bi_f, gbi), (bo_f, gbo), (g_f, gg), (s_f, gs)):
        outs.append(copy(a, b))
    for cp in outs:
        cp.wait()


def finish_call(mix, mixed, gtok, gmem, tot, rx, ins, out, vec):
    S, D = tot.shape[1:]
    R = out.shape[0]
    outs = [(mixed.shape, B16), (gtok.shape, F32), (gmem.shape, F32), ((3, S, D), F32), ((S, D), F32), ((3, S, D), F32), ((S, D), F32),
            ((S, NZ * D), F32), ((R, D), F32), ((1, R), F32), ((1, S), F32), ((3, S), F32), ((3, S), F32)]
    ins_ = (mix, mixed, gtok, gmem, tot, rx, ins, out, vec)
    scratch = [VMEM(v.shape, v.dtype) for v in ins_[1:]] + [VMEM(s, d) for s, d in outs[1:]]
    return pl.pallas_call(
        finish_kernel,
        out_shape=[jax.ShapeDtypeStruct(s, d) for s, d in outs],
        in_specs=[HBM_SPEC] * len(ins_),
        out_specs=[HBM_SPEC] * len(outs),
        scratch_shapes=scratch + [DMA((32,))],
        compiler_params=pltpu.CompilerParams(vmem_limit_bytes=62 * 1024 * 1024),
        name="finish",
    )(*ins_)


def paired_body(tokens, memory, cotangent, text_len, mem_len, image_flag, self_qkv, self_out, cross_qkv, cross_out,
                w_in, w_out, b_in, b_out, norm_gain, norm_bias):
    fw = forward_call(text_len, mem_len, image_flag, tokens, memory, cotangent, self_qkv, self_out, cross_qkv, cross_out,
                      w_in, w_out, pack_small(norm_gain, norm_bias, b_out, b_in))
    outs = finish_call(fw[0], *backward_call(text_len, mem_len, image_flag, fw))
    return (*outs[:9], outs[9][0], outs[10][0], *outs[11:])


def layer_norm(values, gain, shift):
    centre = values - jnp.mean(values, -1, keepdims=True)
    spread = jnp.mean(centre * centre, -1, keepdims=True)
    return centre * lax.rsqrt(spread + EPSILON) * gain + shift


def gelu_exact(values):
    return jax.nn.gelu(values, approximate=False)


def split_heads(values):
    return values.reshape(values.shape[0], values.shape[1], -1, HEAD).transpose(2, 0, 1, 3)


def merge_heads(values):
    return values.transpose(1, 2, 0, 3).reshape(values.shape[1], values.shape[2], -1)


def head_scores(query_matrix, key_matrix, allowed):
    logit_scores = jnp.einsum(
        "cti,cvi->ctv", query_matrix, key_matrix, preferred_element_type=jnp.float32
    ) * HEAD ** (-0.5)
    return jnp.where(allowed, logit_scores, -1000000000.0)


def attend(query_matrix, key_matrix, values, allowed):

    def one_head(parts):
        head_query_rows, head_key_rows, head_value_rows = parts
        logit_scores = head_scores(head_query_rows, head_key_rows, allowed)
        row_max = jnp.max(logit_scores, -1, keepdims=True)
        expo = jnp.exp(logit_scores - row_max)
        row_sum = jnp.sum(expo, -1, keepdims=True)
        reduced_probabilities = (expo / row_sum).astype(jnp.bfloat16)
        attention_output = jnp.einsum(
            "zqf,zfm->zqm",
            reduced_probabilities,
            head_value_rows,
            preferred_element_type=jnp.float32,
        )
        return (attention_output, row_max, row_sum)

    attention_output, row_max, row_sum = lax.map(
        one_head, (split_heads(query_matrix), split_heads(key_matrix), split_heads(values))
    )
    return (merge_heads(attention_output).astype(jnp.bfloat16), row_max, row_sum)


def attend_back(query_matrix, key_matrix, values, allowed, row_max, row_sum, grad_out):

    def one_head(parts):
        (
            head_query_rows,
            head_key_rows,
            head_value_rows,
            head_output_gradient,
            head_max,
            head_sum,
        ) = parts
        logit_scores = head_scores(head_query_rows, head_key_rows, allowed)
        probs = jnp.exp(logit_scores - head_max) / head_sum
        reduced_probabilities = probs.astype(jnp.bfloat16)
        probs_gradient = jnp.einsum(
            "cti,cvi->ctv",
            head_output_gradient,
            head_value_rows,
            preferred_element_type=jnp.float32,
        )
        delta_sum = jnp.sum(probs * probs_gradient, -1, keepdims=True)
        scores_gradient = (probs * (probs_gradient - delta_sum)).astype(jnp.bfloat16)
        d_query = jnp.einsum(
            "zqf,zfm->zqm", scores_gradient, head_key_rows, preferred_element_type=jnp.float32
        ) * HEAD ** (-0.5)
        d_keys = jnp.einsum(
            "pum,pug->pmg", scores_gradient, head_query_rows, preferred_element_type=jnp.float32
        ) * HEAD ** (-0.5)
        values_gradient = jnp.einsum(
            "pum,pug->pmg",
            reduced_probabilities,
            head_output_gradient,
            preferred_element_type=jnp.float32,
        )
        return (d_query, d_keys, values_gradient)

    d_query, d_keys, values_gradient = lax.map(
        one_head,
        (
            split_heads(query_matrix),
            split_heads(key_matrix),
            split_heads(values),
            split_heads(grad_out),
            row_max,
            row_sum,
        ),
    )
    return (merge_heads(d_query), merge_heads(d_keys), merge_heads(values_gradient))


def general_body(
    tokens,
    memory,
    cotangent,
    text_len,
    mem_len,
    image_flag,
    self_qkv,
    self_out,
    cross_qkv,
    cross_out,
    w_in,
    w_out,
    b_in,
    b_out,
    norm_gain,
    norm_bias,
):
    f32 = jnp.float32
    b16 = jnp.bfloat16
    seq_count, own_rows, width = tokens.shape
    offset = lax.axis_index("mem") * own_rows
    gathered = (
        lax.all_gather(self_qkv, "fsdp", axis=1, tiled=True),
        lax.all_gather(self_out, "fsdp", axis=0, tiled=True),
        lax.all_gather(cross_qkv, "fsdp", axis=1, tiled=True),
        lax.all_gather(cross_out, "fsdp", axis=0, tiled=True),
        lax.all_gather(w_in, "fsdp", axis=0, tiled=True),
        lax.all_gather(w_out, "fsdp", axis=0, tiled=True),
        lax.all_gather(b_in, "fsdp", axis=0, tiled=True),
        lax.all_gather(b_out, "fsdp", axis=0, tiled=True),
        lax.all_gather(norm_gain, "fsdp", axis=1, tiled=True),
        lax.all_gather(norm_bias, "fsdp", axis=1, tiled=True),
    )
    (
        self_w,
        self_proj,
        cross_w,
        cross_proj,
        inner_w,
        outer_w,
        inner_bias,
        outer_bias,
        gains,
        shifts,
    ) = gathered
    gains = gains.astype(f32)
    shifts = shifts.astype(f32)
    x0 = tokens.astype(f32)
    h1_full, norm0_back = jax.vjp(layer_norm, x0, gains[0], shifts[0])
    h1 = h1_full.astype(b16)
    qkv = jnp.einsum("srd,kde->ksre", h1, self_w, preferred_element_type=f32).astype(b16)
    keys_all, values_all = (
        lax.all_gather(qkv[1], "mem", axis=1, tiled=True),
        lax.all_gather(qkv[2], "mem", axis=1, tiled=True),
    )
    key_pos = jnp.arange(keys_all.shape[1], dtype=jnp.int32)
    query_pos = offset + jnp.arange(own_rows, dtype=jnp.int32)
    self_mask = (key_pos[None, None, :] <= query_pos[None, :, None]) & (
        key_pos[None, None, :] < text_len[:, None, None]
    )
    attended, self_max, self_sum = attend(qkv[0], keys_all, values_all, self_mask)
    x1 = x0 + jnp.einsum("srd,de->sre", attended, self_proj, preferred_element_type=f32)
    h2_full, norm1_back = jax.vjp(layer_norm, x1, gains[1], shifts[1])
    h2 = h2_full.astype(b16)
    cross_q = jnp.einsum("srd,de->sre", h2, cross_w[0], preferred_element_type=f32).astype(b16)
    memory_all = lax.all_gather(memory, "mem", axis=1, tiled=True)
    cross_kv = jnp.einsum(
        "snd,kde->ksne", memory_all, cross_w[1:], preferred_element_type=f32
    ).astype(b16)
    cross_keys, cross_values = (cross_kv[0], cross_kv[1])
    mem_pos = jnp.arange(cross_keys.shape[1], dtype=jnp.int32)
    cross_mask = mem_pos[None, None, :] < mem_len[:, None, None]
    crossed, cross_max, cross_sum = attend(cross_q, cross_keys, cross_values, cross_mask)
    flag = image_flag.astype(f32)[:, None, None]
    x2 = x1 + jnp.einsum("srd,de->sre", crossed, cross_proj, preferred_element_type=f32) * flag
    h3_full, norm2_back = jax.vjp(layer_norm, x2, gains[2], shifts[2])
    h3 = h3_full.astype(b16)
    pre = jnp.einsum("srd,df->srf", h3, inner_w, preferred_element_type=f32) + inner_bias.astype(
        f32
    )
    act_full, gelu_back = jax.vjp(gelu_exact, pre)
    act_low = act_full.astype(b16)
    attention_output = (
        x2
        + jnp.einsum("srf,fd->srd", act_low, outer_w, preferred_element_type=f32)
        + outer_bias.astype(f32)
    )
    mixed = attention_output.astype(b16)
    grad_top = cotangent.astype(f32)
    grad_low = grad_top.astype(b16)
    grad_outer_bias = jnp.sum(grad_low.astype(f32), (0, 1))
    grad_outer = jnp.einsum("srf,srd->fd", act_low, grad_low, preferred_element_type=f32)
    d_act = jnp.einsum("srd,fd->srf", grad_low, outer_w, preferred_element_type=f32)
    d_pre = gelu_back(d_act)[0].astype(b16)
    grad_inner_bias = jnp.sum(d_pre.astype(f32), (0, 1))
    grad_inner = jnp.einsum("srd,srf->df", h3, d_pre, preferred_element_type=f32)
    d_h3 = jnp.einsum("srf,df->srd", d_pre, inner_w, preferred_element_type=f32)
    d_x2, gain_two, shift_two = norm2_back(d_h3)
    grad_two = grad_top + d_x2
    grad_cross = (grad_two * flag).astype(b16)
    grad_cross_proj = jnp.einsum("srd,sre->de", crossed, grad_cross, preferred_element_type=f32)
    d_crossed = jnp.einsum(
        "sre,de->srd", grad_cross, cross_proj, preferred_element_type=f32
    ).astype(b16)
    d_cross_q, d_cross_k, d_cross_v = attend_back(
        cross_q, cross_keys, cross_values, cross_mask, cross_max, cross_sum, d_crossed
    )
    own_cross_k, own_cross_v = (
        lax.psum_scatter(
            d_cross_k.astype(jnp.bfloat16), "mem", scatter_dimension=1, tiled=True
        ).astype(jnp.float32),
        lax.psum_scatter(
            d_cross_v.astype(jnp.bfloat16), "mem", scatter_dimension=1, tiled=True
        ).astype(jnp.float32),
    )
    d_cross_kv = jnp.stack([own_cross_k, own_cross_v]).astype(b16)
    grad_cross_kv = jnp.einsum("snd,ksne->kde", memory, d_cross_kv, preferred_element_type=f32)
    grad_memory = jnp.einsum("ksne,kde->snd", d_cross_kv, cross_w[1:], preferred_element_type=f32)
    d_cross_low = d_cross_q.astype(b16)
    grad_cross_q = jnp.einsum("srd,sre->de", h2, d_cross_low, preferred_element_type=f32)
    d_h2 = jnp.einsum("sre,de->srd", d_cross_low, cross_w[0], preferred_element_type=f32)
    d_x1, gain_one, shift_one = norm1_back(d_h2)
    grad_one = grad_two + d_x1
    grad_cross_w = jnp.concatenate([grad_cross_q[None], grad_cross_kv], 0)
    grad_one_low = grad_one.astype(b16)
    grad_self_proj = jnp.einsum("srd,sre->de", attended, grad_one_low, preferred_element_type=f32)
    d_attended = jnp.einsum(
        "sre,de->srd", grad_one_low, self_proj, preferred_element_type=f32
    ).astype(b16)
    d_query, d_keys, values_gradient = attend_back(
        qkv[0], keys_all, values_all, self_mask, self_max, self_sum, d_attended
    )
    own_keys, own_values = (
        lax.psum_scatter(
            d_keys.astype(jnp.bfloat16), "mem", scatter_dimension=1, tiled=True
        ).astype(jnp.float32),
        lax.psum_scatter(
            values_gradient.astype(jnp.bfloat16), "mem", scatter_dimension=1, tiled=True
        ).astype(jnp.float32),
    )
    d_qkv = jnp.stack([d_query, own_keys, own_values]).astype(b16)
    grad_self_w = jnp.einsum("srd,ksre->kde", h1, d_qkv, preferred_element_type=f32)
    d_h1 = jnp.einsum("ksre,kde->srd", d_qkv, self_w, preferred_element_type=f32)
    d_x0, gain_zero, shift_zero = norm0_back(d_h1)
    grad_tokens = grad_one + d_x0
    gain_grads = jnp.stack([gain_zero, gain_one, gain_two])
    shift_grads = jnp.stack([shift_zero, shift_one, shift_two])
    full_grads = (
        grad_self_w,
        grad_self_proj,
        grad_cross_w,
        grad_cross_proj,
        grad_inner,
        grad_outer,
        grad_inner_bias,
        grad_outer_bias,
        gain_grads,
        shift_grads,
    )
    shards = (
        lax.psum_scatter(
            full_grads[0].astype(jnp.bfloat16), "fsdp", scatter_dimension=1, tiled=True
        ).astype(jnp.float32),
        lax.psum_scatter(
            full_grads[1].astype(jnp.bfloat16), "fsdp", scatter_dimension=0, tiled=True
        ).astype(jnp.float32),
        lax.psum_scatter(
            full_grads[2].astype(jnp.bfloat16), "fsdp", scatter_dimension=1, tiled=True
        ).astype(jnp.float32),
        lax.psum_scatter(
            full_grads[3].astype(jnp.bfloat16), "fsdp", scatter_dimension=0, tiled=True
        ).astype(jnp.float32),
        lax.psum_scatter(
            full_grads[4].astype(jnp.bfloat16), "fsdp", scatter_dimension=0, tiled=True
        ).astype(jnp.float32),
        lax.psum_scatter(
            full_grads[5].astype(jnp.bfloat16), "fsdp", scatter_dimension=0, tiled=True
        ).astype(jnp.float32),
        lax.psum_scatter(
            full_grads[6].astype(jnp.bfloat16), "fsdp", scatter_dimension=0, tiled=True
        ).astype(jnp.float32),
        lax.psum_scatter(
            full_grads[7].astype(jnp.bfloat16), "fsdp", scatter_dimension=0, tiled=True
        ).astype(jnp.float32),
        lax.psum_scatter(
            full_grads[8].astype(jnp.bfloat16), "fsdp", scatter_dimension=1, tiled=True
        ).astype(jnp.float32),
        lax.psum_scatter(
            full_grads[9].astype(jnp.bfloat16), "fsdp", scatter_dimension=1, tiled=True
        ).astype(jnp.float32),
    )
    totals = (
        lax.psum(shards[0].astype(jnp.bfloat16), "mem").astype(jnp.float32),
        lax.psum(shards[1].astype(jnp.bfloat16), "mem").astype(jnp.float32),
        lax.psum(shards[2].astype(jnp.bfloat16), "mem").astype(jnp.float32),
        lax.psum(shards[3].astype(jnp.bfloat16), "mem").astype(jnp.float32),
        lax.psum(shards[4].astype(jnp.bfloat16), "mem").astype(jnp.float32),
        lax.psum(shards[5].astype(jnp.bfloat16), "mem").astype(jnp.float32),
        lax.psum(shards[6].astype(jnp.bfloat16), "mem").astype(jnp.float32),
        lax.psum(shards[7].astype(jnp.bfloat16), "mem").astype(jnp.float32),
        lax.psum(shards[8].astype(jnp.bfloat16), "mem").astype(jnp.float32),
        lax.psum(shards[9].astype(jnp.bfloat16), "mem").astype(jnp.float32),
    )
    return (
        mixed,
        grad_tokens,
        grad_memory,
        totals[0],
        totals[1],
        totals[2],
        totals[3],
        totals[4],
        totals[5],
        totals[6],
        totals[7],
        totals[8],
        totals[9],
    )


def body(*args):
    if lax.axis_size("mem") == 2 and lax.axis_size("fsdp") == NZ * NY * NC:
        return paired_body(*args)
    return general_body(*args)


def solution(mesh):
    placed = (
        P("fsdp", "mem", None),
        P("fsdp", "mem", None),
        P("fsdp", "mem", None),
        P("fsdp"),
        P("fsdp"),
        P("fsdp"),
        P(None, "fsdp", None),
        P("fsdp", None),
        P(None, "fsdp", None),
        P("fsdp", None),
        P("fsdp", None),
        P("fsdp", None),
        P("fsdp"),
        P("fsdp"),
        P(None, "fsdp"),
        P(None, "fsdp"),
    )
    return jax.shard_map(
        body,
        mesh=mesh,
        in_specs=placed,
        out_specs=(
            P("fsdp", "mem", None),
            P("fsdp", "mem", None),
            P("fsdp", "mem", None),
            P(None, "fsdp", None),
            P("fsdp", None),
            P(None, "fsdp", None),
            P("fsdp", None),
            P("fsdp", None),
            P("fsdp", None),
            P("fsdp"),
            P("fsdp"),
            P(None, "fsdp"),
            P(None, "fsdp"),
        ),
        check_vma=False,
    )
```

```python
import jax
import jax.numpy as jnp
from jax import lax
from jax.experimental import pallas as pl
from jax.experimental.pallas import tpu as pltpu
from jax.sharding import PartitionSpec as P

F32 = jnp.float32
B16 = jnp.bfloat16
HEAD = 64
GROUP = 256
PER = GROUP // HEAD
EPSILON = 1e-05
NEG = -1000000000.0


def dot(a, b):
    return jnp.dot(a, b, preferred_element_type=F32)


def dot_nt(a, b):
    return lax.dot_general(a, b, (((1,), (1,)), ((), ())), preferred_element_type=F32)


def dot_tn(a, b):
    return lax.dot_general(a, b, (((0,), (0,)), ((), ())), preferred_element_type=F32)


def norm_parts(v):
    centre = v - jnp.mean(v, -1, keepdims=True)
    rs = lax.rsqrt(jnp.mean(centre * centre, -1, keepdims=True) + EPSILON)
    return centre * rs, rs


def norm_back(e, v, gain):
    n, rs = norm_parts(v)
    t = e * gain
    dx = rs * (t - jnp.mean(t, -1, keepdims=True) - n * jnp.mean(t * n, -1, keepdims=True))
    return dx, jnp.sum(e * n, 0, keepdims=True), jnp.sum(e, 0, keepdims=True)


def cols(g):
    return pl.ds(pl.multiple_of(g * GROUP, GROUP), GROUP)


def head_rows(h, rows, width):
    return lax.broadcasted_iota(jnp.int32, (rows, width), 0) // HEAD == h


def head_cols(h, rows, width):
    return lax.broadcasted_iota(jnp.int32, (rows, width), 1) // HEAD == h


def allowed_block(first_key, nk, first_query, nq, limit, causal):
    key = first_key + lax.broadcasted_iota(jnp.int32, (nk, nq), 0)
    ok = key < limit
    if causal:
        query = first_query + lax.broadcasted_iota(jnp.int32, (nk, nq), 1)
        ok = ok & (key <= query)
    return ok


def attend_back_group(
    q_ref, k_ref, v_ref, qi_, ki_, vi_, a_ref, da_ref, g, lse_ref, limit, causal, tq,
    qt, kt, at, dat, ps, dss, qm_ref, dm_ref, dqt, dk_acc, dv_acc, step=None,
):
    L = qt.shape[1]
    K = kt.shape[1]
    scale = HEAD**-0.5
    qt[...] = (q_ref[qi_].astype(F32) * scale).T.astype(B16)
    kt[...] = (k_ref[ki_].astype(F32) * scale).T.astype(B16)
    at[...] = a_ref[:, cols(g)].astype(F32).T.astype(B16)
    dat[...] = da_ref[:, cols(g)].astype(F32).T.astype(B16)

    def keys(i):
        return (i + 1) * tq if causal else K

    def front(i, h):
        nk, span = keys(i), slice(i * tq, (i + 1) * tq)
        here = head_rows(h, GROUP, tq)
        block = qt[:, span]
        s = dot(k_ref[ki_ + (pl.ds(0, nk),)], jnp.where(here, block, jnp.zeros_like(block)))
        block = dat[:, span]
        dp = dot(v_ref[vi_ + (pl.ds(0, nk),)], jnp.where(here, block, jnp.zeros_like(block)))
        return s, dp

    def middle(i, h, s, dp):
        nk, span = keys(i), slice(i * tq, (i + 1) * tq)
        hs = slice(h * HEAD, (h + 1) * HEAD)
        delta = jnp.sum(at[hs, span].astype(F32) * dat[hs, span].astype(F32), 0, keepdims=True)
        s = mask_scores(s, nk, i * tq, tq, limit, causal)
        p = jnp.exp(s - lse_ref[g, h : h + 1, span])
        ds = (p * (dp - delta)).astype(B16)
        ps[0:nk, h * tq : (h + 1) * tq] = p.astype(B16)
        dss[0:nk, h * tq : (h + 1) * tq] = ds
        mine = head_cols(h, tq, GROUP)
        qn = q_ref[qi_ + (pl.ds(i * tq, tq),)] * jnp.asarray(scale, B16)
        dn = da_ref[pl.ds(i * tq, tq), cols(g)]
        qm_ref[h * tq : (h + 1) * tq] = jnp.where(mine, qn, jnp.zeros_like(qn))
        dm_ref[h * tq : (h + 1) * tq] = jnp.where(mine, dn, jnp.zeros_like(dn))
        return ds

    def back(i, h, ds):
        nk, span = keys(i), slice(i * tq, (i + 1) * tq)
        hs = slice(h * HEAD, (h + 1) * HEAD)
        dqt[hs, span] = dot(kt[hs, 0:nk], ds).astype(B16)

    def close(i):
        nk = keys(i)
        dvi = dot(ps[0:nk], dm_ref[...])
        dki = dot(dss[0:nk], qm_ref[...])
        if i == tiles[0]:
            dv_acc[0:nk] = dvi
            dk_acc[0:nk] = dki
        else:
            dv_acc[0:nk] += dvi
            dk_acc[0:nk] += dki

    tiles = list(range(L // tq))[::-1]
    order = [(i, h) for i in tiles for h in range(PER)]
    ahead = front(*order[0])
    late = None
    for n, (i, h) in enumerate(order):
        now = ahead
        if h < PER - 1:
            ahead = front(*order[n + 1])
        ds = middle(i, h, *now)
        if late is not None:
            back(*late)
        late = (i, h, ds)
        if h == PER - 1:
            if n + 1 < len(order):
                ahead = front(*order[n + 1])
            back(*late)
            late = None
            close(i)
            if step is not None:
                step(tiles.index(i))


def mask_scores(s, nk, q0, tq, limit, causal):
    if causal and nk > tq:
        top = jnp.where(allowed_block(0, nk - tq, q0, tq, limit, False), s[: nk - tq], NEG)
        bottom = jnp.where(allowed_block(nk - tq, tq, q0, tq, limit, True), s[nk - tq :], NEG)
        return jnp.concatenate([top, bottom], 0)
    return jnp.where(allowed_block(0, nk, q0, tq, limit, causal), s, NEG)


def attend_group(q_ref, k_ref, v_ref, qi_, ki_, vi_, out_ref, g, lse_ref, limit, causal, tq, qt, vt, ot, step=None):
    L = qt.shape[1]
    K = vt.shape[1]
    qt[...] = (q_ref[qi_].astype(F32) * HEAD**-0.5).T.astype(B16)
    vt[...] = v_ref[vi_].astype(F32).T.astype(B16)

    def keys(i):
        return (i + 1) * tq if causal else K

    def front(i, h):
        block = qt[:, i * tq : (i + 1) * tq]
        qm = jnp.where(head_rows(h, GROUP, tq), block, jnp.zeros_like(block))
        return dot(k_ref[ki_ + (pl.ds(0, keys(i)),)], qm)

    def middle(i, h, s):
        s = mask_scores(s, keys(i), i * tq, tq, limit, causal)
        m = jnp.max(s, 0, keepdims=True)
        e = jnp.exp(s - m)
        total = jnp.sum(e, 0, keepdims=True)
        lse_ref[g, h : h + 1, i * tq : (i + 1) * tq] = m + jnp.log(total)
        return (e * (1.0 / total)).astype(B16)

    def back(i, h, p):
        hs = slice(h * HEAD, (h + 1) * HEAD)
        ot[hs, i * tq : (i + 1) * tq] = dot(vt[hs, 0 : keys(i)], p).astype(B16)

    order = [(i, h) for i in range(L // tq) for h in range(PER)]
    ahead = front(*order[0])
    late = None
    for n, (i, h) in enumerate(order):
        now = ahead
        if n + 1 < len(order):
            ahead = front(*order[n + 1])
        p = middle(i, h, now)
        if late is not None:
            back(*late)
        late = (i, h, p)
        if step is not None and h == PER - 1:
            step(i)
    back(*late)
    out_ref[:, cols(g)] = ot[...].astype(F32).T.astype(B16)


ERFCX = (
    0.21161358920977177, 0.2106475215974073, 0.20533035663075158, 0.12143152976148842,
    0.27391662866419597, -0.22972237163936396, 0.432698311257476, -0.287490481514182,
    0.06157492612604076,
)


def gelu_parts(u):
    t = 1.0 / (1.0 + (0.375 * 0.7071067811865476) * jnp.abs(u))
    poly = jnp.full_like(t, 0.5 * ERFCX[8])
    for c in ERFCX[7::-1]:
        poly = poly * t + 0.5 * c
    bell = jnp.exp(u * (-0.5 * u))
    half = (poly * t) * bell
    cdf = jnp.where(u >= 0, 1.0 - half, half)
    return u * cdf, cdf + u * (bell * 0.3989422804014327)


ROWS = 256

VMEM = pltpu.VMEM
SMEM_SPEC = pl.BlockSpec(memory_space=pltpu.SMEM)


MESH = pl.DeviceIdType.MESH
NZ, NY, NC = 4, 2, 2
ANY_SPEC = pl.BlockSpec(memory_space=pl.ANY)
HBM_SPEC = pl.BlockSpec(memory_space=pltpu.HBM)
DMA = pltpu.SemaphoreType.DMA
SMALL = 16


class Place:
    def __init__(self):
        i = lax.axis_index("fsdp")
        self.x = lax.axis_index("mem")
        self.i = i
        self.z, self.y, self.c = i // (NY * NC), (i // NC) % NY, i % NC
        self.other_x, self.other_y, self.other_c = 1 - self.x, 1 - self.y, 1 - self.c

    def at_z(self, z):
        return (self.x, (z * NY + self.y) * NC + self.c)

    def ahead(self, r):
        return lax.rem(self.z + r, NZ)

    def behind(self, r):
        return lax.rem(self.z + NZ - r, NZ)

    def peer_y(self):
        return (self.x, (self.z * NY + self.other_y) * NC + self.c)

    def peer_c(self):
        return (self.x, (self.z * NY + self.y) * NC + self.other_c)

    def peer_x(self):
        return (self.other_x, self.i)

    def greet(self):
        barrier = pltpu.get_barrier_semaphore()
        peers = [self.at_z(self.ahead(r)) for r in (1, 2, 3)] + [self.peer_y(), self.peer_c(), self.peer_x()]
        for peer in peers:
            pl.semaphore_signal(barrier, inc=1, device_id=peer, device_id_type=MESH)
        pl.semaphore_wait(barrier, len(peers))


def remote(src, dst, sems, index, peer):
    return pltpu.make_async_remote_copy(
        src_ref=src, dst_ref=dst, send_sem=sems.at[(0,) + index], recv_sem=sems.at[(1,) + index],
        device_id=peer, device_id_type=MESH)


class Gather:
    def __init__(self, place, ref, zsem, ysem, csem):
        self.p, self.ref, self.zsem, self.ysem, self.csem = place, ref, zsem, ysem, csem

    def block(self, lead, z):
        return self.ref.at[lead + (z, self.p.y, self.p.c)]

    def z_send(self, lead, r):
        mine = self.block(lead, self.p.z)
        return remote(mine, mine, self.zsem, lead + (r - 1,), self.p.at_z(self.p.ahead(r)))

    def z_land(self, lead, r):
        slot = self.block(lead, self.p.behind(r))
        return remote(slot, slot, self.zsem, lead + (r - 1,), self.p.at_z(self.p.behind(r)))

    def column(self, lead, y, c):
        return self.ref.at[lead + (slice(None), y, c)]

    def y_copy(self, lead, y):
        part = self.column(lead, y, self.p.c)
        return remote(part, part, self.ysem, lead, self.p.peer_y())

    def c_copy(self, lead, k, y, c):
        part = self.column(lead, y, c)
        return remote(part, part, self.csem, lead + (k,), self.p.peer_c())

    def begin(self, lead):
        for r in (1, 2, 3):
            self.z_send(lead, r).start()

    def spread(self, lead):
        for r in (1, 2, 3):
            self.z_land(lead, r).wait_recv()
        self.y_copy(lead, self.p.y).start()
        self.c_copy(lead, 0, self.p.y, self.p.c).start()

    def finish(self, lead):
        self.y_copy(lead, self.p.other_y).wait_recv()
        self.c_copy(lead, 1, self.p.other_y, self.p.c).start()

    def ready(self, lead):
        self.c_copy(lead, 0, self.p.y, self.p.other_c).wait_recv()
        self.c_copy(lead, 1, self.p.other_y, self.p.other_c).wait_recv()

    def sent(self, lead):
        for r in (1, 2, 3):
            self.z_send(lead, r).wait_send()
        self.y_copy(lead, self.p.y).wait_send()
        self.c_copy(lead, 0, self.p.y, self.p.c).wait_send()
        self.c_copy(lead, 1, self.p.other_y, self.p.c).wait_send()


class GatherIn(Gather):
    def tile(self, z, r):
        return lax.rem(z + r, NZ)

    def begin(self, r):
        for d in (1, 2, 3):
            self.send(r, d).start()

    def send(self, r, d):
        to = self.p.ahead(d)
        mine = self.block((self.tile(to, r),), self.p.z)
        return remote(mine, mine, self.zsem, (r, d - 1), self.p.at_z(to))

    def lead(self, r):
        return (self.tile(self.p.z, r),)

    def y_in(self, r, y):
        part = self.column(self.lead(r), y, self.p.c)
        return remote(part, part, self.ysem, (r,), self.p.peer_y())

    def c_in(self, r, k, y, c):
        part = self.column(self.lead(r), y, c)
        return remote(part, part, self.csem, (r, k), self.p.peer_c())

    def spread(self, r):
        for d in (1, 2, 3):
            slot = self.block(self.lead(r), self.p.behind(d))
            remote(slot, slot, self.zsem, (r, d - 1), self.p.at_z(self.p.behind(d))).wait_recv()
        self.y_in(r, self.p.y).start()
        self.c_in(r, 0, self.p.y, self.p.c).start()

    def finish(self, r):
        self.y_in(r, self.p.other_y).wait_recv()
        self.c_in(r, 1, self.p.other_y, self.p.c).start()

    def ready(self, r):
        self.c_in(r, 0, self.p.y, self.p.other_c).wait_recv()
        self.c_in(r, 1, self.p.other_y, self.p.other_c).wait_recv()

    def sent(self, r):
        for d in (1, 2, 3):
            self.send(r, d).wait_send()
        self.y_in(r, self.p.y).wait_send()
        self.c_in(r, 0, self.p.y, self.p.c).wait_send()
        self.c_in(r, 1, self.p.other_y, self.p.c).wait_send()


class GatherHalves(Gather):
    def __init__(self, place, ref, first, zsem, ysem, xsem, csem):
        super().__init__(place, ref, zsem, ysem, csem)
        self.first, self.xsem = first, xsem
        half = ref.shape[-1] // 2
        self.mine = pl.ds(pl.multiple_of(place.x * half, half), half)
        self.theirs = pl.ds(pl.multiple_of(place.other_x * half, half), half)

    def z_send(self, n, r):
        part = self.ref.at[n, self.p.z, self.p.y, self.p.c, :, self.mine]
        return remote(part, part, self.zsem, (n - self.first, r - 1), self.p.at_z(self.p.ahead(r)))

    def z_land(self, n, r):
        part = self.ref.at[n, self.p.behind(r), self.p.y, self.p.c, :, self.mine]
        return remote(part, part, self.zsem, (n - self.first, r - 1), self.p.at_z(self.p.behind(r)))

    def part(self, n, y, c, columns):
        return self.ref.at[n, :, y, c, :, columns]

    def y_half(self, n, y):
        part = self.part(n, y, self.p.c, self.mine)
        return remote(part, part, self.ysem, (n - self.first,), self.p.peer_y())

    def x_half(self, n, k, y, columns):
        part = self.part(n, y, self.p.c, columns)
        return remote(part, part, self.xsem, (n - self.first, k), self.p.peer_x())

    def c_half(self, n, k, y, c, columns):
        part = self.part(n, y, c, columns)
        return remote(part, part, self.csem, (n - self.first, k), self.p.peer_c())

    def quarters(self):
        return ((0, self.p.y, self.mine), (1, self.p.other_y, self.mine), (2, self.p.y, self.theirs), (3, self.p.other_y, self.theirs))

    def spread(self, n):
        for r in (1, 2, 3):
            self.z_land(n, r).wait_recv()
        self.x_half(n, 0, self.p.y, self.mine).start()
        self.y_half(n, self.p.y).start()
        self.c_half(n, 0, self.p.y, self.p.c, self.mine).start()

    def finish(self, n):
        self.y_half(n, self.p.other_y).wait_recv()
        self.x_half(n, 1, self.p.other_y, self.mine).start()
        self.c_half(n, 1, self.p.other_y, self.p.c, self.mine).start()

    def relay(self, n):
        for k, y in ((0, self.p.y), (1, self.p.other_y)):
            self.x_half(n, k, y, self.theirs).wait_recv()
            self.c_half(n, 2 + k, y, self.p.c, self.theirs).start()

    def ready(self, n):
        for k, y, columns in self.quarters():
            self.c_half(n, k, y, self.p.other_c, columns).wait_recv()

    def sent(self, n):
        for r in (1, 2, 3):
            self.z_send(n, r).wait_send()
        self.y_half(n, self.p.y).wait_send()
        for k, y in ((0, self.p.y), (1, self.p.other_y)):
            self.x_half(n, k, y, self.mine).wait_send()
        for k, y, columns in self.quarters():
            self.c_half(n, k, y, self.p.c, columns).wait_send()


class GatherOut:
    def __init__(self, place, ref, zsem, ysem, xsem, csem):
        self.p, self.ref, self.zsem, self.ysem, self.xsem, self.csem = place, ref, zsem, ysem, xsem, csem
        half = ref.shape[-1] // 2
        self.mine = pl.ds(pl.multiple_of(place.x * half, half), half)
        self.theirs = pl.ds(pl.multiple_of(place.other_x * half, half), half)

    def block(self, z, y, c, columns):
        return self.ref.at[z, y, c, :, columns]

    def z_copy(self, r, src_z, to):
        part = self.block(src_z, self.p.y, self.p.c, self.mine)
        return remote(part, part, self.zsem, (r,), self.p.at_z(to))

    def y_copy(self, r, y):
        part = self.block(self.p.ahead(r), y, self.p.c, self.mine)
        return remote(part, part, self.ysem, (r,), self.p.peer_y())

    def x_copy(self, r, k, y, columns):
        part = self.block(self.p.ahead(r), y, self.p.c, columns)
        return remote(part, part, self.xsem, (r, k), self.p.peer_x())

    def c_copy(self, r, k, y, c, columns):
        part = self.block(self.p.ahead(r), y, c, columns)
        return remote(part, part, self.csem, (r, k), self.p.peer_c())

    def begin(self, r):
        self.z_copy(r, self.p.z, self.p.behind(r)).start()

    def spread(self, r, landed=True):
        if landed:
            self.z_copy(r, self.p.ahead(r), self.p.ahead(r)).wait_recv()
        if r:
            self.x_copy(r, 0, self.p.y, self.mine).start()
        self.y_copy(r, self.p.y).start()
        self.c_copy(r, 0, self.p.y, self.p.c, self.mine).start()

    def finish(self, r):
        self.y_copy(r, self.p.other_y).wait_recv()
        self.x_copy(r, 1, self.p.other_y, self.mine).start()
        self.c_copy(r, 1, self.p.other_y, self.p.c, self.mine).start()

    def relay(self, r):
        for k, y in ((0, self.p.y), (1, self.p.other_y)):
            if r or k:
                self.x_copy(r, k, y, self.theirs).wait_recv()
            self.c_copy(r, 2 + k, y, self.p.c, self.theirs).start()

    def ready(self, r):
        for k, y, columns in ((0, self.p.y, self.mine), (1, self.p.other_y, self.mine), (2, self.p.y, self.theirs), (3, self.p.other_y, self.theirs)):
            self.c_copy(r, k, y, self.p.other_c, columns).wait_recv()

    def sent(self, r, began=True):
        if began:
            self.z_copy(r, self.p.z, self.p.behind(r)).wait_send()
        self.y_copy(r, self.p.y).wait_send()
        for k, y in ((0, self.p.y), (1, self.p.other_y)):
            if r or k:
                self.x_copy(r, k, y, self.mine).wait_send()
        for k, y, columns in ((0, self.p.y, self.mine), (1, self.p.other_y, self.mine), (2, self.p.y, self.theirs), (3, self.p.other_y, self.theirs)):
            self.c_copy(r, k, y, self.p.c, columns).wait_send()


def unpack_small(v):
    n = NZ * NY * NC
    D = 48 * n
    total = jnp.zeros((8, D), F32)
    tiles = jnp.zeros((8, D), F32)
    lane = lax.broadcasted_iota(jnp.int32, (8, 256), 1)
    row = lax.broadcasted_iota(jnp.int32, (8, D), 0)
    for i in range(n):
        block = v[i // 4, (i // 2) % 2, i % 2]
        pad = jnp.zeros((8, D - 256), F32)
        total = total + roll_lanes(jnp.concatenate([jnp.where(lane < 48, block, 0.0), pad], 1), 48 * i)
        wide = roll_lanes(jnp.concatenate([jnp.where(lane < 192, block, 0.0), pad], 1), 192 * (i % 4))
        tiles = tiles + jnp.where(row == i // 4, jnp.broadcast_to(wide[7:8], wide.shape), 0.0)
    return jnp.concatenate([total, tiles], 0)


def roll_lanes(v, by):
    return pltpu.roll(v, by, 1) if by else v


def flat(v):
    return v.reshape(-1, v.shape[-1])


PRE, SELF, NEXT, CROSS, FEED, LATE, TAIL = range(7)
BP, SP, FP, LP, RP, BI, SI, FI, BO, SO, FO, LO, TE, RA, XB, XA, PY, PZ, PX, TX, TY, TZ, TF, ME, SY, SZ, SX = range(27)
SPLIT = (5, 6, 7)
FORWARD_PLAN = {
    (PRE, 0, 0): ((SO, 0), (TE, 0), (BP, 0),),
    (PRE, 1, 0): ((BP, 1), (SP, 0),),
    (PRE, 2, 0): ((BP, 5), (FP, 0), (BP, 2), (SP, 1), (SP, 5), (TE, 2), (BP, 6),),
    (PRE, 3, 0): ((BP, 3),),
    (SELF, 0, 0): ((SP, 6),),
    (SELF, 0, 1): ((SP, 2), (FP, 1),),
    (SELF, 0, 2): ((BP, 4),),
    (SELF, 1, 0): ((FP, 5), (TE, 1),),
    (SELF, 1, 1): ((SP, 3), (FP, 6),),
    (SELF, 1, 2): ((BO, 1), (FP, 2), (BP, 7),),
    (SELF, 2, 0): ((SP, 4),),
    (SELF, 2, 1): ((BI, 0),),
    (SELF, 2, 2): ((FP, 3),),
    (SELF, 2, 3): ((SP, 7),),
    (NEXT, 1, 0): ((FP, 4), (SO, 1), (BI, 1),),
    (CROSS, 0, 1): ((LP, 5), (FP, 7),),
    (CROSS, 0, 2): ((SI, 0),),
    (CROSS, 0, 3): ((BO, 2), (LP, 6),),
    (CROSS, 1, 0): ((BI, 3),),
    (CROSS, 1, 3): ((BO, 3),),
    (CROSS, 2, 0): ((FO, 0), (SI, 1),),
    (CROSS, 2, 1): ((LP, 7),),
    (CROSS, 2, 2): ((FO, 1),),
    (CROSS, 2, 3): ((FI, 0),),
    (NEXT, 2, 0): ((LO, 0), (BI, 2), (SO, 3), (LO, 1), (FI, 1), (SO, 2),),
    (FEED, 0, 3): ((SI, 2), (FO, 2),),
    (FEED, 1, 0): ((RA, 0),),
    (FEED, 1, 1): ((SI, 3), (LO, 2),),
    (FEED, 1, 2): ((FO, 3), (FI, 2), (XB, 0),),
    (FEED, 2, 1): ((RA, 1),),
    (FEED, 2, 2): ((LO, 3), (FI, 3),),
    (FEED, 3, 1): ((RA, 2),),
    (FEED, 3, 4): ((XA, 0),),
    (TAIL, 0, 0): ((RA, 3),),
}


def run_plan(plan, steps, point):
    for kind, n in plan.get(point, ()):
        steps[kind](n)


def run_plan_at(plan, steps, prefix, index, count, i):
    for at in range(count):
        point = (prefix, at, i)
        if point in plan:

            @pl.when(index == at)
            def _(point=point):
                run_plan(plan, steps, point)


def forward_kernel(
    tlen, mlen, flag, tokens_h, memory_h, cot_h, sw_h, sp_h, cw_h, cp_h, wi_h, wo_h, small_h,
    mixed_h, tok_h, h1_h, qkv_h, a_h, lse_h, x1_h, mem_h, h2_h, cq_h, ckv_h, c_h, clse_h, g2_h, w_h, s1i_h, s1o_h, s2i_h, s2o_h, vecs_h, gbi_h, gains_h,
    W, WI, WO, V, tok, mem, cot, vec, h1, qkv, a, lse, x1, h2, ckv, clse, x2, h3t, acc, dh3, gwi, gwo, rci, rco, rxi, rxo,
    qt, vt, vtc, ot, gbi, vout,
    wz, wy, wc, iz, iy, ic, oz, oy, ox, oc, hz, hy, hx, hc, vz, vy, vc, xs, rs_sem, rx_sem, loc, spill_sem,
):
    p = Place()
    L, D = tok.shape
    half = L // 2
    M = mem.shape[0]
    FT = WI.shape[-1]
    local = []

    def fetch(src, dst):
        cp = pltpu.make_async_copy(src, dst, loc.at[len(local)])
        cp.start()
        local.append(cp)
        return cp

    me = (p.z, p.y, p.c)
    pieces = [[] for _ in range(8)]
    for n in SPLIT:
        if n < 7:
            g = n - 4
            for k in range(3):
                pieces[n].append(fetch(cw_h.at[k, :, pl.ds(g * GROUP, GROUP)], W.at[(n,) + me + (slice(None), pl.ds(k * GROUP, GROUP))]))
    pieces[7].append(fetch(cp_h, W.at[(7,) + me]))
    small_cp = fetch(small_h, V.at[me])
    for g in range(3):
        for k in range(3):
            pieces[g].append(fetch(sw_h.at[k, :, pl.ds(g * GROUP, GROUP)], W.at[(g,) + me + (slice(None), pl.ds(k * GROUP, GROUP))]))
    tok_cp = fetch(tokens_h.at[p.x], tok.at[pl.ds(pl.multiple_of(p.x * half, half), half)])
    pieces[3].append(fetch(sp_h, W.at[(3,) + me]))
    for g in range(3):
        for k in range(3):
            if 4 + g not in SPLIT:
                pieces[4 + g].append(fetch(cw_h.at[k, :, pl.ds(g * GROUP, GROUP)], W.at[(4 + g,) + me + (slice(None), pl.ds(k * GROUP, GROUP))]))
    mem_cp = fetch(memory_h.at[p.x], mem.at[pl.ds(pl.multiple_of(p.x * (M // 2), M // 2), M // 2)])
    in_cp = [fetch(wi_h.at[:, pl.ds(t * FT, FT)], WI.at[(t,) + me]) for t in range(NZ)]
    out_cp = fetch(wo_h, WO.at[me])
    cot_cp = fetch(cot_h.at[p.x], cot.at[pl.ds(pl.multiple_of(p.x * half, half), half)])

    for n in SPLIT:
        for cp in pieces[n]:
            cp.wait()
    p.greet()
    gw = Gather(p, W, wz, wy, wc)
    gh = GatherHalves(p, W, SPLIT[0], hz, hy, hx, hc)
    gi = GatherIn(p, WI, iz, iy, ic)
    go = GatherOut(p, WO, oz, oy, ox, oc)
    gv = Gather(p, V, vz, vy, vc)

    def x_part(src_h, dst, rows, k):
        send = remote(src_h.at[p.other_x], dst.at[pl.ds(pl.multiple_of(p.x * rows, rows), rows)], xs, (k,), p.peer_x())
        land = dst.at[pl.ds(pl.multiple_of(p.other_x * rows, rows), rows)]
        return send, remote(src_h.at[p.other_x], land, xs, (k,), p.peer_x())

    tok_send, tok_land = x_part(tokens_h, tok, half, 0)
    mem_send, mem_land = x_part(memory_h, mem, M // 2, 1)
    cot_send, cot_land = x_part(cot_h, cot, half, 2)
    small_cp.wait()
    gv.begin(())

    def piece(method, halves):
        def step(n):
            if n in SPLIT:
                getattr(gh, halves)(n)
            else:
                getattr(gw, method)((n,))

        return step

    steps = {
        BP: piece("begin", "begin"), SP: piece("spread", "spread"), FP: piece("finish", "finish"), LP: gh.relay,
        RP: piece("ready", "ready"), BI: gi.begin, SI: gi.spread, FI: gi.finish,
        BO: go.begin, SO: lambda r: go.spread(r, r > 0), FO: go.finish, LO: go.relay,
        TE: lambda k: (tok_send, mem_send, cot_send)[k].start(),
    }
    for n, cps in enumerate(pieces):
        for cp in cps:
            if n not in SPLIT:
                cp.wait()
    for cp in in_cp + [out_cp, mem_cp, cot_cp]:
        cp.wait()

    def point(name):
        run_plan(FORWARD_PLAN, steps, name)

    point((PRE, 0, 0))
    gv.spread(())
    gv.finish(())
    gv.ready(())
    vec[...] = unpack_small(V)
    gains, shifts = vec, vec
    GAIN, SHIFT, BOUT, BIN = 0, 3, 6, 8

    def norm_rows(src, dst, k, start, count):
        for r in range(0, count, ROWS):
            rs = pl.ds(pl.multiple_of(start + r, ROWS), ROWS)
            n, _ = norm_parts(src[rs].astype(F32))
            dst[rs] = (n * gains[GAIN + k : GAIN + k + 1] + shifts[SHIFT + k : SHIFT + k + 1]).astype(B16)

    point((PRE, 1, 0))
    tok_cp.wait()
    norm_rows(tok, h1, 0, p.x * half, half)
    point((PRE, 2, 0))
    tok_land.wait_recv()
    norm_rows(tok, h1, 0, p.other_x * half, half)
    point((PRE, 3, 0))

    spills = []

    def spill(src, dst):
        cp = pltpu.make_async_copy(src, dst, spill_sem.at[len(spills)])
        cp.start()
        spills.append(cp)
        return cp

    tok_spill = spill(tok, tok_h)
    h1_spill = spill(h1, h1_h)

    def self_group(g, _):
        gw.ready((g,))
        for r in range(0, L, ROWS):
            rs = pl.ds(r, ROWS)
            out = dot(h1[rs], flat(W[g])).astype(B16)
            for k in range(3):
                qkv[k, g, rs] = out[:, k * GROUP : (k + 1) * GROUP]

        def step(i):
            run_plan_at(FORWARD_PLAN, steps, SELF, g, 3, i)

        attend_group(qkv, qkv, qkv, (0, g), (1, g), (2, g), a, g, lse, tlen[p.x], True, 256, qt, vt, ot, step)
        return 0

    lax.fori_loop(0, 3, self_group, 0)
    qkv_spill = spill(qkv, qkv_h)
    a_spill = spill(a, a_h)
    spill(lse, lse_h)
    steps[RP](3)
    for r in range(0, L, ROWS):
        rs = pl.ds(r, ROWS)
        x1[rs] = tok[rs].astype(F32) + dot(a[rs], flat(W[3]))
        norm_rows(x1, h2, 1, r, ROWS)
    point((NEXT, 1, 0))
    mem_land.wait_recv()
    spill(mem, mem_h)
    spill(x1, x1_h)
    h2_spill = spill(h2, h2_h)
    tok_spill.wait()
    qkv_spill.wait()
    c = tok
    cq = qkv.at[0]

    def cross_group(g, _):
        for k in range(3):

            @pl.when(g == k)
            def _(k=k):
                steps[RP](4 + k)

        for r in range(0, L, ROWS):
            rs = pl.ds(r, ROWS)
            cq[g, rs] = dot(h2[rs], flat(W[4 + g, :, :, :, :, 0:GROUP])).astype(B16)
        kv = dot(mem[...], flat(W[4 + g, :, :, :, :, GROUP : 3 * GROUP])).astype(B16)
        ckv[0, g] = kv[:, :GROUP]
        ckv[1, g] = kv[:, GROUP:]

        def step(i):
            run_plan_at(FORWARD_PLAN, steps, CROSS, g, 3, i)

        attend_group(cq, ckv, ckv, (g,), (0, g), (1, g), c, g, clse, mlen[p.x], False, 256, qt, vtc, ot, step)
        return 0

    lax.fori_loop(0, 3, cross_group, 0)
    spill(cq, cq_h)
    spill(ckv, ckv_h)
    spill(c, c_h)
    spill(clse, clse_h)
    steps[RP](7)
    f = flag[p.x].astype(F32)
    h1_spill.wait()
    a_spill.wait()
    h2_spill.wait()
    h3, act, dpre = h1, h2, a
    for r in range(0, L, ROWS):
        rs = pl.ds(r, ROWS)
        x2[rs] = x1[rs] + f * dot(c[rs], flat(W[7]))
        n, _ = norm_parts(x2[rs])
        h = n * gains[GAIN + 2 : GAIN + 3] + shifts[SHIFT + 2 : SHIFT + 3]
        h3[rs] = h.astype(B16)
        h3t[:, r : r + ROWS] = h.T.astype(B16)
        acc[rs] = x2[rs] + vec[BOUT : BOUT + 1]
        dh3[rs] = jnp.zeros((ROWS, D), F32)
    point((NEXT, 2, 0))
    spill(W, w_h)
    cot_land.wait_recv()
    gb_out = jnp.zeros((1, D), F32)
    for r in range(0, L, ROWS):
        gb_out += jnp.sum(cot[pl.ds(r, ROWS)].astype(F32), 0, keepdims=True)
    vout[2:3] = gb_out

    def reduce_copy(r, which):
        if which == 0:
            return remote(gwi.at[:, :, p.other_c], rci.at[r], rs_sem, (r, 0), p.peer_c())
        return remote(gwo.at[:, p.other_c], rco.at[r], rs_sem, (r, 1), p.peer_c())

    def reduce_add(r):
        reduce_copy(r, 0).wait()
        for k in range(NZ):
            rci[r, k] = (rci[r, k].astype(F32) + gwi[k, :, p.c].astype(F32)).astype(B16)
        reduce_copy(r, 1).wait()
        for k in range(NY):
            rco[r, k] = (rco[r, k].astype(F32) + gwo[k, p.c].astype(F32)).astype(B16)

    def x_copy(r, which):
        if which == 0:
            return remote(rci.at[r, :, :, :, go.theirs], rxi, rx_sem, (0,), p.peer_x())
        return remote(rco.at[r, :, :, go.theirs], rxo, rx_sem, (1,), p.peer_x())

    def x_begin(r):
        x_copy(r, 0).start()
        x_copy(r, 1).start()

    def x_add(r):
        x_copy(r, 0).wait()
        for k in range(NZ):
            rxi[k] = (rxi[k].astype(F32) + rci[r, k, :, :, go.mine].astype(F32)).astype(B16)
        x_copy(r, 1).wait()
        for k in range(NY):
            rxo[k] = (rxo[k].astype(F32) + rco[r, k, :, go.mine].astype(F32)).astype(B16)

    steps.update({RA: reduce_add, XB: x_begin, XA: x_add})

    def out_rows(t, j):
        return flat(WO[t])[j * GROUP : (j + 1) * GROUP]

    def ffn_round(r, _):
        t = p.ahead(r)
        gi.ready(r)
        go.ready(r)
        b_in = vec[pl.ds(BIN + t, 1)]
        sums = [jnp.zeros((1, GROUP), F32) for _ in range(0, FT, GROUP)]

        def front(q, j):
            rs, js = pl.ds(q, ROWS), slice(j * GROUP, (j + 1) * GROUP)
            w = flat(WI[t, :, :, :, :, js])
            return dot(h3[rs], w) + b_in[:, js], dot_nt(cot[rs], out_rows(t, j))

        def middle(q, j, pre, d_act):
            rs, js = pl.ds(q, ROWS), slice(j * GROUP, (j + 1) * GROUP)
            up, slope = gelu_parts(pre)
            act[rs, js] = up.astype(B16)
            d = (d_act * slope).astype(B16)
            dpre[rs, js] = d
            sums[j] = sums[j] + jnp.sum(d.astype(F32), 0, keepdims=True)

        def back(q):
            rs = pl.ds(q, ROWS)
            acc[rs] += dot(act[rs], flat(WO[t]))
            dh3[rs] += dot_nt(dpre[rs], flat(WI[t]))

        order = [(q, j) for q in range(0, L, ROWS) for j in range(FT // GROUP)]
        ahead = front(*order[0])
        for n, (q, j) in enumerate(order):
            now = ahead
            if n + 1 < len(order):
                ahead = front(*order[n + 1])
            middle(q, j, *now)
            if j == FT // GROUP - 1:
                back(q)
            if n in (4, 8):
                run_plan_at(FORWARD_PLAN, steps, FEED, r, NZ, n // 4 - 1)

        for j in range(FT // GROUP):
            gbi[t, :, j * GROUP : (j + 1) * GROUP] = jnp.broadcast_to(sums[j], (8, GROUP))

        run_plan_at(FORWARD_PLAN, steps, FEED, r, NZ, 2)
        for j in range(0, D, GROUP):
            part = dot_tn(act[...], cot[:, j : j + GROUP]).astype(B16)
            gwo[:, :, :, j : j + GROUP] = part.reshape(gwo.shape[:3] + (GROUP,))
        reduce_copy(r, 1).start()
        run_plan_at(FORWARD_PLAN, steps, FEED, r, NZ, 3)
        for j in range(0, FT, GROUP):
            part = dot(h3t[...], dpre[:, j : j + GROUP]).astype(B16)
            gwi[:, :, :, :, j : j + GROUP] = part.reshape(gwi.shape[:4] + (GROUP,))
        reduce_copy(r, 0).start()

        run_plan_at(FORWARD_PLAN, steps, FEED, r, NZ, 4)
        return 0

    lax.fori_loop(0, NZ, ffn_round, 0)
    mixed = act
    sg = jnp.zeros((1, D), F32)
    sb = jnp.zeros((1, D), F32)
    for r in range(0, L, ROWS):
        mixed[pl.ds(r, ROWS)] = acc[pl.ds(r, ROWS)].astype(B16)
    spill(mixed, mixed_h)
    for r in range(0, L, ROWS):
        rs = pl.ds(r, ROWS)
        dx, s, b = norm_back(dh3[rs], x2[rs], gains[GAIN + 2 : GAIN + 3])
        acc[rs] = cot[rs].astype(F32) + dx
        sg += s
        sb += b
    vout[0:1] = sg
    vout[1:2] = sb
    spill(acc, g2_h)
    spill(vout, vecs_h)
    spill(gbi, gbi_h)
    spill(vec, gains_h)
    point((TAIL, 0, 0))
    spill(rxi, s2i_h)
    spill(rxo, s2o_h)
    spill(rci.at[pl.ds(1, 3)], s1i_h)
    spill(rco.at[pl.ds(1, 3)], s1o_h)

    gv.sent(())
    for n in range(8):
        piece("sent", "sent")(n)
    for r in range(NZ):
        gi.sent(r)
        go.sent(r, r > 0)
    for cp in (tok_send, mem_send, cot_send):
        cp.wait_send()
    freed = (tok_spill, qkv_spill, h1_spill, a_spill, h2_spill)
    for cp in spills:
        if not any(cp is q for q in freed):
            cp.wait()


def forward_call(tlen, mlen, flag, tokens, memory, cot, sw, sp, cw, cp, wi, wo, small):
    _, half, D = tokens.shape
    L = 2 * half
    M = 2 * memory.shape[1]
    G = D // GROUP
    S = D // (NZ * NY * NC)
    FT = wi.shape[1] // NZ
    R = wo.shape[0]
    H = len(SPLIT)
    outs = [
        ((L, D), B16), ((L, D), B16), ((L, D), B16), ((3, G, L, GROUP), B16), ((L, D), B16), ((G, 8, L), F32),
        ((L, D), F32), ((M, D), B16), ((L, D), B16), ((G, L, GROUP), B16), ((2, G, M, GROUP), B16), ((L, D), B16),
        ((G, 8, L), F32), ((L, D), F32), ((8, NZ, NY, NC, S, D), B16), ((3, NZ, NY, S, FT), B16), ((3, NY, R, D), B16),
        ((NZ, NY, S, FT // 2), B16), ((NY, R, D // 2), B16), ((8, D), F32), ((NZ, 8, FT), F32), ((SMALL, D), F32),
    ]
    scratch = [
        ((8, NZ, NY, NC, S, D), B16), ((NZ, NZ, NY, NC, S, FT), B16), ((NZ, NY, NC, R, D), B16), ((NZ, NY, NC, 8, 256), F32),
        ((L, D), B16), ((M, D), B16), ((L, D), B16), ((SMALL, D), F32), ((L, D), B16), ((3, G, L, GROUP), B16), ((L, D), B16),
        ((G, 8, L), F32), ((L, D), F32), ((L, D), B16), ((2, G, M, GROUP), B16), ((G, 8, L), F32),
        ((L, D), F32), ((D, L), B16), ((L, D), F32), ((L, D), F32),
        ((NZ, NY, NC, S, FT), B16), ((NY, NC, R, D), B16), ((NZ, NZ, NY, S, FT), B16), ((NZ, NY, R, D), B16),
        ((NZ, NY, S, FT // 2), B16), ((NY, R, D // 2), B16),
        ((GROUP, L), B16), ((GROUP, L), B16), ((GROUP, M), B16), ((GROUP, L), B16), ((NZ, 8, FT), F32), ((8, D), F32),
    ]
    sems = [(2, 8, 3), (2, 8), (2, 8, 2), (2, 4, 3), (2, 4), (2, 4, 2), (2, 4), (2, 4), (2, 4, 2), (2, 4, 4), (2, H, 3), (2, H), (2, H, 2), (2, H, 4), (2, 3), (2,), (2, 2), (2, 4), (2, 4, 2), (2, 2), (40,), (24,)]
    return pl.pallas_call(
        forward_kernel,
        out_shape=[jax.ShapeDtypeStruct(s, d) for s, d in outs],
        in_specs=[SMEM_SPEC] * 3 + [ANY_SPEC] * 10,
        out_specs=[ANY_SPEC] * len(outs),
        scratch_shapes=[VMEM(s, d) for s, d in scratch] + [DMA(s) for s in sems],
        compiler_params=pltpu.CompilerParams(vmem_limit_bytes=63 * 1024 * 1024, collective_id=0, has_side_effects=True),
        name="forward",
    )(tlen, mlen, flag, tokens, memory, cot, sw, sp, cw, cp, wi, wo, small)


def pack_small(norm_gain, norm_bias, b_out, b_in):
    s = norm_gain.shape[1]
    rows = jnp.concatenate([norm_gain, norm_bias, b_out[None]], 0).astype(F32)
    rows = jnp.pad(rows, ((0, 0), (0, 256 - s)))
    return jnp.concatenate([rows, jnp.pad(b_in.astype(F32), (0, 256 - b_in.shape[0]))[None]], 0)


def quarter(n):
    return n % 4 if isinstance(n, int) else lax.rem(n, 4)


class Reduce:
    def __init__(self, place, G, rc, ry, rz, tot_h, rx_h, csem, ysem, zsem, xsem, lsem):
        self.p, self.G, self.rc, self.ry, self.rz, self.tot_h, self.rx_h = place, G, rc, ry, rz, tot_h, rx_h
        self.csem, self.ysem, self.zsem, self.xsem, self.lsem = csem, ysem, zsem, xsem, lsem

    def c_copy(self, n):
        return remote(self.G.at[quarter(n), :, :, self.p.other_c], self.rc.at[n], self.csem, (n,), self.p.peer_c())

    def y_copy(self, n):
        return remote(self.rc.at[n, :, self.p.other_y], self.ry.at[n], self.ysem, (n,), self.p.peer_y())

    def z_copy(self, n, r):
        to = self.p.ahead(r)
        return remote(self.ry.at[n, to], self.rz.at[n, r - 1], self.zsem, (n, r - 1), self.p.at_z(to))

    def x_copy(self, n):
        return remote(self.ry.at[n, self.p.z], self.rx_h.at[n], self.xsem, (n,), self.p.peer_x())

    def own_copy(self, n):
        return pltpu.make_async_copy(self.ry.at[n, self.p.z], self.tot_h.at[n], self.lsem.at[n])

    def over_c(self, n):
        self.c_copy(n).start()

    def over_y(self, n):
        self.c_copy(n).wait()
        for k in range(NZ):
            self.rc[n, k] = (self.rc[n, k].astype(F32) + self.G[quarter(n), k, :, self.p.c].astype(F32)).astype(B16)
        self.y_copy(n).start()

    def over_z(self, n):
        self.y_copy(n).wait_recv()
        for k in range(NZ):
            self.ry[n, k] = (self.ry[n, k].astype(F32) + self.rc[n, k, self.p.y].astype(F32)).astype(B16)
        for r in (1, 2, 3):
            self.z_copy(n, r).start()

    def over_x(self, n):
        for r in (1, 2, 3):
            self.z_copy(n, r).wait_recv()
        total = self.ry[n, self.p.z].astype(F32)
        for r in range(3):
            total = total + self.rz[n, r].astype(F32)
        self.ry[n, self.p.z] = total.astype(B16)
        self.x_copy(n).start()
        self.own_copy(n).start()

    def done(self, n):
        self.y_copy(n).wait_send()
        for r in (1, 2, 3):
            self.z_copy(n, r).wait_send()
        self.x_copy(n).wait()
        self.own_copy(n).wait()


class ReduceTiles:
    def __init__(self, place, s1i, s1o, s2i, s2o, own, land, outs, sems):
        self.p = place
        self.s1, self.s2 = (s1i, s1o), (s2i, s2o)
        self.own = own
        self.xi, self.xo, self.yi, self.yo, self.zi, self.zo = land
        self.outi_h, self.outo_h = outs
        self.xs, self.ys, self.zi_s, self.zo_s, self.fi, self.fo, self.lsem = sems
        half = s2i.shape[-1]
        self.mine = pl.ds(pl.multiple_of(place.x * half, half), half)
        self.theirs = pl.ds(pl.multiple_of(place.other_x * half, half), half)

    def full(self, r, which, columns):
        return self.s1[0].at[r - 1, :, :, :, columns] if which == 0 else self.s1[1].at[r - 1, :, :, columns]

    def x_copy(self, r, which):
        return remote(self.full(r, which, self.theirs), (self.xi, self.xo)[which].at[r - 1], self.xs, (r - 1, which), self.p.peer_x())

    def x_load(self, r, which):
        return pltpu.make_async_copy(self.full(r, which, self.mine), self.own[which].at[r - 1], self.lsem.at[which, r])

    def side(self, r, which, y):
        if which == 0:
            return self.xi.at[r - 1, :, y] if r else self.s2[0].at[:, y]
        return self.xo.at[r - 1, y] if r else self.s2[1].at[y]

    def y_copy(self, r, which):
        return remote(self.side(r, which, self.p.other_y), (self.yi, self.yo)[which].at[r], self.ys, (r, which), self.p.peer_y())

    def y_load(self, r, which):
        return pltpu.make_async_copy(self.side(r, which, self.p.y), self.own[2 + which], self.lsem.at[which, r])

    def z_in(self, r, d):
        to, t = self.p.ahead(d), self.p.ahead(r)
        return remote(self.yi.at[r, to], self.zi.at[t, d - 1], self.zi_s, (t, d - 1), self.p.at_z(to))

    def z_out(self, r):
        return remote(self.yo.at[r], self.zo.at[r - 1], self.zo_s, (r - 1,), self.p.at_z(self.p.ahead(r)))

    def last(self, t, r, columns):
        return remote(self.yi.at[r, self.p.z], self.outi_h.at[t, :, columns], self.fi, (t,), self.p.peer_x())

    def last_out(self, columns):
        return remote(self.yo.at[0], self.outo_h.at[:, columns], self.fo, (0,), self.p.peer_x())

    def keep(self, t, r):
        return pltpu.make_async_copy(self.yi.at[r, self.p.z], self.outi_h.at[t, :, self.mine], self.lsem.at[2, t])

    def keep_out(self):
        return pltpu.make_async_copy(self.yo.at[0], self.outo_h.at[:, self.mine], self.lsem.at[3, 0])

    def over_x(self, r):
        for which in range(2):
            self.x_copy(r, which).start()
            self.x_load(r, which).start()

    def over_y(self, r):
        for which in range(2):
            if r:
                self.x_copy(r, which).wait()
                self.x_load(r, which).wait()
                here, own = (self.xi, self.xo)[which], self.own[which]
                for k in range(here.shape[1]):
                    here[r - 1, k] = (here[r - 1, k].astype(F32) + own[r - 1, k].astype(F32)).astype(B16)
            else:
                self.y_load(r, which).start()
            self.y_copy(r, which).start()

    def over_z(self, r):
        if not r:
            self.y_load(r, 0).wait()
        self.y_copy(r, 0).wait_recv()
        for k in range(NZ):
            own = self.xi[r - 1, k, self.p.y] if r else self.own[2][k]
            self.yi[r, k] = (self.yi[r, k].astype(F32) + own.astype(F32)).astype(B16)
        for d in (1, 2, 3):
            self.z_in(r, d).start()
        if not r:
            self.y_load(r, 1).wait()
        self.y_copy(r, 1).wait_recv()
        own = self.xo[r - 1, self.p.y] if r else self.own[3][...]
        self.yo[r] = (self.yo[r].astype(F32) + own.astype(F32)).astype(B16)
        if r:
            self.z_out(r).start()

    def finish(self):
        for t in range(NZ):
            r = lax.rem(t + NZ - self.p.z, NZ)
            total = self.yi[r, self.p.z].astype(F32)
            for d in (1, 2, 3):
                slot = self.zi.at[t, d - 1]
                remote(slot, slot, self.zi_s, (t, d - 1), self.p.at_z(self.p.behind(d))).wait_recv()
                total = total + self.zi[t, d - 1].astype(F32)
            self.yi[r, self.p.z] = total.astype(B16)
            self.last(t, r, self.mine).start()
            self.keep(t, r).start()
        total = self.yo[0].astype(F32)
        for r in (1, 2, 3):
            self.z_out(r).wait_recv()
            total = total + self.zo[r - 1].astype(F32)
        self.yo[0] = total.astype(B16)
        self.last_out(self.mine).start()
        self.keep_out().start()

    def done(self):
        for r in range(NZ):
            for which in range(2):
                self.y_copy(r, which).wait_send()
            for d in (1, 2, 3):
                self.z_in(r, d).wait_send()
            if r:
                self.z_out(r).wait_send()
            t = self.p.ahead(r)
            self.last(t, r, self.mine).wait_send()
            self.last(t, r, self.theirs).wait_recv()
            self.keep(t, r).wait()
        self.last_out(self.mine).wait_send()
        self.last_out(self.theirs).wait_recv()
        self.keep_out().wait()


class SumAll:
    def __init__(self, place, v, land, sems):
        self.p, self.v, self.land, self.sems = place, v, land, sems

    def copy(self, k, peer):
        return remote(self.v.at[k], self.land.at[k], self.sems, (k,), peer)

    def begin(self):
        self.copy(0, self.p.peer_c()).start()

    def over_y(self):
        self.copy(0, self.p.peer_c()).wait_recv()
        self.v[1] = self.v[0] + self.land[0]
        self.copy(1, self.p.peer_y()).start()

    def z_copy(self, r, to):
        return remote(self.v.at[2], self.land.at[1 + r], self.sems, (1 + r,), self.p.at_z(to))

    def over_z(self):
        self.copy(1, self.p.peer_y()).wait_recv()
        self.v[2] = self.v[1] + self.land[1]
        for r in (1, 2, 3):
            self.z_copy(r, self.p.ahead(r)).start()

    def over_x(self):
        for r in (1, 2, 3):
            self.z_copy(r, self.p.ahead(r)).wait_recv()
        total = jnp.zeros_like(self.v[2])
        for z in range(NZ):
            r = lax.rem(self.p.z + NZ - z, NZ)
            part = self.v[2]
            for d in (1, 2, 3):
                part = jnp.where(r == d, self.land[1 + d], part)
            total = total + part
        self.v[3] = total
        remote(self.v.at[3], self.land.at[5], self.sems, (5,), self.p.peer_x()).start()

    def done(self):
        for k, peer in ((0, self.p.peer_c()), (1, self.p.peer_y())):
            self.copy(k, peer).wait_send()
        for r in (1, 2, 3):
            self.z_copy(r, self.p.ahead(r)).wait_send()
        remote(self.v.at[3], self.land.at[5], self.sems, (5,), self.p.peer_x()).wait()
        self.v[0] = self.v[3] + self.land[5]


BACKWARD_PLAN = {
    (PRE, 0, 0): ((TX, 1), (TY, 0),),
    (CROSS, 0, 1): ((PY, 3),),
    (CROSS, 0, 3): ((TX, 2),),
    (CROSS, 1, 0): ((TZ, 0), (TX, 3), (PY, 0),),
    (CROSS, 1, 2): ((PZ, 3),),
    (CROSS, 1, 3): ((TY, 1),),
    (CROSS, 1, 4): ((ME, 0),),
    (CROSS, 2, 1): ((PY, 1), (PZ, 0),),
    (LATE, 1, 0): ((TY, 2),),
    (LATE, 2, 0): ((TZ, 1),),
    (SELF, 0, 0): ((PZ, 1),),
    (SELF, 0, 2): ((PX, 3), (TY, 3), (TZ, 2),),
    (SELF, 0, 4): ((PY, 2),),
    (SELF, 1, 1): ((PX, 0), (TZ, 3),),
    (SELF, 1, 2): ((PY, 4),),
    (SELF, 1, 4): ((PZ, 2),),
    (SELF, 2, 0): ((PY, 5), (TF, 0),),
    (SELF, 2, 1): ((PZ, 4), (PX, 1),),
    (SELF, 2, 3): ((PY, 7),),
    (SELF, 2, 4): ((PX, 2), (PZ, 5),),
    (TAIL, 1, 0): ((PY, 6), (PX, 4), (SY, 0), (PZ, 7), (PZ, 6), (SZ, 0), (PX, 5), (PX, 7), (PX, 6), (SX, 0),),
}


def backward_kernel(
    tlen, mlen, flag, mix_h, tok_h, h1_h, qkv_h, a_h, lse_h, x1_h, mem_h, h2_h, cq_h, ckv_h, c_h, clse_h, g2_h, w_h, s1i_h, s1o_h, s2i_h, s2o_h,
    vecs_h, gbi_h, gains_h,
    mixed_h, gtok_h, gmem_h, tot_h, rx_h, outi_h, outo_h, vec_h,
    W, G, rc, ry, rz, ownxi, ownxo, ownyi, ownyo, rxi, rxo, ryi, ryo, rzi, rzo, sv, sland,
    h, att, qkv, ckv, lse, clse, x1, mem, g2, gb, db, dh, gm, gmb, vec, vin, gbi,
    qt, kt, ktc, at, dat, ps, dss, qm, dm, dqt, dk_acc, dv_acc, dkc_acc, dvc_acc, dq, dk, dv, dck, dcv,
    csem, ysem, zsem, xsem, lsem, txs, tys, tzi, tzo, tfi, tfo, tlsem, vsem, gsem, loc,
):
    p = Place()
    L, D = h.shape
    M = mem.shape[0]
    half = L // 2
    count = []

    def fetch(src, dst):
        cp = pltpu.make_async_copy(src, dst, loc.at[len(count)])
        cp.start()
        count.append(cp)
        return cp

    vec_cp = [fetch(gains_h, vec), fetch(vecs_h, vin), fetch(gbi_h, gbi)]
    g2_cp = fetch(g2_h, g2)
    w_cp = [None] * 4
    w_cp[3] = fetch(w_h.at[7], W.at[3])
    c_cp = fetch(c_h, att)
    cross_cp = [fetch(cq_h, qkv.at[0]), fetch(ckv_h, ckv), fetch(clse_h, clse), fetch(h2_h, h), fetch(mem_h, mem)]
    for g in range(3):
        w_cp[g] = fetch(w_h.at[4 + g], W.at[g])
    x1_cp = fetch(x1_h, x1)
    kv_cp = [fetch(qkv_h.at[1], qkv.at[1]), fetch(qkv_h.at[2], qkv.at[2]), fetch(lse_h, lse)]
    p.greet()
    rs_ = Reduce(p, G, rc, ry, rz, tot_h, rx_h, csem, ysem, zsem, xsem, lsem)
    tiles = ReduceTiles(p, s1i_h, s1o_h, s2i_h, s2o_h, (ownxi, ownxo, ownyi, ownyo), (rxi, rxo, ryi, ryo, rzi, rzo), (outi_h, outo_h),
                        (txs, tys, tzi, tzo, tfi, tfo, tlsem))
    small = SumAll(p, sv, sland, vsem)
    theirs = pl.ds(pl.multiple_of(p.other_x * half, half), half)
    ours = pl.ds(pl.multiple_of(p.x * half, half), half)
    mix_send = remote(mix_h.at[theirs], mixed_h.at[p.x], gsem, (2,), p.peer_x())
    mix_land = remote(mix_h.at[theirs], mixed_h.at[p.other_x], gsem, (2,), p.peer_x())
    steps = {
        PY: rs_.over_y, PZ: rs_.over_z, PX: rs_.over_x, TX: tiles.over_x, TY: tiles.over_y, TZ: tiles.over_z,
        TF: lambda _: tiles.finish(), ME: lambda _: mix_send.start(),
        SY: lambda _: small.over_y(), SZ: lambda _: small.over_z(), SX: lambda _: small.over_x(),
    }

    def point(name):
        run_plan(BACKWARD_PLAN, steps, name)

    point((PRE, 0, 0))
    f = flag[p.x].astype(F32)
    for cp in vec_cp:
        cp.wait()
    g2_cp.wait()
    w_cp[3].wait()
    for r in range(0, L, ROWS):
        rs = pl.ds(r, ROWS)
        gcr = (f * g2[rs]).astype(B16)
        gb[rs] = gcr
        db[rs] = dot_nt(gcr, flat(W[3])).astype(B16)
        dh[rs] = jnp.zeros((ROWS, D), F32)
    gm[...] = jnp.zeros_like(gm)
    point((PRE, 1, 0))

    def put(n, lo, hi, value):
        G[quarter(n), :, :, :, :, lo:hi] = value.astype(B16).reshape(G.shape[1:5] + (hi - lo,))

    def out_projection(n):
        for j in range(0, D, GROUP):
            put(n, j, j + GROUP, dot_tn(att[...], gb[:, j : j + GROUP]))

    c_cp.wait()
    out_projection(3)
    rs_.over_c(3)
    for cp in cross_cp:
        cp.wait()
    for g in range(3):
        w_cp[g].wait()

    def wpart(n, k):
        return flat(W[n, :, :, :, :, k * GROUP : (k + 1) * GROUP])

    def cross_group(g, _):
        def step(i):
            run_plan_at(BACKWARD_PLAN, steps, CROSS, g, 3, i)

        attend_back_group(qkv, ckv, ckv, (0, g), (0, g), (1, g), att, db, g, clse, mlen[p.x], False, 256,
                          qt, ktc, at, dat, ps, dss, qm, dm, dqt, dkc_acc, dvc_acc, step)
        dq[...] = dqt[...].astype(F32).T.astype(B16)
        dck[...] = dkc_acc[...].astype(B16)
        dcv[...] = dvc_acc[...].astype(B16)
        put(g, 0, GROUP, dot_tn(h[...], dq[...]))
        put(g, GROUP, 2 * GROUP, dot_tn(mem[...], dck[...]))
        put(g, 2 * GROUP, 3 * GROUP, dot_tn(mem[...], dcv[...]))
        rs_.over_c(g)
        for r in range(0, L, ROWS):
            rs = pl.ds(r, ROWS)
            dh[rs] += dot_nt(dq[rs], wpart(g, 0))
        gm[...] += dot_nt(dck[...], wpart(g, 1)) + dot_nt(dcv[...], wpart(g, 2))

        step(4)
        return 0

    lax.fori_loop(0, 3, cross_group, 0)
    self_cp = [fetch(w_h.at[3], W.at[3]), fetch(a_h, att), fetch(h1_h, h), fetch(qkv_h.at[0], qkv.at[0])]
    for g in range(3):
        self_cp.append(fetch(w_h.at[g], W.at[g]))
    gmb[...] = gm[...].astype(B16)
    mhalf = M // 2
    gm_send = remote(gmb.at[pl.ds(pl.multiple_of(p.other_x * mhalf, mhalf), mhalf)], gmem_h.at[p.x], gsem, (0,), p.peer_x())
    gm_land = remote(gmb.at[pl.ds(0, mhalf)], gmem_h.at[p.other_x], gsem, (0,), p.peer_x())
    gm_send.start()
    gm_own = fetch(gmb.at[pl.ds(pl.multiple_of(p.x * mhalf, mhalf), mhalf)], gmem_h.at[p.x])
    point((LATE, 0, 0))
    x1_cp.wait()
    sg = jnp.zeros((1, D), F32)
    sb = jnp.zeros((1, D), F32)
    for r in range(0, L, ROWS):
        rs = pl.ds(r, ROWS)
        dx, s, b = norm_back(dh[rs], x1[rs], vec[1:2])
        g1 = g2[rs] + dx
        g2[rs] = g1
        gb[rs] = g1.astype(B16)
        sg += s
        sb += b
    sv[0, 1:2] = sg
    sv[0, 4:5] = sb
    sv[0, 2:3] = vin[0:1]
    sv[0, 5:6] = vin[1:2]
    sv[0, 6:7] = vin[2:3]
    sv[0, 7:8] = jnp.zeros((1, D), F32)
    for t in range(NZ):
        sv[0, 8 + t : 9 + t] = gbi[t, 0:1]
    sv[0, 12:16] = jnp.zeros((4, D), F32)
    point((LATE, 1, 0))
    self_cp[0].wait()
    for r in range(0, L, ROWS):
        rs = pl.ds(r, ROWS)
        db[rs] = dot_nt(gb[rs], flat(W[3])).astype(B16)
        dh[rs] = jnp.zeros((ROWS, D), F32)
    point((LATE, 2, 0))
    self_cp[1].wait()
    out_projection(7)
    rs_.over_c(7)
    tok = gb
    tok_cp = fetch(tok_h, tok)
    for cp in self_cp[2:] + kv_cp:
        cp.wait()

    def self_group(g, _):
        def step(i):
            run_plan_at(BACKWARD_PLAN, steps, SELF, g, 3, i)

        attend_back_group(qkv, qkv, qkv, (0, g), (1, g), (2, g), att, db, g, lse, tlen[p.x], True, 256,
                          qt, kt, at, dat, ps, dss, qm, dm, dqt, dk_acc, dv_acc, step)
        dq[...] = dqt[...].astype(F32).T.astype(B16)
        dk[...] = dk_acc[...].astype(B16)
        dv[...] = dv_acc[...].astype(B16)
        for k, d in enumerate((dq, dk, dv)):
            put(4 + g, k * GROUP, (k + 1) * GROUP, dot_tn(h[...], d[...]))
        rs_.over_c(4 + g)
        for r in range(0, L, ROWS):
            rs = pl.ds(r, ROWS)
            dh[rs] += dot_nt(dq[rs], wpart(g, 0)) + dot_nt(dk[rs], wpart(g, 1)) + dot_nt(dv[rs], wpart(g, 2))
        step(4)
        return 0

    lax.fori_loop(0, 3, self_group, 0)
    tok_cp.wait()
    sg = jnp.zeros((1, D), F32)
    sb = jnp.zeros((1, D), F32)
    gt = db
    sent = False
    gt_send = remote(gt.at[theirs], gtok_h.at[p.x], gsem, (1,), p.peer_x())
    gt_land = remote(gt.at[theirs], gtok_h.at[p.other_x], gsem, (1,), p.peer_x())
    for start in (p.other_x * half, p.x * half):
        for r in range(0, half, ROWS):
            rs = pl.ds(pl.multiple_of(start + r, ROWS), ROWS)
            dx, s, b = norm_back(dh[rs], tok[rs].astype(F32), vec[0:1])
            gt[rs] = (g2[rs] + dx).astype(B16)
            sg += s
            sb += b
        if not sent:
            gt_send.start()
            point((TAIL, 0, 0))
        sent = True
    sv[0, 0:1] = sg
    sv[0, 3:4] = sb
    small.begin()
    gt_own = fetch(gt.at[ours], gtok_h.at[p.x])
    point((TAIL, 1, 0))
    for n in range(8):
        rs_.done(n)
    tiles.done()
    small.done()
    vec_out = fetch(sv.at[0], vec_h)
    for cp in (mix_send, gm_send, gt_send):
        cp.wait_send()
    for cp in (mix_land, gm_land, gt_land):
        cp.wait_recv()
    for cp in (gm_own, gt_own, vec_out):
        cp.wait()


def backward_call(tlen, mlen, flag, arrays):
    mix, tok, h1, qkv, a, lse, x1, mem, h2, cq, ckv, c, clse, g2, w, s1i, s1o, s2i, s2o, vecs, gbi, gains = arrays
    L, D = tok.shape
    M = mem.shape[0]
    G = D // GROUP
    S = w.shape[4]
    R = s1o.shape[2]
    H = D // 2
    outs = [((2, L // 2, D), B16), ((2, L // 2, D), B16), ((2, M // 2, D), B16), ((8, S, D), B16), ((8, S, D), B16), ((NZ, S, D), B16),
            ((R, D), B16), ((SMALL, D), F32)]
    scratch = [
        ((4, NZ, NY, NC, S, D), B16), ((4, NZ, NY, NC, S, D), B16), ((8, NZ, NY, S, D), B16), ((8, NZ, S, D), B16), ((8, 3, S, D), B16),
        ((3, NZ, NY, S, H), B16), ((3, NY, R, H), B16), ((NZ, S, H), B16), ((R, H), B16),
        ((3, NZ, NY, S, H), B16), ((3, NY, R, H), B16), ((NZ, NZ, S, H), B16), ((NZ, R, H), B16), ((NZ, 3, S, H), B16), ((3, R, H), B16),
        ((4, SMALL, D), F32), ((6, SMALL, D), F32),
        ((L, D), B16), ((L, D), B16), ((3, G, L, GROUP), B16), ((2, G, M, GROUP), B16), ((G, 8, L), F32), ((G, 8, L), F32), ((L, D), F32),
        ((M, D), B16), ((L, D), F32), ((L, D), B16), ((L, D), B16), ((L, D), F32), ((M, D), F32), ((M, D), B16), ((SMALL, D), F32), ((8, D), F32),
        ((NZ, 8, D), F32),
        ((GROUP, L), B16), ((GROUP, L), B16), ((GROUP, M), B16), ((GROUP, L), B16), ((GROUP, L), B16),
        ((L, PER * 256), B16), ((L, PER * 256), B16), ((PER * 256, GROUP), B16), ((PER * 256, GROUP), B16),
        ((GROUP, L), B16), ((L, GROUP), F32), ((L, GROUP), F32), ((M, GROUP), F32), ((M, GROUP), F32),
        ((L, GROUP), B16), ((L, GROUP), B16), ((L, GROUP), B16), ((M, GROUP), B16), ((M, GROUP), B16),
    ]
    sems = [(2, 8), (2, 8), (2, 8, 3), (2, 8), (8,), (2, 3, 2), (2, 4, 2), (2, 4, 3), (2, 3), (2, 4), (2, 1), (4, 4), (2, 6), (2, 3), (40,)]
    return pl.pallas_call(
        backward_kernel,
        out_shape=[jax.ShapeDtypeStruct(s, d) for s, d in outs],
        in_specs=[SMEM_SPEC] * 3 + [ANY_SPEC] * len(arrays),
        out_specs=[ANY_SPEC] * len(outs),
        scratch_shapes=[VMEM(s, d) for s, d in scratch] + [DMA(s) for s in sems],
        compiler_params=pltpu.CompilerParams(vmem_limit_bytes=63 * 1024 * 1024, collective_id=1, has_side_effects=True),
        name="backward",
    )(tlen, mlen, flag, *arrays)


def finish_kernel(
    mix_i, mixed_i, gtok_i, gmem_i, tot_i, rx_i, ins_i, out_i, vec_i,
    mixed, gtok, gmem, gsw, gsp, gcw, gcp, gwi, gwo, gbi, gbo, gg, gs,
    mix_v, tok_v, mem_v, tot_v, rx_v, ins_v, out_v, vec_v, tok_f, mem_f, sw_f, sp_f, cw_f, cp_f, wi_f, wo_f, bi_f, bo_f, g_f, s_f, sems,
):
    count = []

    def copy(src, dst):
        cp = pltpu.make_async_copy(src, dst, sems.at[len(count)])
        cp.start()
        count.append(cp)
        return cp

    S = gsp.shape[0]
    halves = [copy(gtok_i.at[k], tok_v.at[k]) for k in range(2)]
    rest = [copy(a, b) for a, b in ((tot_i, tot_v), (rx_i, rx_v), (ins_i, ins_v), (out_i, out_v), (gmem_i, mem_v), (vec_i, vec_v))]
    x = lax.axis_index("mem")
    half = mixed.shape[1]
    both = [copy(mix_i.at[pl.ds(pl.multiple_of(x * half, half), half)], mix_v.at[0]), copy(mixed_i.at[1 - x], mix_v.at[1])]
    outs = []
    for k in range(2):
        halves[k].wait()
        tok_f[k] = tok_v[k].astype(F32)
        outs.append(copy(tok_f.at[k], gtok.at[k]))
    for k, cp in enumerate(both):
        cp.wait()
        outs.append(copy(mix_v.at[k], mixed.at[1 - x if k else x]))
    for cp in rest:
        cp.wait()
    for first, dst in ((0, cw_f), (4, sw_f)):
        for g in range(3):
            v = tot_v[first + g].astype(F32) + rx_v[first + g].astype(F32)
            for k in range(3):
                dst[k, :, g * GROUP : (g + 1) * GROUP] = v[:, k * GROUP : (k + 1) * GROUP]
    cp_f[...] = tot_v[3].astype(F32) + rx_v[3].astype(F32)
    sp_f[...] = tot_v[7].astype(F32) + rx_v[7].astype(F32)
    D = sp_f.shape[1]
    for t in range(NZ):
        wi_f[:, t * D : (t + 1) * D] = ins_v[t].astype(F32)
    wo_f[...] = out_v[...].astype(F32)
    mem_f[...] = mem_v[...].astype(F32)
    i = lax.axis_index("fsdp")
    R = wo_f.shape[0]
    mine = pltpu.roll(vec_v[0:8], lax.rem(D - i * S, D), 1)
    g_f[...] = mine[0:3, :S]
    s_f[...] = mine[3:6, :S]
    bo_f[...] = mine[6:7, :S]
    row = lax.broadcasted_iota(jnp.int32, (8, D), 0)
    tile = jnp.sum(jnp.where(row == i // (NY * NC), vec_v[8:16], 0.0), 0, keepdims=True)
    tile = pltpu.roll(jnp.broadcast_to(tile, (8, D)), lax.rem(D - lax.rem(i, NY * NC) * R, D), 1)
    bi_f[...] = tile[0:1, :R]
    for a, b in ((mem_f, gmem), (sw_f, gsw), (sp_f, gsp), (cw_f, gcw), (cp_f, gcp), (wi_f, gwi), (wo_f, gwo), (bi_f, gbi), (bo_f, gbo), (g_f, gg), (s_f, gs)):
        outs.append(copy(a, b))
    for cp in outs:
        cp.wait()


def finish_call(mix, mixed, gtok, gmem, tot, rx, ins, out, vec):
    S, D = tot.shape[1:]
    R = out.shape[0]
    outs = [(mixed.shape, B16), (gtok.shape, F32), (gmem.shape, F32), ((3, S, D), F32), ((S, D), F32), ((3, S, D), F32), ((S, D), F32),
            ((S, NZ * D), F32), ((R, D), F32), ((1, R), F32), ((1, S), F32), ((3, S), F32), ((3, S), F32)]
    ins_ = (mix, mixed, gtok, gmem, tot, rx, ins, out, vec)
    scratch = [VMEM(v.shape, v.dtype) for v in ins_[1:]] + [VMEM(s, d) for s, d in outs[1:]]
    return pl.pallas_call(
        finish_kernel,
        out_shape=[jax.ShapeDtypeStruct(s, d) for s, d in outs],
        in_specs=[HBM_SPEC] * len(ins_),
        out_specs=[HBM_SPEC] * len(outs),
        scratch_shapes=scratch + [DMA((32,))],
        compiler_params=pltpu.CompilerParams(vmem_limit_bytes=62 * 1024 * 1024),
        name="finish",
    )(*ins_)


def paired_body(tokens, memory, cotangent, text_len, mem_len, image_flag, self_qkv, self_out, cross_qkv, cross_out,
                w_in, w_out, b_in, b_out, norm_gain, norm_bias):
    fw = forward_call(text_len, mem_len, image_flag, tokens, memory, cotangent, self_qkv, self_out, cross_qkv, cross_out,
                      w_in, w_out, pack_small(norm_gain, norm_bias, b_out, b_in))
    outs = finish_call(fw[0], *backward_call(text_len, mem_len, image_flag, fw))
    return (*outs[:9], outs[9][0], outs[10][0], *outs[11:])


def layer_norm(values, gain, shift):
    centre = values - jnp.mean(values, -1, keepdims=True)
    spread = jnp.mean(centre * centre, -1, keepdims=True)
    return centre * lax.rsqrt(spread + EPSILON) * gain + shift


def gelu_exact(values):
    return jax.nn.gelu(values, approximate=False)


def split_heads(values):
    return values.reshape(values.shape[0], values.shape[1], -1, HEAD).transpose(2, 0, 1, 3)


def merge_heads(values):
    return values.transpose(1, 2, 0, 3).reshape(values.shape[1], values.shape[2], -1)


def head_scores(query_matrix, key_matrix, allowed):
    logit_scores = jnp.einsum(
        "cti,cvi->ctv", query_matrix, key_matrix, preferred_element_type=jnp.float32
    ) * HEAD ** (-0.5)
    return jnp.where(allowed, logit_scores, -1000000000.0)


def attend(query_matrix, key_matrix, values, allowed):

    def one_head(parts):
        head_query_rows, head_key_rows, head_value_rows = parts
        logit_scores = head_scores(head_query_rows, head_key_rows, allowed)
        row_max = jnp.max(logit_scores, -1, keepdims=True)
        expo = jnp.exp(logit_scores - row_max)
        row_sum = jnp.sum(expo, -1, keepdims=True)
        reduced_probabilities = (expo / row_sum).astype(jnp.bfloat16)
        attention_output = jnp.einsum(
            "zqf,zfm->zqm",
            reduced_probabilities,
            head_value_rows,
            preferred_element_type=jnp.float32,
        )
        return (attention_output, row_max, row_sum)

    attention_output, row_max, row_sum = lax.map(
        one_head, (split_heads(query_matrix), split_heads(key_matrix), split_heads(values))
    )
    return (merge_heads(attention_output).astype(jnp.bfloat16), row_max, row_sum)


def attend_back(query_matrix, key_matrix, values, allowed, row_max, row_sum, grad_out):

    def one_head(parts):
        (
            head_query_rows,
            head_key_rows,
            head_value_rows,
            head_output_gradient,
            head_max,
            head_sum,
        ) = parts
        logit_scores = head_scores(head_query_rows, head_key_rows, allowed)
        probs = jnp.exp(logit_scores - head_max) / head_sum
        reduced_probabilities = probs.astype(jnp.bfloat16)
        probs_gradient = jnp.einsum(
            "cti,cvi->ctv",
            head_output_gradient,
            head_value_rows,
            preferred_element_type=jnp.float32,
        )
        delta_sum = jnp.sum(probs * probs_gradient, -1, keepdims=True)
        scores_gradient = (probs * (probs_gradient - delta_sum)).astype(jnp.bfloat16)
        d_query = jnp.einsum(
            "zqf,zfm->zqm", scores_gradient, head_key_rows, preferred_element_type=jnp.float32
        ) * HEAD ** (-0.5)
        d_keys = jnp.einsum(
            "pum,pug->pmg", scores_gradient, head_query_rows, preferred_element_type=jnp.float32
        ) * HEAD ** (-0.5)
        values_gradient = jnp.einsum(
            "pum,pug->pmg",
            reduced_probabilities,
            head_output_gradient,
            preferred_element_type=jnp.float32,
        )
        return (d_query, d_keys, values_gradient)

    d_query, d_keys, values_gradient = lax.map(
        one_head,
        (
            split_heads(query_matrix),
            split_heads(key_matrix),
            split_heads(values),
            split_heads(grad_out),
            row_max,
            row_sum,
        ),
    )
    return (merge_heads(d_query), merge_heads(d_keys), merge_heads(values_gradient))


def general_body(
    tokens,
    memory,
    cotangent,
    text_len,
    mem_len,
    image_flag,
    self_qkv,
    self_out,
    cross_qkv,
    cross_out,
    w_in,
    w_out,
    b_in,
    b_out,
    norm_gain,
    norm_bias,
):
    f32 = jnp.float32
    b16 = jnp.bfloat16
    seq_count, own_rows, width = tokens.shape
    offset = lax.axis_index("mem") * own_rows
    gathered = (
        lax.all_gather(self_qkv, "fsdp", axis=1, tiled=True),
        lax.all_gather(self_out, "fsdp", axis=0, tiled=True),
        lax.all_gather(cross_qkv, "fsdp", axis=1, tiled=True),
        lax.all_gather(cross_out, "fsdp", axis=0, tiled=True),
        lax.all_gather(w_in, "fsdp", axis=0, tiled=True),
        lax.all_gather(w_out, "fsdp", axis=0, tiled=True),
        lax.all_gather(b_in, "fsdp", axis=0, tiled=True),
        lax.all_gather(b_out, "fsdp", axis=0, tiled=True),
        lax.all_gather(norm_gain, "fsdp", axis=1, tiled=True),
        lax.all_gather(norm_bias, "fsdp", axis=1, tiled=True),
    )
    (
        self_w,
        self_proj,
        cross_w,
        cross_proj,
        inner_w,
        outer_w,
        inner_bias,
        outer_bias,
        gains,
        shifts,
    ) = gathered
    gains = gains.astype(f32)
    shifts = shifts.astype(f32)
    x0 = tokens.astype(f32)
    h1_full, norm0_back = jax.vjp(layer_norm, x0, gains[0], shifts[0])
    h1 = h1_full.astype(b16)
    qkv = jnp.einsum("srd,kde->ksre", h1, self_w, preferred_element_type=f32).astype(b16)
    keys_all, values_all = (
        lax.all_gather(qkv[1], "mem", axis=1, tiled=True),
        lax.all_gather(qkv[2], "mem", axis=1, tiled=True),
    )
    key_pos = jnp.arange(keys_all.shape[1], dtype=jnp.int32)
    query_pos = offset + jnp.arange(own_rows, dtype=jnp.int32)
    self_mask = (key_pos[None, None, :] <= query_pos[None, :, None]) & (
        key_pos[None, None, :] < text_len[:, None, None]
    )
    attended, self_max, self_sum = attend(qkv[0], keys_all, values_all, self_mask)
    x1 = x0 + jnp.einsum("srd,de->sre", attended, self_proj, preferred_element_type=f32)
    h2_full, norm1_back = jax.vjp(layer_norm, x1, gains[1], shifts[1])
    h2 = h2_full.astype(b16)
    cross_q = jnp.einsum("srd,de->sre", h2, cross_w[0], preferred_element_type=f32).astype(b16)
    memory_all = lax.all_gather(memory, "mem", axis=1, tiled=True)
    cross_kv = jnp.einsum(
        "snd,kde->ksne", memory_all, cross_w[1:], preferred_element_type=f32
    ).astype(b16)
    cross_keys, cross_values = (cross_kv[0], cross_kv[1])
    mem_pos = jnp.arange(cross_keys.shape[1], dtype=jnp.int32)
    cross_mask = mem_pos[None, None, :] < mem_len[:, None, None]
    crossed, cross_max, cross_sum = attend(cross_q, cross_keys, cross_values, cross_mask)
    flag = image_flag.astype(f32)[:, None, None]
    x2 = x1 + jnp.einsum("srd,de->sre", crossed, cross_proj, preferred_element_type=f32) * flag
    h3_full, norm2_back = jax.vjp(layer_norm, x2, gains[2], shifts[2])
    h3 = h3_full.astype(b16)
    pre = jnp.einsum("srd,df->srf", h3, inner_w, preferred_element_type=f32) + inner_bias.astype(
        f32
    )
    act_full, gelu_back = jax.vjp(gelu_exact, pre)
    act_low = act_full.astype(b16)
    attention_output = (
        x2
        + jnp.einsum("srf,fd->srd", act_low, outer_w, preferred_element_type=f32)
        + outer_bias.astype(f32)
    )
    mixed = attention_output.astype(b16)
    grad_top = cotangent.astype(f32)
    grad_low = grad_top.astype(b16)
    grad_outer_bias = jnp.sum(grad_low.astype(f32), (0, 1))
    grad_outer = jnp.einsum("srf,srd->fd", act_low, grad_low, preferred_element_type=f32)
    d_act = jnp.einsum("srd,fd->srf", grad_low, outer_w, preferred_element_type=f32)
    d_pre = gelu_back(d_act)[0].astype(b16)
    grad_inner_bias = jnp.sum(d_pre.astype(f32), (0, 1))
    grad_inner = jnp.einsum("srd,srf->df", h3, d_pre, preferred_element_type=f32)
    d_h3 = jnp.einsum("srf,df->srd", d_pre, inner_w, preferred_element_type=f32)
    d_x2, gain_two, shift_two = norm2_back(d_h3)
    grad_two = grad_top + d_x2
    grad_cross = (grad_two * flag).astype(b16)
    grad_cross_proj = jnp.einsum("srd,sre->de", crossed, grad_cross, preferred_element_type=f32)
    d_crossed = jnp.einsum(
        "sre,de->srd", grad_cross, cross_proj, preferred_element_type=f32
    ).astype(b16)
    d_cross_q, d_cross_k, d_cross_v = attend_back(
        cross_q, cross_keys, cross_values, cross_mask, cross_max, cross_sum, d_crossed
    )
    own_cross_k, own_cross_v = (
        lax.psum_scatter(
            d_cross_k.astype(jnp.bfloat16), "mem", scatter_dimension=1, tiled=True
        ).astype(jnp.float32),
        lax.psum_scatter(
            d_cross_v.astype(jnp.bfloat16), "mem", scatter_dimension=1, tiled=True
        ).astype(jnp.float32),
    )
    d_cross_kv = jnp.stack([own_cross_k, own_cross_v]).astype(b16)
    grad_cross_kv = jnp.einsum("snd,ksne->kde", memory, d_cross_kv, preferred_element_type=f32)
    grad_memory = jnp.einsum("ksne,kde->snd", d_cross_kv, cross_w[1:], preferred_element_type=f32)
    d_cross_low = d_cross_q.astype(b16)
    grad_cross_q = jnp.einsum("srd,sre->de", h2, d_cross_low, preferred_element_type=f32)
    d_h2 = jnp.einsum("sre,de->srd", d_cross_low, cross_w[0], preferred_element_type=f32)
    d_x1, gain_one, shift_one = norm1_back(d_h2)
    grad_one = grad_two + d_x1
    grad_cross_w = jnp.concatenate([grad_cross_q[None], grad_cross_kv], 0)
    grad_one_low = grad_one.astype(b16)
    grad_self_proj = jnp.einsum("srd,sre->de", attended, grad_one_low, preferred_element_type=f32)
    d_attended = jnp.einsum(
        "sre,de->srd", grad_one_low, self_proj, preferred_element_type=f32
    ).astype(b16)
    d_query, d_keys, values_gradient = attend_back(
        qkv[0], keys_all, values_all, self_mask, self_max, self_sum, d_attended
    )
    own_keys, own_values = (
        lax.psum_scatter(
            d_keys.astype(jnp.bfloat16), "mem", scatter_dimension=1, tiled=True
        ).astype(jnp.float32),
        lax.psum_scatter(
            values_gradient.astype(jnp.bfloat16), "mem", scatter_dimension=1, tiled=True
        ).astype(jnp.float32),
    )
    d_qkv = jnp.stack([d_query, own_keys, own_values]).astype(b16)
    grad_self_w = jnp.einsum("srd,ksre->kde", h1, d_qkv, preferred_element_type=f32)
    d_h1 = jnp.einsum("ksre,kde->srd", d_qkv, self_w, preferred_element_type=f32)
    d_x0, gain_zero, shift_zero = norm0_back(d_h1)
    grad_tokens = grad_one + d_x0
    gain_grads = jnp.stack([gain_zero, gain_one, gain_two])
    shift_grads = jnp.stack([shift_zero, shift_one, shift_two])
    full_grads = (
        grad_self_w,
        grad_self_proj,
        grad_cross_w,
        grad_cross_proj,
        grad_inner,
        grad_outer,
        grad_inner_bias,
        grad_outer_bias,
        gain_grads,
        shift_grads,
    )
    shards = (
        lax.psum_scatter(
            full_grads[0].astype(jnp.bfloat16), "fsdp", scatter_dimension=1, tiled=True
        ).astype(jnp.float32),
        lax.psum_scatter(
            full_grads[1].astype(jnp.bfloat16), "fsdp", scatter_dimension=0, tiled=True
        ).astype(jnp.float32),
        lax.psum_scatter(
            full_grads[2].astype(jnp.bfloat16), "fsdp", scatter_dimension=1, tiled=True
        ).astype(jnp.float32),
        lax.psum_scatter(
            full_grads[3].astype(jnp.bfloat16), "fsdp", scatter_dimension=0, tiled=True
        ).astype(jnp.float32),
        lax.psum_scatter(
            full_grads[4].astype(jnp.bfloat16), "fsdp", scatter_dimension=0, tiled=True
        ).astype(jnp.float32),
        lax.psum_scatter(
            full_grads[5].astype(jnp.bfloat16), "fsdp", scatter_dimension=0, tiled=True
        ).astype(jnp.float32),
        lax.psum_scatter(
            full_grads[6].astype(jnp.bfloat16), "fsdp", scatter_dimension=0, tiled=True
        ).astype(jnp.float32),
        lax.psum_scatter(
            full_grads[7].astype(jnp.bfloat16), "fsdp", scatter_dimension=0, tiled=True
        ).astype(jnp.float32),
        lax.psum_scatter(
            full_grads[8].astype(jnp.bfloat16), "fsdp", scatter_dimension=1, tiled=True
        ).astype(jnp.float32),
        lax.psum_scatter(
            full_grads[9].astype(jnp.bfloat16), "fsdp", scatter_dimension=1, tiled=True
        ).astype(jnp.float32),
    )
    totals = (
        lax.psum(shards[0].astype(jnp.bfloat16), "mem").astype(jnp.float32),
        lax.psum(shards[1].astype(jnp.bfloat16), "mem").astype(jnp.float32),
        lax.psum(shards[2].astype(jnp.bfloat16), "mem").astype(jnp.float32),
        lax.psum(shards[3].astype(jnp.bfloat16), "mem").astype(jnp.float32),
        lax.psum(shards[4].astype(jnp.bfloat16), "mem").astype(jnp.float32),
        lax.psum(shards[5].astype(jnp.bfloat16), "mem").astype(jnp.float32),
        lax.psum(shards[6].astype(jnp.bfloat16), "mem").astype(jnp.float32),
        lax.psum(shards[7].astype(jnp.bfloat16), "mem").astype(jnp.float32),
        lax.psum(shards[8].astype(jnp.bfloat16), "mem").astype(jnp.float32),
        lax.psum(shards[9].astype(jnp.bfloat16), "mem").astype(jnp.float32),
    )
    return (
        mixed,
        grad_tokens,
        grad_memory,
        totals[0],
        totals[1],
        totals[2],
        totals[3],
        totals[4],
        totals[5],
        totals[6],
        totals[7],
        totals[8],
        totals[9],
    )


def body(*args):
    if lax.axis_size("mem") == 2 and lax.axis_size("fsdp") == NZ * NY * NC:
        return paired_body(*args)
    return general_body(*args)


def solution(mesh):
    placed = (
        P("fsdp", "mem", None),
        P("fsdp", "mem", None),
        P("fsdp", "mem", None),
        P("fsdp"),
        P("fsdp"),
        P("fsdp"),
        P(None, "fsdp", None),
        P("fsdp", None),
        P(None, "fsdp", None),
        P("fsdp", None),
        P("fsdp", None),
        P("fsdp", None),
        P("fsdp"),
        P("fsdp"),
        P(None, "fsdp"),
        P(None, "fsdp"),
    )
    return jax.shard_map(
        body,
        mesh=mesh,
        in_specs=placed,
        out_specs=(
            P("fsdp", "mem", None),
            P("fsdp", "mem", None),
            P("fsdp", "mem", None),
            P(None, "fsdp", None),
            P("fsdp", None),
            P(None, "fsdp", None),
            P("fsdp", None),
            P("fsdp", None),
            P("fsdp", None),
            P("fsdp"),
            P("fsdp"),
            P(None, "fsdp"),
            P(None, "fsdp"),
        ),
        check_vma=False,
    )
```

```python
import jax
import jax.numpy as jnp
from jax import lax
from jax.experimental import pallas as pl
from jax.experimental.pallas import tpu as pltpu
from jax.sharding import PartitionSpec as P

F32 = jnp.float32
B16 = jnp.bfloat16
HEAD = 64
GROUP = 256
PER = GROUP // HEAD
EPSILON = 1e-05
NEG = -1000000000.0


def dot(a, b):
    return jnp.dot(a, b, preferred_element_type=F32)


def dot_nt(a, b):
    return lax.dot_general(a, b, (((1,), (1,)), ((), ())), preferred_element_type=F32)


def dot_tn(a, b):
    return lax.dot_general(a, b, (((0,), (0,)), ((), ())), preferred_element_type=F32)


def norm_parts(v):
    centre = v - jnp.mean(v, -1, keepdims=True)
    rs = lax.rsqrt(jnp.mean(centre * centre, -1, keepdims=True) + EPSILON)
    return centre * rs, rs


def norm_back(e, v, gain):
    n, rs = norm_parts(v)
    t = e * gain
    dx = rs * (t - jnp.mean(t, -1, keepdims=True) - n * jnp.mean(t * n, -1, keepdims=True))
    return dx, jnp.sum(e * n, 0, keepdims=True), jnp.sum(e, 0, keepdims=True)


def cols(g):
    return pl.ds(pl.multiple_of(g * GROUP, GROUP), GROUP)


def head_rows(h, rows, width):
    return lax.broadcasted_iota(jnp.int32, (rows, width), 0) // HEAD == h


def head_cols(h, rows, width):
    return lax.broadcasted_iota(jnp.int32, (rows, width), 1) // HEAD == h


def allowed_block(first_key, nk, first_query, nq, limit, causal):
    key = first_key + lax.broadcasted_iota(jnp.int32, (nk, nq), 0)
    ok = key < limit
    if causal:
        query = first_query + lax.broadcasted_iota(jnp.int32, (nk, nq), 1)
        ok = ok & (key <= query)
    return ok


def attend_back_group(
    q_ref, k_ref, v_ref, qi_, ki_, vi_, a_ref, da_ref, g, lse_ref, limit, causal, tq,
    qt, kt, at, dat, ps, dss, qm_ref, dm_ref, dqt, dk_acc, dv_acc, step=None,
):
    L = qt.shape[1]
    K = kt.shape[1]
    scale = HEAD**-0.5
    qt[...] = (q_ref[qi_].astype(F32) * scale).T.astype(B16)
    kt[...] = (k_ref[ki_].astype(F32) * scale).T.astype(B16)
    at[...] = a_ref[:, cols(g)].astype(F32).T.astype(B16)
    dat[...] = da_ref[:, cols(g)].astype(F32).T.astype(B16)

    def keys(i):
        return (i + 1) * tq if causal else K

    def front(i, h):
        nk, span = keys(i), slice(i * tq, (i + 1) * tq)
        here = head_rows(h, GROUP, tq)
        block = qt[:, span]
        s = dot(k_ref[ki_ + (pl.ds(0, nk),)], jnp.where(here, block, jnp.zeros_like(block)))
        block = dat[:, span]
        dp = dot(v_ref[vi_ + (pl.ds(0, nk),)], jnp.where(here, block, jnp.zeros_like(block)))
        return s, dp

    def middle(i, h, s, dp):
        nk, span = keys(i), slice(i * tq, (i + 1) * tq)
        hs = slice(h * HEAD, (h + 1) * HEAD)
        delta = jnp.sum(at[hs, span].astype(F32) * dat[hs, span].astype(F32), 0, keepdims=True)
        s = mask_scores(s, nk, i * tq, tq, limit, causal)
        p = jnp.exp(s - lse_ref[g, h : h + 1, span])
        ds = (p * (dp - delta)).astype(B16)
        ps[0:nk, h * tq : (h + 1) * tq] = p.astype(B16)
        dss[0:nk, h * tq : (h + 1) * tq] = ds
        mine = head_cols(h, tq, GROUP)
        qn = q_ref[qi_ + (pl.ds(i * tq, tq),)] * jnp.asarray(scale, B16)
        dn = da_ref[pl.ds(i * tq, tq), cols(g)]
        qm_ref[h * tq : (h + 1) * tq] = jnp.where(mine, qn, jnp.zeros_like(qn))
        dm_ref[h * tq : (h + 1) * tq] = jnp.where(mine, dn, jnp.zeros_like(dn))
        return ds

    def back(i, h, ds):
        nk, span = keys(i), slice(i * tq, (i + 1) * tq)
        hs = slice(h * HEAD, (h + 1) * HEAD)
        dqt[hs, span] = dot(kt[hs, 0:nk], ds).astype(B16)

    def close(i):
        nk = keys(i)
        dvi = dot(ps[0:nk], dm_ref[...])
        dki = dot(dss[0:nk], qm_ref[...])
        if i == tiles[0]:
            dv_acc[0:nk] = dvi
            dk_acc[0:nk] = dki
        else:
            dv_acc[0:nk] += dvi
            dk_acc[0:nk] += dki

    tiles = list(range(L // tq))[::-1]
    order = [(i, h) for i in tiles for h in range(PER)]
    ahead = front(*order[0])
    late = None
    for n, (i, h) in enumerate(order):
        now = ahead
        if h < PER - 1:
            ahead = front(*order[n + 1])
        ds = middle(i, h, *now)
        if late is not None:
            back(*late)
        late = (i, h, ds)
        if h == PER - 1:
            if n + 1 < len(order):
                ahead = front(*order[n + 1])
            back(*late)
            late = None
            close(i)
            if step is not None:
                step(tiles.index(i))


def mask_scores(s, nk, q0, tq, limit, causal):
    if causal and nk > tq:
        top = jnp.where(allowed_block(0, nk - tq, q0, tq, limit, False), s[: nk - tq], NEG)
        bottom = jnp.where(allowed_block(nk - tq, tq, q0, tq, limit, True), s[nk - tq :], NEG)
        return jnp.concatenate([top, bottom], 0)
    return jnp.where(allowed_block(0, nk, q0, tq, limit, causal), s, NEG)


def attend_group(q_ref, k_ref, v_ref, qi_, ki_, vi_, out_ref, g, lse_ref, limit, causal, tq, qt, vt, ot, step=None):
    L = qt.shape[1]
    K = vt.shape[1]
    qt[...] = (q_ref[qi_].astype(F32) * HEAD**-0.5).T.astype(B16)
    vt[...] = v_ref[vi_].astype(F32).T.astype(B16)

    def keys(i):
        return (i + 1) * tq if causal else K

    def front(i, h):
        block = qt[:, i * tq : (i + 1) * tq]
        qm = jnp.where(head_rows(h, GROUP, tq), block, jnp.zeros_like(block))
        return dot(k_ref[ki_ + (pl.ds(0, keys(i)),)], qm)

    def middle(i, h, s):
        s = mask_scores(s, keys(i), i * tq, tq, limit, causal)
        m = jnp.max(s, 0, keepdims=True)
        e = jnp.exp(s - m)
        total = jnp.sum(e, 0, keepdims=True)
        lse_ref[g, h : h + 1, i * tq : (i + 1) * tq] = m + jnp.log(total)
        return (e * (1.0 / total)).astype(B16)

    def back(i, h, p):
        hs = slice(h * HEAD, (h + 1) * HEAD)
        ot[hs, i * tq : (i + 1) * tq] = dot(vt[hs, 0 : keys(i)], p).astype(B16)

    order = [(i, h) for i in range(L // tq) for h in range(PER)]
    ahead = front(*order[0])
    late = None
    for n, (i, h) in enumerate(order):
        now = ahead
        if n + 1 < len(order):
            ahead = front(*order[n + 1])
        p = middle(i, h, now)
        if late is not None:
            back(*late)
        late = (i, h, p)
        if step is not None and h == PER - 1:
            step(i)
    back(*late)
    out_ref[:, cols(g)] = ot[...].astype(F32).T.astype(B16)


ERFCX = (
    0.21161358920977177, 0.2106475215974073, 0.20533035663075158, 0.12143152976148842,
    0.27391662866419597, -0.22972237163936396, 0.432698311257476, -0.287490481514182,
    0.06157492612604076,
)


def gelu_parts(u):
    t = 1.0 / (1.0 + (0.375 * 0.7071067811865476) * jnp.abs(u))
    poly = jnp.full_like(t, 0.5 * ERFCX[8])
    for c in ERFCX[7::-1]:
        poly = poly * t + 0.5 * c
    bell = jnp.exp(u * (-0.5 * u))
    half = (poly * t) * bell
    cdf = jnp.where(u >= 0, 1.0 - half, half)
    return u * cdf, cdf + u * (bell * 0.3989422804014327)


ROWS = 256

VMEM = pltpu.VMEM
SMEM_SPEC = pl.BlockSpec(memory_space=pltpu.SMEM)


MESH = pl.DeviceIdType.MESH
NZ, NY, NC = 4, 2, 2
ANY_SPEC = pl.BlockSpec(memory_space=pl.ANY)
HBM_SPEC = pl.BlockSpec(memory_space=pltpu.HBM)
DMA = pltpu.SemaphoreType.DMA
SMALL = 16


class Place:
    def __init__(self):
        i = lax.axis_index("fsdp")
        self.x = lax.axis_index("mem")
        self.i = i
        self.z, self.y, self.c = i // (NY * NC), (i // NC) % NY, i % NC
        self.other_x, self.other_y, self.other_c = 1 - self.x, 1 - self.y, 1 - self.c

    def at_z(self, z):
        return (self.x, (z * NY + self.y) * NC + self.c)

    def ahead(self, r):
        return lax.rem(self.z + r, NZ)

    def behind(self, r):
        return lax.rem(self.z + NZ - r, NZ)

    def peer_y(self):
        return (self.x, (self.z * NY + self.other_y) * NC + self.c)

    def peer_c(self):
        return (self.x, (self.z * NY + self.y) * NC + self.other_c)

    def peer_x(self):
        return (self.other_x, self.i)

    def greet(self):
        barrier = pltpu.get_barrier_semaphore()
        peers = [self.at_z(self.ahead(r)) for r in (1, 2, 3)] + [self.peer_y(), self.peer_c(), self.peer_x()]
        for peer in peers:
            pl.semaphore_signal(barrier, inc=1, device_id=peer, device_id_type=MESH)
        pl.semaphore_wait(barrier, len(peers))


def remote(src, dst, sems, index, peer):
    return pltpu.make_async_remote_copy(
        src_ref=src, dst_ref=dst, send_sem=sems.at[(0,) + index], recv_sem=sems.at[(1,) + index],
        device_id=peer, device_id_type=MESH)


class Gather:
    def __init__(self, place, ref, zsem, ysem, csem):
        self.p, self.ref, self.zsem, self.ysem, self.csem = place, ref, zsem, ysem, csem

    def block(self, lead, z):
        return self.ref.at[lead + (z, self.p.y, self.p.c)]

    def z_send(self, lead, r):
        mine = self.block(lead, self.p.z)
        return remote(mine, mine, self.zsem, lead + (r - 1,), self.p.at_z(self.p.ahead(r)))

    def z_land(self, lead, r):
        slot = self.block(lead, self.p.behind(r))
        return remote(slot, slot, self.zsem, lead + (r - 1,), self.p.at_z(self.p.behind(r)))

    def column(self, lead, y, c):
        return self.ref.at[lead + (slice(None), y, c)]

    def y_copy(self, lead, y):
        part = self.column(lead, y, self.p.c)
        return remote(part, part, self.ysem, lead, self.p.peer_y())

    def c_copy(self, lead, k, y, c):
        part = self.column(lead, y, c)
        return remote(part, part, self.csem, lead + (k,), self.p.peer_c())

    def begin(self, lead):
        for r in (1, 2, 3):
            self.z_send(lead, r).start()

    def spread(self, lead):
        for r in (1, 2, 3):
            self.z_land(lead, r).wait_recv()
        self.y_copy(lead, self.p.y).start()
        self.c_copy(lead, 0, self.p.y, self.p.c).start()

    def finish(self, lead):
        self.y_copy(lead, self.p.other_y).wait_recv()
        self.c_copy(lead, 1, self.p.other_y, self.p.c).start()

    def ready(self, lead):
        self.c_copy(lead, 0, self.p.y, self.p.other_c).wait_recv()
        self.c_copy(lead, 1, self.p.other_y, self.p.other_c).wait_recv()

    def sent(self, lead):
        for r in (1, 2, 3):
            self.z_send(lead, r).wait_send()
        self.y_copy(lead, self.p.y).wait_send()
        self.c_copy(lead, 0, self.p.y, self.p.c).wait_send()
        self.c_copy(lead, 1, self.p.other_y, self.p.c).wait_send()


class GatherIn(Gather):
    def tile(self, z, r):
        return lax.rem(z + r, NZ)

    def begin(self, r):
        for d in (1, 2, 3):
            self.send(r, d).start()

    def send(self, r, d):
        to = self.p.ahead(d)
        mine = self.block((self.tile(to, r),), self.p.z)
        return remote(mine, mine, self.zsem, (r, d - 1), self.p.at_z(to))

    def lead(self, r):
        return (self.tile(self.p.z, r),)

    def y_in(self, r, y):
        part = self.column(self.lead(r), y, self.p.c)
        return remote(part, part, self.ysem, (r,), self.p.peer_y())

    def c_in(self, r, k, y, c):
        part = self.column(self.lead(r), y, c)
        return remote(part, part, self.csem, (r, k), self.p.peer_c())

    def spread(self, r):
        for d in (1, 2, 3):
            slot = self.block(self.lead(r), self.p.behind(d))
            remote(slot, slot, self.zsem, (r, d - 1), self.p.at_z(self.p.behind(d))).wait_recv()
        self.y_in(r, self.p.y).start()
        self.c_in(r, 0, self.p.y, self.p.c).start()

    def finish(self, r):
        self.y_in(r, self.p.other_y).wait_recv()
        self.c_in(r, 1, self.p.other_y, self.p.c).start()

    def ready(self, r):
        self.c_in(r, 0, self.p.y, self.p.other_c).wait_recv()
        self.c_in(r, 1, self.p.other_y, self.p.other_c).wait_recv()

    def sent(self, r):
        for d in (1, 2, 3):
            self.send(r, d).wait_send()
        self.y_in(r, self.p.y).wait_send()
        self.c_in(r, 0, self.p.y, self.p.c).wait_send()
        self.c_in(r, 1, self.p.other_y, self.p.c).wait_send()


class GatherHalves(Gather):
    def __init__(self, place, ref, first, zsem, ysem, xsem, csem):
        super().__init__(place, ref, zsem, ysem, csem)
        self.first, self.xsem = first, xsem
        half = ref.shape[-1] // 2
        self.mine = pl.ds(pl.multiple_of(place.x * half, half), half)
        self.theirs = pl.ds(pl.multiple_of(place.other_x * half, half), half)

    def z_send(self, n, r):
        part = self.ref.at[n, self.p.z, self.p.y, self.p.c, :, self.mine]
        return remote(part, part, self.zsem, (n - self.first, r - 1), self.p.at_z(self.p.ahead(r)))

    def z_land(self, n, r):
        part = self.ref.at[n, self.p.behind(r), self.p.y, self.p.c, :, self.mine]
        return remote(part, part, self.zsem, (n - self.first, r - 1), self.p.at_z(self.p.behind(r)))

    def part(self, n, y, c, columns):
        return self.ref.at[n, :, y, c, :, columns]

    def y_half(self, n, y):
        part = self.part(n, y, self.p.c, self.mine)
        return remote(part, part, self.ysem, (n - self.first,), self.p.peer_y())

    def x_half(self, n, k, y, columns):
        part = self.part(n, y, self.p.c, columns)
        return remote(part, part, self.xsem, (n - self.first, k), self.p.peer_x())

    def c_half(self, n, k, y, c, columns):
        part = self.part(n, y, c, columns)
        return remote(part, part, self.csem, (n - self.first, k), self.p.peer_c())

    def quarters(self):
        return ((0, self.p.y, self.mine), (1, self.p.other_y, self.mine), (2, self.p.y, self.theirs), (3, self.p.other_y, self.theirs))

    def spread(self, n):
        for r in (1, 2, 3):
            self.z_land(n, r).wait_recv()
        self.x_half(n, 0, self.p.y, self.mine).start()
        self.y_half(n, self.p.y).start()
        self.c_half(n, 0, self.p.y, self.p.c, self.mine).start()

    def finish(self, n):
        self.y_half(n, self.p.other_y).wait_recv()
        self.x_half(n, 1, self.p.other_y, self.mine).start()
        self.c_half(n, 1, self.p.other_y, self.p.c, self.mine).start()

    def relay(self, n):
        for k, y in ((0, self.p.y), (1, self.p.other_y)):
            self.x_half(n, k, y, self.theirs).wait_recv()
            self.c_half(n, 2 + k, y, self.p.c, self.theirs).start()

    def ready(self, n):
        for k, y, columns in self.quarters():
            self.c_half(n, k, y, self.p.other_c, columns).wait_recv()

    def sent(self, n):
        for r in (1, 2, 3):
            self.z_send(n, r).wait_send()
        self.y_half(n, self.p.y).wait_send()
        for k, y in ((0, self.p.y), (1, self.p.other_y)):
            self.x_half(n, k, y, self.mine).wait_send()
        for k, y, columns in self.quarters():
            self.c_half(n, k, y, self.p.c, columns).wait_send()


class GatherOut:
    def __init__(self, place, ref, zsem, ysem, xsem, csem):
        self.p, self.ref, self.zsem, self.ysem, self.xsem, self.csem = place, ref, zsem, ysem, xsem, csem
        half = ref.shape[-1] // 2
        self.mine = pl.ds(pl.multiple_of(place.x * half, half), half)
        self.theirs = pl.ds(pl.multiple_of(place.other_x * half, half), half)

    def block(self, z, y, c, columns):
        return self.ref.at[z, y, c, :, columns]

    def z_copy(self, r, src_z, to):
        part = self.block(src_z, self.p.y, self.p.c, self.mine)
        return remote(part, part, self.zsem, (r,), self.p.at_z(to))

    def y_copy(self, r, y):
        part = self.block(self.p.ahead(r), y, self.p.c, self.mine)
        return remote(part, part, self.ysem, (r,), self.p.peer_y())

    def x_copy(self, r, k, y, columns):
        part = self.block(self.p.ahead(r), y, self.p.c, columns)
        return remote(part, part, self.xsem, (r, k), self.p.peer_x())

    def c_copy(self, r, k, y, c, columns):
        part = self.block(self.p.ahead(r), y, c, columns)
        return remote(part, part, self.csem, (r, k), self.p.peer_c())

    def begin(self, r):
        self.z_copy(r, self.p.z, self.p.behind(r)).start()

    def spread(self, r, landed=True):
        if landed:
            self.z_copy(r, self.p.ahead(r), self.p.ahead(r)).wait_recv()
        if r:
            self.x_copy(r, 0, self.p.y, self.mine).start()
        self.y_copy(r, self.p.y).start()
        self.c_copy(r, 0, self.p.y, self.p.c, self.mine).start()

    def finish(self, r):
        self.y_copy(r, self.p.other_y).wait_recv()
        self.x_copy(r, 1, self.p.other_y, self.mine).start()
        self.c_copy(r, 1, self.p.other_y, self.p.c, self.mine).start()

    def relay(self, r):
        for k, y in ((0, self.p.y), (1, self.p.other_y)):
            if r or k:
                self.x_copy(r, k, y, self.theirs).wait_recv()
            self.c_copy(r, 2 + k, y, self.p.c, self.theirs).start()

    def ready(self, r):
        for k, y, columns in ((0, self.p.y, self.mine), (1, self.p.other_y, self.mine), (2, self.p.y, self.theirs), (3, self.p.other_y, self.theirs)):
            self.c_copy(r, k, y, self.p.other_c, columns).wait_recv()

    def sent(self, r, began=True):
        if began:
            self.z_copy(r, self.p.z, self.p.behind(r)).wait_send()
        self.y_copy(r, self.p.y).wait_send()
        for k, y in ((0, self.p.y), (1, self.p.other_y)):
            if r or k:
                self.x_copy(r, k, y, self.mine).wait_send()
        for k, y, columns in ((0, self.p.y, self.mine), (1, self.p.other_y, self.mine), (2, self.p.y, self.theirs), (3, self.p.other_y, self.theirs)):
            self.c_copy(r, k, y, self.p.c, columns).wait_send()


def unpack_small(v):
    n = NZ * NY * NC
    D = 48 * n
    total = jnp.zeros((8, D), F32)
    tiles = jnp.zeros((8, D), F32)
    lane = lax.broadcasted_iota(jnp.int32, (8, 256), 1)
    row = lax.broadcasted_iota(jnp.int32, (8, D), 0)
    for i in range(n):
        block = v[i // 4, (i // 2) % 2, i % 2]
        pad = jnp.zeros((8, D - 256), F32)
        total = total + roll_lanes(jnp.concatenate([jnp.where(lane < 48, block, 0.0), pad], 1), 48 * i)
        wide = roll_lanes(jnp.concatenate([jnp.where(lane < 192, block, 0.0), pad], 1), 192 * (i % 4))
        tiles = tiles + jnp.where(row == i // 4, jnp.broadcast_to(wide[7:8], wide.shape), 0.0)
    return jnp.concatenate([total, tiles], 0)


def roll_lanes(v, by):
    return pltpu.roll(v, by, 1) if by else v


def flat(v):
    return v.reshape(-1, v.shape[-1])


PRE, SELF, NEXT, CROSS, FEED, LATE, TAIL = range(7)
BP, SP, FP, LP, RP, BI, SI, FI, BO, SO, FO, LO, TE, RA, XB, XA, PY, PZ, PX, TX, TY, TZ, TF, ME, SY, SZ, SX = range(27)
SPLIT = (6, 7)
FORWARD_PLAN = {
    (PRE, 0, 0): ((BP, 1), (BP, 6), (TE, 0), (SO, 0), (SP, 1), (BP, 0), (BP, 2),),
    (PRE, 1, 0): ((SP, 6), (BP, 3), (SP, 0), (TE, 2), (BP, 4),),
    (PRE, 2, 0): ((BP, 5),),
    (PRE, 3, 0): ((SP, 2), (FP, 0),),
    (SELF, 0, 0): ((FP, 1),),
    (SELF, 0, 1): ((SP, 3), (BP, 7),),
    (SELF, 0, 2): ((BO, 1),),
    (SELF, 1, 0): ((FP, 2),),
    (SELF, 1, 1): ((TE, 1), (SP, 4), (BI, 0),),
    (SELF, 1, 2): ((FP, 6),),
    (SELF, 2, 0): ((SP, 5), (FP, 3),),
    (SELF, 2, 1): ((FO, 0),),
    (SELF, 2, 2): ((FP, 4),),
    (SELF, 2, 3): ((BI, 1), (SP, 7),),
    (NEXT, 1, 0): ((SO, 1), (BO, 2),),
    (CROSS, 0, 1): ((LP, 6),),
    (CROSS, 0, 2): ((FP, 5),),
    (CROSS, 0, 3): ((SI, 0), (FP, 7),),
    (CROSS, 1, 0): ((BO, 3),),
    (CROSS, 1, 1): ((FO, 1),),
    (CROSS, 2, 0): ((LO, 0), (LP, 7),),
    (CROSS, 2, 1): ((BI, 2), (BI, 3),),
    (CROSS, 2, 3): ((SI, 1), (FI, 0),),
    (NEXT, 2, 0): ((SO, 2),),
    (FEED, 0, 0): ((SO, 3), (LO, 1),),
    (FEED, 0, 1): ((FI, 1),),
    (FEED, 0, 2): ((FO, 2),),
    (FEED, 0, 3): ((SI, 2),),
    (FEED, 0, 4): ((FO, 3),),
    (FEED, 1, 0): ((RA, 0), (SI, 3),),
    (FEED, 1, 2): ((LO, 2), (FI, 2),),
    (FEED, 1, 3): ((LO, 3),),
    (FEED, 2, 1): ((FI, 3), (XB, 0),),
    (FEED, 2, 2): ((RA, 1),),
    (FEED, 3, 2): ((RA, 2),),
    (TAIL, 0, 0): ((XA, 0), (RA, 3),),
}


def run_plan(plan, steps, point):
    for kind, n in plan.get(point, ()):
        steps[kind](n)


def run_plan_at(plan, steps, prefix, index, count, i):
    for at in range(count):
        point = (prefix, at, i)
        if point in plan:

            @pl.when(index == at)
            def _(point=point):
                run_plan(plan, steps, point)


def forward_kernel(
    tlen, mlen, flag, tokens_h, memory_h, cot_h, sw_h, sp_h, cw_h, cp_h, wi_h, wo_h, small_h,
    mixed_h, tok_h, h1_h, qkv_h, a_h, lse_h, x1_h, mem_h, h2_h, cq_h, ckv_h, c_h, clse_h, g2_h, w_h, s1i_h, s1o_h, s2i_h, s2o_h, vecs_h, gbi_h, gains_h,
    W, WI, WO, V, tok, mem, cot, vec, h1, qkv, a, lse, x1, h2, ckv, clse, x2, h3t, acc, dh3, gwi, gwo, rci, rco, rxi, rxo,
    qt, vt, vtc, ot, gbi, vout,
    wz, wy, wc, iz, iy, ic, oz, oy, ox, oc, hz, hy, hx, hc, vz, vy, vc, xs, rs_sem, rx_sem, loc, spill_sem,
):
    p = Place()
    L, D = tok.shape
    half = L // 2
    M = mem.shape[0]
    FT = WI.shape[-1]
    local = []

    def fetch(src, dst):
        cp = pltpu.make_async_copy(src, dst, loc.at[len(local)])
        cp.start()
        local.append(cp)
        return cp

    me = (p.z, p.y, p.c)
    pieces = [[] for _ in range(8)]
    for n in SPLIT:
        if n < 7:
            g = n - 4
            for k in range(3):
                pieces[n].append(fetch(cw_h.at[k, :, pl.ds(g * GROUP, GROUP)], W.at[(n,) + me + (slice(None), pl.ds(k * GROUP, GROUP))]))
    pieces[7].append(fetch(cp_h, W.at[(7,) + me]))
    small_cp = fetch(small_h, V.at[me])
    for g in range(3):
        for k in range(3):
            pieces[g].append(fetch(sw_h.at[k, :, pl.ds(g * GROUP, GROUP)], W.at[(g,) + me + (slice(None), pl.ds(k * GROUP, GROUP))]))
    tok_cp = fetch(tokens_h.at[p.x], tok.at[pl.ds(pl.multiple_of(p.x * half, half), half)])
    pieces[3].append(fetch(sp_h, W.at[(3,) + me]))
    for g in range(3):
        for k in range(3):
            if 4 + g not in SPLIT:
                pieces[4 + g].append(fetch(cw_h.at[k, :, pl.ds(g * GROUP, GROUP)], W.at[(4 + g,) + me + (slice(None), pl.ds(k * GROUP, GROUP))]))
    mem_cp = fetch(memory_h.at[p.x], mem.at[pl.ds(pl.multiple_of(p.x * (M // 2), M // 2), M // 2)])
    in_cp = [fetch(wi_h.at[:, pl.ds(t * FT, FT)], WI.at[(t,) + me]) for t in range(NZ)]
    out_cp = fetch(wo_h, WO.at[me])
    cot_cp = fetch(cot_h.at[p.x], cot.at[pl.ds(pl.multiple_of(p.x * half, half), half)])

    for n in SPLIT:
        for cp in pieces[n]:
            cp.wait()
    p.greet()
    gw = Gather(p, W, wz, wy, wc)
    gh = GatherHalves(p, W, SPLIT[0], hz, hy, hx, hc)
    gi = GatherIn(p, WI, iz, iy, ic)
    go = GatherOut(p, WO, oz, oy, ox, oc)
    gv = Gather(p, V, vz, vy, vc)

    def x_part(src_h, dst, rows, k):
        send = remote(src_h.at[p.other_x], dst.at[pl.ds(pl.multiple_of(p.x * rows, rows), rows)], xs, (k,), p.peer_x())
        land = dst.at[pl.ds(pl.multiple_of(p.other_x * rows, rows), rows)]
        return send, remote(src_h.at[p.other_x], land, xs, (k,), p.peer_x())

    tok_send, tok_land = x_part(tokens_h, tok, half, 0)
    mem_send, mem_land = x_part(memory_h, mem, M // 2, 1)
    cot_send, cot_land = x_part(cot_h, cot, half, 2)
    small_cp.wait()
    gv.begin(())

    def piece(method, halves):
        def step(n):
            if n in SPLIT:
                getattr(gh, halves)(n)
            else:
                getattr(gw, method)((n,))

        return step

    steps = {
        BP: piece("begin", "begin"), SP: piece("spread", "spread"), FP: piece("finish", "finish"), LP: gh.relay,
        RP: piece("ready", "ready"), BI: gi.begin, SI: gi.spread, FI: gi.finish,
        BO: go.begin, SO: lambda r: go.spread(r, r > 0), FO: go.finish, LO: go.relay,
        TE: lambda k: (tok_send, mem_send, cot_send)[k].start(),
    }
    for n, cps in enumerate(pieces):
        for cp in cps:
            if n not in SPLIT:
                cp.wait()
    for cp in in_cp + [out_cp, mem_cp, cot_cp]:
        cp.wait()

    def point(name):
        run_plan(FORWARD_PLAN, steps, name)

    point((PRE, 0, 0))
    gv.spread(())
    gv.finish(())
    gv.ready(())
    vec[...] = unpack_small(V)
    gains, shifts = vec, vec
    GAIN, SHIFT, BOUT, BIN = 0, 3, 6, 8

    def norm_rows(src, dst, k, start, count):
        for r in range(0, count, ROWS):
            rs = pl.ds(pl.multiple_of(start + r, ROWS), ROWS)
            n, _ = norm_parts(src[rs].astype(F32))
            dst[rs] = (n * gains[GAIN + k : GAIN + k + 1] + shifts[SHIFT + k : SHIFT + k + 1]).astype(B16)

    point((PRE, 1, 0))
    tok_cp.wait()
    norm_rows(tok, h1, 0, p.x * half, half)
    point((PRE, 2, 0))
    tok_land.wait_recv()
    norm_rows(tok, h1, 0, p.other_x * half, half)
    point((PRE, 3, 0))

    spills = []

    def spill(src, dst):
        cp = pltpu.make_async_copy(src, dst, spill_sem.at[len(spills)])
        cp.start()
        spills.append(cp)
        return cp

    tok_spill = spill(tok, tok_h)
    h1_spill = spill(h1, h1_h)

    def self_group(g, _):
        gw.ready((g,))
        for r in range(0, L, ROWS):
            rs = pl.ds(r, ROWS)
            out = dot(h1[rs], flat(W[g])).astype(B16)
            for k in range(3):
                qkv[k, g, rs] = out[:, k * GROUP : (k + 1) * GROUP]

        def step(i):
            run_plan_at(FORWARD_PLAN, steps, SELF, g, 3, i)

        attend_group(qkv, qkv, qkv, (0, g), (1, g), (2, g), a, g, lse, tlen[p.x], True, 256, qt, vt, ot, step)
        return 0

    lax.fori_loop(0, 3, self_group, 0)
    qkv_spill = spill(qkv, qkv_h)
    a_spill = spill(a, a_h)
    spill(lse, lse_h)
    steps[RP](3)
    for r in range(0, L, ROWS):
        rs = pl.ds(r, ROWS)
        x1[rs] = tok[rs].astype(F32) + dot(a[rs], flat(W[3]))
        norm_rows(x1, h2, 1, r, ROWS)
    point((NEXT, 1, 0))
    mem_land.wait_recv()
    spill(mem, mem_h)
    spill(x1, x1_h)
    h2_spill = spill(h2, h2_h)
    tok_spill.wait()
    qkv_spill.wait()
    c = tok
    cq = qkv.at[0]

    def cross_group(g, _):
        for k in range(3):

            @pl.when(g == k)
            def _(k=k):
                steps[RP](4 + k)

        for r in range(0, L, ROWS):
            rs = pl.ds(r, ROWS)
            cq[g, rs] = dot(h2[rs], flat(W[4 + g, :, :, :, :, 0:GROUP])).astype(B16)
        kv = dot(mem[...], flat(W[4 + g, :, :, :, :, GROUP : 3 * GROUP])).astype(B16)
        ckv[0, g] = kv[:, :GROUP]
        ckv[1, g] = kv[:, GROUP:]

        def step(i):
            run_plan_at(FORWARD_PLAN, steps, CROSS, g, 3, i)

        attend_group(cq, ckv, ckv, (g,), (0, g), (1, g), c, g, clse, mlen[p.x], False, 256, qt, vtc, ot, step)
        return 0

    lax.fori_loop(0, 3, cross_group, 0)
    spill(cq, cq_h)
    spill(ckv, ckv_h)
    spill(c, c_h)
    spill(clse, clse_h)
    steps[RP](7)
    f = flag[p.x].astype(F32)
    h1_spill.wait()
    a_spill.wait()
    h2_spill.wait()
    h3, act, dpre = h1, h2, a
    for r in range(0, L, ROWS):
        rs = pl.ds(r, ROWS)
        x2[rs] = x1[rs] + f * dot(c[rs], flat(W[7]))
        n, _ = norm_parts(x2[rs])
        h = n * gains[GAIN + 2 : GAIN + 3] + shifts[SHIFT + 2 : SHIFT + 3]
        h3[rs] = h.astype(B16)
        h3t[:, r : r + ROWS] = h.T.astype(B16)
        acc[rs] = x2[rs] + vec[BOUT : BOUT + 1]
        dh3[rs] = jnp.zeros((ROWS, D), F32)
    point((NEXT, 2, 0))
    spill(W, w_h)
    cot_land.wait_recv()
    gb_out = jnp.zeros((1, D), F32)
    for r in range(0, L, ROWS):
        gb_out += jnp.sum(cot[pl.ds(r, ROWS)].astype(F32), 0, keepdims=True)
    vout[2:3] = gb_out

    def reduce_copy(r, which):
        if which == 0:
            return remote(gwi.at[:, :, p.other_c], rci.at[r], rs_sem, (r, 0), p.peer_c())
        return remote(gwo.at[:, p.other_c], rco.at[r], rs_sem, (r, 1), p.peer_c())

    def reduce_add(r):
        reduce_copy(r, 0).wait()
        for k in range(NZ):
            rci[r, k] = (rci[r, k].astype(F32) + gwi[k, :, p.c].astype(F32)).astype(B16)
        reduce_copy(r, 1).wait()
        for k in range(NY):
            rco[r, k] = (rco[r, k].astype(F32) + gwo[k, p.c].astype(F32)).astype(B16)

    def x_copy(r, which):
        if which == 0:
            return remote(rci.at[r, :, :, :, go.theirs], rxi, rx_sem, (0,), p.peer_x())
        return remote(rco.at[r, :, :, go.theirs], rxo, rx_sem, (1,), p.peer_x())

    def x_begin(r):
        x_copy(r, 0).start()
        x_copy(r, 1).start()

    def x_add(r):
        x_copy(r, 0).wait()
        for k in range(NZ):
            rxi[k] = (rxi[k].astype(F32) + rci[r, k, :, :, go.mine].astype(F32)).astype(B16)
        x_copy(r, 1).wait()
        for k in range(NY):
            rxo[k] = (rxo[k].astype(F32) + rco[r, k, :, go.mine].astype(F32)).astype(B16)

    steps.update({RA: reduce_add, XB: x_begin, XA: x_add})

    def out_rows(t, j):
        return flat(WO[t])[j * GROUP : (j + 1) * GROUP]

    def ffn_round(r, _):
        t = p.ahead(r)
        gi.ready(r)
        go.ready(r)
        b_in = vec[pl.ds(BIN + t, 1)]
        sums = [jnp.zeros((1, GROUP), F32) for _ in range(0, FT, GROUP)]

        def front(q, j):
            rs, js = pl.ds(q, ROWS), slice(j * GROUP, (j + 1) * GROUP)
            w = flat(WI[t, :, :, :, :, js])
            return dot(h3[rs], w) + b_in[:, js], dot_nt(cot[rs], out_rows(t, j))

        def middle(q, j, pre, d_act):
            rs, js = pl.ds(q, ROWS), slice(j * GROUP, (j + 1) * GROUP)
            up, slope = gelu_parts(pre)
            act[rs, js] = up.astype(B16)
            d = (d_act * slope).astype(B16)
            dpre[rs, js] = d
            sums[j] = sums[j] + jnp.sum(d.astype(F32), 0, keepdims=True)

        def back(q):
            rs = pl.ds(q, ROWS)
            acc[rs] += dot(act[rs], flat(WO[t]))
            dh3[rs] += dot_nt(dpre[rs], flat(WI[t]))

        order = [(q, j) for q in range(0, L, ROWS) for j in range(FT // GROUP)]
        ahead = front(*order[0])
        for n, (q, j) in enumerate(order):
            now = ahead
            if n + 1 < len(order):
                ahead = front(*order[n + 1])
            middle(q, j, *now)
            if j == FT // GROUP - 1:
                back(q)
            if n in (4, 8):
                run_plan_at(FORWARD_PLAN, steps, FEED, r, NZ, n // 4 - 1)

        for j in range(FT // GROUP):
            gbi[t, :, j * GROUP : (j + 1) * GROUP] = jnp.broadcast_to(sums[j], (8, GROUP))

        run_plan_at(FORWARD_PLAN, steps, FEED, r, NZ, 2)
        for j in range(0, D, GROUP):
            part = dot_tn(act[...], cot[:, j : j + GROUP]).astype(B16)
            gwo[:, :, :, j : j + GROUP] = part.reshape(gwo.shape[:3] + (GROUP,))
        reduce_copy(r, 1).start()
        run_plan_at(FORWARD_PLAN, steps, FEED, r, NZ, 3)
        for j in range(0, FT, GROUP):
            part = dot(h3t[...], dpre[:, j : j + GROUP]).astype(B16)
            gwi[:, :, :, :, j : j + GROUP] = part.reshape(gwi.shape[:4] + (GROUP,))
        reduce_copy(r, 0).start()

        run_plan_at(FORWARD_PLAN, steps, FEED, r, NZ, 4)
        return 0

    lax.fori_loop(0, NZ, ffn_round, 0)
    mixed = act
    sg = jnp.zeros((1, D), F32)
    sb = jnp.zeros((1, D), F32)
    for r in range(0, L, ROWS):
        mixed[pl.ds(r, ROWS)] = acc[pl.ds(r, ROWS)].astype(B16)
    spill(mixed, mixed_h)
    spill(rci.at[pl.ds(1, 2)], s1i_h.at[pl.ds(0, 2)])
    spill(rco.at[pl.ds(1, 2)], s1o_h.at[pl.ds(0, 2)])
    for r in range(0, L, ROWS):
        rs = pl.ds(r, ROWS)
        dx, s, b = norm_back(dh3[rs], x2[rs], gains[GAIN + 2 : GAIN + 3])
        acc[rs] = cot[rs].astype(F32) + dx
        sg += s
        sb += b
    vout[0:1] = sg
    vout[1:2] = sb
    spill(acc, g2_h)
    spill(vout, vecs_h)
    spill(gbi, gbi_h)
    spill(vec, gains_h)
    point((TAIL, 0, 0))
    spill(rxi, s2i_h)
    spill(rxo, s2o_h)
    spill(rci.at[pl.ds(3, 1)], s1i_h.at[pl.ds(2, 1)])
    spill(rco.at[pl.ds(3, 1)], s1o_h.at[pl.ds(2, 1)])

    gv.sent(())
    for n in range(8):
        piece("sent", "sent")(n)
    for r in range(NZ):
        gi.sent(r)
        go.sent(r, r > 0)
    for cp in (tok_send, mem_send, cot_send):
        cp.wait_send()
    freed = (tok_spill, qkv_spill, h1_spill, a_spill, h2_spill)
    for cp in spills:
        if not any(cp is q for q in freed):
            cp.wait()


def forward_call(tlen, mlen, flag, tokens, memory, cot, sw, sp, cw, cp, wi, wo, small):
    _, half, D = tokens.shape
    L = 2 * half
    M = 2 * memory.shape[1]
    G = D // GROUP
    S = D // (NZ * NY * NC)
    FT = wi.shape[1] // NZ
    R = wo.shape[0]
    H = len(SPLIT)
    outs = [
        ((L, D), B16), ((L, D), B16), ((L, D), B16), ((3, G, L, GROUP), B16), ((L, D), B16), ((G, 8, L), F32),
        ((L, D), F32), ((M, D), B16), ((L, D), B16), ((G, L, GROUP), B16), ((2, G, M, GROUP), B16), ((L, D), B16),
        ((G, 8, L), F32), ((L, D), F32), ((8, NZ, NY, NC, S, D), B16), ((3, NZ, NY, S, FT), B16), ((3, NY, R, D), B16),
        ((NZ, NY, S, FT // 2), B16), ((NY, R, D // 2), B16), ((8, D), F32), ((NZ, 8, FT), F32), ((SMALL, D), F32),
    ]
    scratch = [
        ((8, NZ, NY, NC, S, D), B16), ((NZ, NZ, NY, NC, S, FT), B16), ((NZ, NY, NC, R, D), B16), ((NZ, NY, NC, 8, 256), F32),
        ((L, D), B16), ((M, D), B16), ((L, D), B16), ((SMALL, D), F32), ((L, D), B16), ((3, G, L, GROUP), B16), ((L, D), B16),
        ((G, 8, L), F32), ((L, D), F32), ((L, D), B16), ((2, G, M, GROUP), B16), ((G, 8, L), F32),
        ((L, D), F32), ((D, L), B16), ((L, D), F32), ((L, D), F32),
        ((NZ, NY, NC, S, FT), B16), ((NY, NC, R, D), B16), ((NZ, NZ, NY, S, FT), B16), ((NZ, NY, R, D), B16),
        ((NZ, NY, S, FT // 2), B16), ((NY, R, D // 2), B16),
        ((GROUP, L), B16), ((GROUP, L), B16), ((GROUP, M), B16), ((GROUP, L), B16), ((NZ, 8, FT), F32), ((8, D), F32),
    ]
    sems = [(2, 8, 3), (2, 8), (2, 8, 2), (2, 4, 3), (2, 4), (2, 4, 2), (2, 4), (2, 4), (2, 4, 2), (2, 4, 4), (2, H, 3), (2, H), (2, H, 2), (2, H, 4), (2, 3), (2,), (2, 2), (2, 4), (2, 4, 2), (2, 2), (40,), (24,)]
    return pl.pallas_call(
        forward_kernel,
        out_shape=[jax.ShapeDtypeStruct(s, d) for s, d in outs],
        in_specs=[SMEM_SPEC] * 3 + [ANY_SPEC] * 10,
        out_specs=[ANY_SPEC] * len(outs),
        scratch_shapes=[VMEM(s, d) for s, d in scratch] + [DMA(s) for s in sems],
        compiler_params=pltpu.CompilerParams(vmem_limit_bytes=63 * 1024 * 1024, collective_id=0, has_side_effects=True),
        name="forward",
    )(tlen, mlen, flag, tokens, memory, cot, sw, sp, cw, cp, wi, wo, small)


def pack_small(norm_gain, norm_bias, b_out, b_in):
    s = norm_gain.shape[1]
    rows = jnp.concatenate([norm_gain, norm_bias, b_out[None]], 0).astype(F32)
    rows = jnp.pad(rows, ((0, 0), (0, 256 - s)))
    return jnp.concatenate([rows, jnp.pad(b_in.astype(F32), (0, 256 - b_in.shape[0]))[None]], 0)


def quarter(n):
    return n % 4 if isinstance(n, int) else lax.rem(n, 4)


class Reduce:
    def __init__(self, place, G, rc, ry, rz, tot_h, rx_h, csem, ysem, zsem, xsem, lsem):
        self.p, self.G, self.rc, self.ry, self.rz, self.tot_h, self.rx_h = place, G, rc, ry, rz, tot_h, rx_h
        self.csem, self.ysem, self.zsem, self.xsem, self.lsem = csem, ysem, zsem, xsem, lsem

    def c_copy(self, n):
        return remote(self.G.at[quarter(n), :, :, self.p.other_c], self.rc.at[n], self.csem, (n,), self.p.peer_c())

    def y_copy(self, n):
        return remote(self.rc.at[n, :, self.p.other_y], self.ry.at[n], self.ysem, (n,), self.p.peer_y())

    def z_copy(self, n, r):
        to = self.p.ahead(r)
        return remote(self.ry.at[n, to], self.rz.at[n, r - 1], self.zsem, (n, r - 1), self.p.at_z(to))

    def x_copy(self, n):
        return remote(self.ry.at[n, self.p.z], self.rx_h.at[n], self.xsem, (n,), self.p.peer_x())

    def own_copy(self, n):
        return pltpu.make_async_copy(self.ry.at[n, self.p.z], self.tot_h.at[n], self.lsem.at[n])

    def over_c(self, n):
        self.c_copy(n).start()

    def over_y(self, n):
        self.c_copy(n).wait()
        for k in range(NZ):
            self.rc[n, k] = (self.rc[n, k].astype(F32) + self.G[quarter(n), k, :, self.p.c].astype(F32)).astype(B16)
        self.y_copy(n).start()

    def over_z(self, n):
        self.y_copy(n).wait_recv()
        for k in range(NZ):
            self.ry[n, k] = (self.ry[n, k].astype(F32) + self.rc[n, k, self.p.y].astype(F32)).astype(B16)
        for r in (1, 2, 3):
            self.z_copy(n, r).start()

    def over_x(self, n):
        for r in (1, 2, 3):
            self.z_copy(n, r).wait_recv()
        total = self.ry[n, self.p.z].astype(F32)
        for r in range(3):
            total = total + self.rz[n, r].astype(F32)
        self.ry[n, self.p.z] = total.astype(B16)
        self.x_copy(n).start()
        self.own_copy(n).start()

    def done(self, n):
        self.y_copy(n).wait_send()
        for r in (1, 2, 3):
            self.z_copy(n, r).wait_send()
        self.x_copy(n).wait()
        self.own_copy(n).wait()


class ReduceTiles:
    def __init__(self, place, s1i, s1o, s2i, s2o, own, land, outs, sems):
        self.p = place
        self.s1, self.s2 = (s1i, s1o), (s2i, s2o)
        self.own = own
        self.xi, self.xo, self.yi, self.yo, self.zi, self.zo = land
        self.outi_h, self.outo_h = outs
        self.xs, self.ys, self.zi_s, self.zo_s, self.fi, self.fo, self.lsem = sems
        half = s2i.shape[-1]
        self.mine = pl.ds(pl.multiple_of(place.x * half, half), half)
        self.theirs = pl.ds(pl.multiple_of(place.other_x * half, half), half)

    def full(self, r, which, columns):
        return self.s1[0].at[r - 1, :, :, :, columns] if which == 0 else self.s1[1].at[r - 1, :, :, columns]

    def x_copy(self, r, which):
        return remote(self.full(r, which, self.theirs), (self.xi, self.xo)[which].at[r - 1], self.xs, (r - 1, which), self.p.peer_x())

    def x_load(self, r, which):
        return pltpu.make_async_copy(self.full(r, which, self.mine), self.own[which].at[r - 1], self.lsem.at[which, r])

    def side(self, r, which, y):
        if which == 0:
            return self.xi.at[r - 1, :, y] if r else self.s2[0].at[:, y]
        return self.xo.at[r - 1, y] if r else self.s2[1].at[y]

    def y_copy(self, r, which):
        return remote(self.side(r, which, self.p.other_y), (self.yi, self.yo)[which].at[r], self.ys, (r, which), self.p.peer_y())

    def y_load(self, r, which):
        return pltpu.make_async_copy(self.side(r, which, self.p.y), self.own[2 + which], self.lsem.at[which, r])

    def z_in(self, r, d):
        to, t = self.p.ahead(d), self.p.ahead(r)
        return remote(self.yi.at[r, to], self.zi.at[t, d - 1], self.zi_s, (t, d - 1), self.p.at_z(to))

    def z_out(self, r):
        return remote(self.yo.at[r], self.zo.at[r - 1], self.zo_s, (r - 1,), self.p.at_z(self.p.ahead(r)))

    def last(self, t, r, columns):
        return remote(self.yi.at[r, self.p.z], self.outi_h.at[t, :, columns], self.fi, (t,), self.p.peer_x())

    def last_out(self, columns):
        return remote(self.yo.at[0], self.outo_h.at[:, columns], self.fo, (0,), self.p.peer_x())

    def keep(self, t, r):
        return pltpu.make_async_copy(self.yi.at[r, self.p.z], self.outi_h.at[t, :, self.mine], self.lsem.at[2, t])

    def keep_out(self):
        return pltpu.make_async_copy(self.yo.at[0], self.outo_h.at[:, self.mine], self.lsem.at[3, 0])

    def over_x(self, r):
        for which in range(2):
            self.x_copy(r, which).start()
            self.x_load(r, which).start()

    def over_y(self, r):
        for which in range(2):
            if r:
                self.x_copy(r, which).wait()
                self.x_load(r, which).wait()
                here, own = (self.xi, self.xo)[which], self.own[which]
                for k in range(here.shape[1]):
                    here[r - 1, k] = (here[r - 1, k].astype(F32) + own[r - 1, k].astype(F32)).astype(B16)
            else:
                self.y_load(r, which).start()
            self.y_copy(r, which).start()

    def over_z(self, r):
        if not r:
            self.y_load(r, 0).wait()
        self.y_copy(r, 0).wait_recv()
        for k in range(NZ):
            own = self.xi[r - 1, k, self.p.y] if r else self.own[2][k]
            self.yi[r, k] = (self.yi[r, k].astype(F32) + own.astype(F32)).astype(B16)
        for d in (1, 2, 3):
            self.z_in(r, d).start()
        if not r:
            self.y_load(r, 1).wait()
        self.y_copy(r, 1).wait_recv()
        own = self.xo[r - 1, self.p.y] if r else self.own[3][...]
        self.yo[r] = (self.yo[r].astype(F32) + own.astype(F32)).astype(B16)
        if r:
            self.z_out(r).start()

    def finish(self):
        for t in range(NZ):
            r = lax.rem(t + NZ - self.p.z, NZ)
            total = self.yi[r, self.p.z].astype(F32)
            for d in (1, 2, 3):
                slot = self.zi.at[t, d - 1]
                remote(slot, slot, self.zi_s, (t, d - 1), self.p.at_z(self.p.behind(d))).wait_recv()
                total = total + self.zi[t, d - 1].astype(F32)
            self.yi[r, self.p.z] = total.astype(B16)
            self.last(t, r, self.mine).start()
            self.keep(t, r).start()
        total = self.yo[0].astype(F32)
        for r in (1, 2, 3):
            self.z_out(r).wait_recv()
            total = total + self.zo[r - 1].astype(F32)
        self.yo[0] = total.astype(B16)
        self.last_out(self.mine).start()
        self.keep_out().start()

    def done(self):
        for r in range(NZ):
            for which in range(2):
                self.y_copy(r, which).wait_send()
            for d in (1, 2, 3):
                self.z_in(r, d).wait_send()
            if r:
                self.z_out(r).wait_send()
            t = self.p.ahead(r)
            self.last(t, r, self.mine).wait_send()
            self.last(t, r, self.theirs).wait_recv()
            self.keep(t, r).wait()
        self.last_out(self.mine).wait_send()
        self.last_out(self.theirs).wait_recv()
        self.keep_out().wait()


class SumAll:
    def __init__(self, place, v, land, sems):
        self.p, self.v, self.land, self.sems = place, v, land, sems

    def copy(self, k, peer):
        return remote(self.v.at[k], self.land.at[k], self.sems, (k,), peer)

    def begin(self):
        self.copy(0, self.p.peer_c()).start()

    def over_y(self):
        self.copy(0, self.p.peer_c()).wait_recv()
        self.v[1] = self.v[0] + self.land[0]
        self.copy(1, self.p.peer_y()).start()

    def z_copy(self, r, to):
        return remote(self.v.at[2], self.land.at[1 + r], self.sems, (1 + r,), self.p.at_z(to))

    def over_z(self):
        self.copy(1, self.p.peer_y()).wait_recv()
        self.v[2] = self.v[1] + self.land[1]
        for r in (1, 2, 3):
            self.z_copy(r, self.p.ahead(r)).start()

    def over_x(self):
        for r in (1, 2, 3):
            self.z_copy(r, self.p.ahead(r)).wait_recv()
        total = jnp.zeros_like(self.v[2])
        for z in range(NZ):
            r = lax.rem(self.p.z + NZ - z, NZ)
            part = self.v[2]
            for d in (1, 2, 3):
                part = jnp.where(r == d, self.land[1 + d], part)
            total = total + part
        self.v[3] = total
        remote(self.v.at[3], self.land.at[5], self.sems, (5,), self.p.peer_x()).start()

    def done(self):
        for k, peer in ((0, self.p.peer_c()), (1, self.p.peer_y())):
            self.copy(k, peer).wait_send()
        for r in (1, 2, 3):
            self.z_copy(r, self.p.ahead(r)).wait_send()
        remote(self.v.at[3], self.land.at[5], self.sems, (5,), self.p.peer_x()).wait()
        self.v[0] = self.v[3] + self.land[5]


BACKWARD_PLAN = {
    (PRE, 0, 0): ((TX, 1), (TY, 0),),
    (CROSS, 0, 1): ((PY, 3),),
    (CROSS, 0, 3): ((TX, 2),),
    (CROSS, 1, 0): ((TZ, 0), (TX, 3), (PY, 0),),
    (CROSS, 1, 2): ((PZ, 3),),
    (CROSS, 1, 3): ((TY, 1),),
    (CROSS, 1, 4): ((ME, 0),),
    (CROSS, 2, 1): ((PY, 1), (PZ, 0),),
    (LATE, 1, 0): ((TY, 2),),
    (LATE, 2, 0): ((TZ, 1),),
    (SELF, 0, 0): ((PZ, 1),),
    (SELF, 0, 2): ((PX, 3), (TY, 3), (TZ, 2),),
    (SELF, 0, 4): ((PY, 2),),
    (SELF, 1, 1): ((PX, 0), (TZ, 3),),
    (SELF, 1, 2): ((PY, 4),),
    (SELF, 1, 4): ((PZ, 2),),
    (SELF, 2, 0): ((PY, 5), (TF, 0),),
    (SELF, 2, 1): ((PZ, 4), (PX, 1),),
    (SELF, 2, 3): ((PY, 7),),
    (SELF, 2, 4): ((PX, 2), (PZ, 5),),
    (TAIL, 1, 0): ((PX, 4), (SY, 0), (PZ, 7), (SZ, 0), (PZ, 6), (PX, 5), (PX, 7), (SX, 0), (PX, 6),),
    (TAIL, 0, 0): ((PY, 6),),
}


def backward_kernel(
    tlen, mlen, flag, mix_h, tok_h, h1_h, qkv_h, a_h, lse_h, x1_h, mem_h, h2_h, cq_h, ckv_h, c_h, clse_h, g2_h, w_h, s1i_h, s1o_h, s2i_h, s2o_h,
    vecs_h, gbi_h, gains_h,
    mixed_h, gtok_h, gmem_h, tot_h, rx_h, outi_h, outo_h, vec_h,
    W, G, rc, ry, rz, ownxi, ownxo, ownyi, ownyo, rxi, rxo, ryi, ryo, rzi, rzo, sv, sland,
    h, att, qkv, ckv, lse, clse, x1, mem, g2, gb, db, dh, gm, gmb, vec, vin, gbi,
    qt, kt, ktc, at, dat, ps, dss, qm, dm, dqt, dk_acc, dv_acc, dkc_acc, dvc_acc, dq, dk, dv, dck, dcv,
    csem, ysem, zsem, xsem, lsem, txs, tys, tzi, tzo, tfi, tfo, tlsem, vsem, gsem, loc,
):
    p = Place()
    L, D = h.shape
    M = mem.shape[0]
    half = L // 2
    count = []

    def fetch(src, dst):
        cp = pltpu.make_async_copy(src, dst, loc.at[len(count)])
        cp.start()
        count.append(cp)
        return cp

    vec_cp = [fetch(gains_h, vec), fetch(vecs_h, vin), fetch(gbi_h, gbi)]
    g2_cp = fetch(g2_h, g2)
    w_cp = [None] * 4
    w_cp[3] = fetch(w_h.at[7], W.at[3])
    c_cp = fetch(c_h, att)
    cross_cp = [fetch(cq_h, qkv.at[0]), fetch(ckv_h, ckv), fetch(clse_h, clse), fetch(h2_h, h), fetch(mem_h, mem)]
    for g in range(3):
        w_cp[g] = fetch(w_h.at[4 + g], W.at[g])
    x1_cp = fetch(x1_h, x1)
    kv_cp = [fetch(qkv_h.at[1], qkv.at[1]), fetch(qkv_h.at[2], qkv.at[2]), fetch(lse_h, lse)]
    p.greet()
    rs_ = Reduce(p, G, rc, ry, rz, tot_h, rx_h, csem, ysem, zsem, xsem, lsem)
    tiles = ReduceTiles(p, s1i_h, s1o_h, s2i_h, s2o_h, (ownxi, ownxo, ownyi, ownyo), (rxi, rxo, ryi, ryo, rzi, rzo), (outi_h, outo_h),
                        (txs, tys, tzi, tzo, tfi, tfo, tlsem))
    small = SumAll(p, sv, sland, vsem)
    theirs = pl.ds(pl.multiple_of(p.other_x * half, half), half)
    ours = pl.ds(pl.multiple_of(p.x * half, half), half)
    mix_send = remote(mix_h.at[theirs], mixed_h.at[p.x], gsem, (2,), p.peer_x())
    mix_land = remote(mix_h.at[theirs], mixed_h.at[p.other_x], gsem, (2,), p.peer_x())
    steps = {
        PY: rs_.over_y, PZ: rs_.over_z, PX: rs_.over_x, TX: tiles.over_x, TY: tiles.over_y, TZ: tiles.over_z,
        TF: lambda _: tiles.finish(), ME: lambda _: mix_send.start(),
        SY: lambda _: small.over_y(), SZ: lambda _: small.over_z(), SX: lambda _: small.over_x(),
    }

    def point(name):
        run_plan(BACKWARD_PLAN, steps, name)

    point((PRE, 0, 0))
    f = flag[p.x].astype(F32)
    for cp in vec_cp:
        cp.wait()
    g2_cp.wait()
    w_cp[3].wait()
    for r in range(0, L, ROWS):
        rs = pl.ds(r, ROWS)
        gcr = (f * g2[rs]).astype(B16)
        gb[rs] = gcr
        db[rs] = dot_nt(gcr, flat(W[3])).astype(B16)
        dh[rs] = jnp.zeros((ROWS, D), F32)
    gm[...] = jnp.zeros_like(gm)
    point((PRE, 1, 0))

    def put(n, lo, hi, value):
        G[quarter(n), :, :, :, :, lo:hi] = value.astype(B16).reshape(G.shape[1:5] + (hi - lo,))

    def out_projection(n):
        for j in range(0, D, GROUP):
            put(n, j, j + GROUP, dot_tn(att[...], gb[:, j : j + GROUP]))

    c_cp.wait()
    out_projection(3)
    rs_.over_c(3)
    for cp in cross_cp:
        cp.wait()
    for g in range(3):
        w_cp[g].wait()

    def wpart(n, k):
        return flat(W[n, :, :, :, :, k * GROUP : (k + 1) * GROUP])

    def cross_group(g, _):
        def step(i):
            run_plan_at(BACKWARD_PLAN, steps, CROSS, g, 3, i)

        attend_back_group(qkv, ckv, ckv, (0, g), (0, g), (1, g), att, db, g, clse, mlen[p.x], False, 256,
                          qt, ktc, at, dat, ps, dss, qm, dm, dqt, dkc_acc, dvc_acc, step)
        dq[...] = dqt[...].astype(F32).T.astype(B16)
        dck[...] = dkc_acc[...].astype(B16)
        dcv[...] = dvc_acc[...].astype(B16)
        put(g, 0, GROUP, dot_tn(h[...], dq[...]))
        put(g, GROUP, 2 * GROUP, dot_tn(mem[...], dck[...]))
        put(g, 2 * GROUP, 3 * GROUP, dot_tn(mem[...], dcv[...]))
        rs_.over_c(g)
        for r in range(0, L, ROWS):
            rs = pl.ds(r, ROWS)
            dh[rs] += dot_nt(dq[rs], wpart(g, 0))
        gm[...] += dot_nt(dck[...], wpart(g, 1)) + dot_nt(dcv[...], wpart(g, 2))

        step(4)
        return 0

    lax.fori_loop(0, 3, cross_group, 0)
    self_cp = [fetch(w_h.at[3], W.at[3]), fetch(a_h, att), fetch(h1_h, h), fetch(qkv_h.at[0], qkv.at[0])]
    for g in range(3):
        self_cp.append(fetch(w_h.at[g], W.at[g]))
    gmb[...] = gm[...].astype(B16)
    mhalf = M // 2
    gm_send = remote(gmb.at[pl.ds(pl.multiple_of(p.other_x * mhalf, mhalf), mhalf)], gmem_h.at[p.x], gsem, (0,), p.peer_x())
    gm_land = remote(gmb.at[pl.ds(0, mhalf)], gmem_h.at[p.other_x], gsem, (0,), p.peer_x())
    gm_send.start()
    gm_own = fetch(gmb.at[pl.ds(pl.multiple_of(p.x * mhalf, mhalf), mhalf)], gmem_h.at[p.x])
    point((LATE, 0, 0))
    x1_cp.wait()
    sg = jnp.zeros((1, D), F32)
    sb = jnp.zeros((1, D), F32)
    for r in range(0, L, ROWS):
        rs = pl.ds(r, ROWS)
        dx, s, b = norm_back(dh[rs], x1[rs], vec[1:2])
        g1 = g2[rs] + dx
        g2[rs] = g1
        gb[rs] = g1.astype(B16)
        sg += s
        sb += b
    sv[0, 1:2] = sg
    sv[0, 4:5] = sb
    sv[0, 2:3] = vin[0:1]
    sv[0, 5:6] = vin[1:2]
    sv[0, 6:7] = vin[2:3]
    sv[0, 7:8] = jnp.zeros((1, D), F32)
    for t in range(NZ):
        sv[0, 8 + t : 9 + t] = gbi[t, 0:1]
    sv[0, 12:16] = jnp.zeros((4, D), F32)
    point((LATE, 1, 0))
    self_cp[0].wait()
    for r in range(0, L, ROWS):
        rs = pl.ds(r, ROWS)
        db[rs] = dot_nt(gb[rs], flat(W[3])).astype(B16)
        dh[rs] = jnp.zeros((ROWS, D), F32)
    point((LATE, 2, 0))
    self_cp[1].wait()
    out_projection(7)
    rs_.over_c(7)
    tok = gb
    tok_cp = fetch(tok_h, tok)
    for cp in self_cp[2:] + kv_cp:
        cp.wait()

    def self_group(g, _):
        def step(i):
            run_plan_at(BACKWARD_PLAN, steps, SELF, g, 3, i)

        attend_back_group(qkv, qkv, qkv, (0, g), (1, g), (2, g), att, db, g, lse, tlen[p.x], True, 256,
                          qt, kt, at, dat, ps, dss, qm, dm, dqt, dk_acc, dv_acc, step)
        dq[...] = dqt[...].astype(F32).T.astype(B16)
        dk[...] = dk_acc[...].astype(B16)
        dv[...] = dv_acc[...].astype(B16)
        for k, d in enumerate((dq, dk, dv)):
            put(4 + g, k * GROUP, (k + 1) * GROUP, dot_tn(h[...], d[...]))
        rs_.over_c(4 + g)
        for r in range(0, L, ROWS):
            rs = pl.ds(r, ROWS)
            dh[rs] += dot_nt(dq[rs], wpart(g, 0)) + dot_nt(dk[rs], wpart(g, 1)) + dot_nt(dv[rs], wpart(g, 2))
        step(4)
        return 0

    lax.fori_loop(0, 3, self_group, 0)
    tok_cp.wait()
    sg = jnp.zeros((1, D), F32)
    sb = jnp.zeros((1, D), F32)
    gt = db
    sent = False
    gt_send = remote(gt.at[theirs], gtok_h.at[p.x], gsem, (1,), p.peer_x())
    gt_land = remote(gt.at[theirs], gtok_h.at[p.other_x], gsem, (1,), p.peer_x())
    for start in (p.other_x * half, p.x * half):
        for r in range(0, half, ROWS):
            rs = pl.ds(pl.multiple_of(start + r, ROWS), ROWS)
            dx, s, b = norm_back(dh[rs], tok[rs].astype(F32), vec[0:1])
            gt[rs] = (g2[rs] + dx).astype(B16)
            sg += s
            sb += b
        if not sent:
            gt_send.start()
            point((TAIL, 0, 0))
        sent = True
    sv[0, 0:1] = sg
    sv[0, 3:4] = sb
    small.begin()
    gt_own = fetch(gt.at[ours], gtok_h.at[p.x])
    point((TAIL, 1, 0))
    for n in range(8):
        rs_.done(n)
    tiles.done()
    small.done()
    vec_out = fetch(sv.at[0], vec_h)
    for cp in (mix_send, gm_send, gt_send):
        cp.wait_send()
    for cp in (mix_land, gm_land, gt_land):
        cp.wait_recv()
    for cp in (gm_own, gt_own, vec_out):
        cp.wait()


def backward_call(tlen, mlen, flag, arrays):
    mix, tok, h1, qkv, a, lse, x1, mem, h2, cq, ckv, c, clse, g2, w, s1i, s1o, s2i, s2o, vecs, gbi, gains = arrays
    L, D = tok.shape
    M = mem.shape[0]
    G = D // GROUP
    S = w.shape[4]
    R = s1o.shape[2]
    H = D // 2
    outs = [((2, L // 2, D), B16), ((2, L // 2, D), B16), ((2, M // 2, D), B16), ((8, S, D), B16), ((8, S, D), B16), ((NZ, S, D), B16),
            ((R, D), B16), ((SMALL, D), F32)]
    scratch = [
        ((4, NZ, NY, NC, S, D), B16), ((4, NZ, NY, NC, S, D), B16), ((8, NZ, NY, S, D), B16), ((8, NZ, S, D), B16), ((8, 3, S, D), B16),
        ((3, NZ, NY, S, H), B16), ((3, NY, R, H), B16), ((NZ, S, H), B16), ((R, H), B16),
        ((3, NZ, NY, S, H), B16), ((3, NY, R, H), B16), ((NZ, NZ, S, H), B16), ((NZ, R, H), B16), ((NZ, 3, S, H), B16), ((3, R, H), B16),
        ((4, SMALL, D), F32), ((6, SMALL, D), F32),
        ((L, D), B16), ((L, D), B16), ((3, G, L, GROUP), B16), ((2, G, M, GROUP), B16), ((G, 8, L), F32), ((G, 8, L), F32), ((L, D), F32),
        ((M, D), B16), ((L, D), F32), ((L, D), B16), ((L, D), B16), ((L, D), F32), ((M, D), F32), ((M, D), B16), ((SMALL, D), F32), ((8, D), F32),
        ((NZ, 8, D), F32),
        ((GROUP, L), B16), ((GROUP, L), B16), ((GROUP, M), B16), ((GROUP, L), B16), ((GROUP, L), B16),
        ((L, PER * 256), B16), ((L, PER * 256), B16), ((PER * 256, GROUP), B16), ((PER * 256, GROUP), B16),
        ((GROUP, L), B16), ((L, GROUP), F32), ((L, GROUP), F32), ((M, GROUP), F32), ((M, GROUP), F32),
        ((L, GROUP), B16), ((L, GROUP), B16), ((L, GROUP), B16), ((M, GROUP), B16), ((M, GROUP), B16),
    ]
    sems = [(2, 8), (2, 8), (2, 8, 3), (2, 8), (8,), (2, 3, 2), (2, 4, 2), (2, 4, 3), (2, 3), (2, 4), (2, 1), (4, 4), (2, 6), (2, 3), (40,)]
    return pl.pallas_call(
        backward_kernel,
        out_shape=[jax.ShapeDtypeStruct(s, d) for s, d in outs],
        in_specs=[SMEM_SPEC] * 3 + [ANY_SPEC] * len(arrays),
        out_specs=[ANY_SPEC] * len(outs),
        scratch_shapes=[VMEM(s, d) for s, d in scratch] + [DMA(s) for s in sems],
        compiler_params=pltpu.CompilerParams(vmem_limit_bytes=63 * 1024 * 1024, collective_id=1, has_side_effects=True),
        name="backward",
    )(tlen, mlen, flag, *arrays)


def finish_kernel(
    mix_i, mixed_i, gtok_i, gmem_i, tot_i, rx_i, ins_i, out_i, vec_i,
    mixed, gtok, gmem, gsw, gsp, gcw, gcp, gwi, gwo, gbi, gbo, gg, gs,
    mix_v, tok_v, mem_v, tot_v, rx_v, ins_v, out_v, vec_v, tok_f, mem_f, sw_f, sp_f, cw_f, cp_f, wi_f, wo_f, bi_f, bo_f, g_f, s_f, sems,
):
    count = []

    def copy(src, dst):
        cp = pltpu.make_async_copy(src, dst, sems.at[len(count)])
        cp.start()
        count.append(cp)
        return cp

    S = gsp.shape[0]
    halves = [copy(gtok_i.at[k], tok_v.at[k]) for k in range(2)]
    rest = [copy(a, b) for a, b in ((tot_i, tot_v), (rx_i, rx_v), (ins_i, ins_v), (out_i, out_v), (gmem_i, mem_v), (vec_i, vec_v))]
    x = lax.axis_index("mem")
    half = mixed.shape[1]
    both = [copy(mix_i.at[pl.ds(pl.multiple_of(x * half, half), half)], mix_v.at[0]), copy(mixed_i.at[1 - x], mix_v.at[1])]
    outs = []
    for k in range(2):
        halves[k].wait()
        tok_f[k] = tok_v[k].astype(F32)
        outs.append(copy(tok_f.at[k], gtok.at[k]))
    for k, cp in enumerate(both):
        cp.wait()
        outs.append(copy(mix_v.at[k], mixed.at[1 - x if k else x]))
    for cp in rest:
        cp.wait()
    for first, dst in ((0, cw_f), (4, sw_f)):
        for g in range(3):
            v = tot_v[first + g].astype(F32) + rx_v[first + g].astype(F32)
            for k in range(3):
                dst[k, :, g * GROUP : (g + 1) * GROUP] = v[:, k * GROUP : (k + 1) * GROUP]
    cp_f[...] = tot_v[3].astype(F32) + rx_v[3].astype(F32)
    sp_f[...] = tot_v[7].astype(F32) + rx_v[7].astype(F32)
    D = sp_f.shape[1]
    for t in range(NZ):
        wi_f[:, t * D : (t + 1) * D] = ins_v[t].astype(F32)
    wo_f[...] = out_v[...].astype(F32)
    mem_f[...] = mem_v[...].astype(F32)
    i = lax.axis_index("fsdp")
    R = wo_f.shape[0]
    mine = pltpu.roll(vec_v[0:8], lax.rem(D - i * S, D), 1)
    g_f[...] = mine[0:3, :S]
    s_f[...] = mine[3:6, :S]
    bo_f[...] = mine[6:7, :S]
    row = lax.broadcasted_iota(jnp.int32, (8, D), 0)
    tile = jnp.sum(jnp.where(row == i // (NY * NC), vec_v[8:16], 0.0), 0, keepdims=True)
    tile = pltpu.roll(jnp.broadcast_to(tile, (8, D)), lax.rem(D - lax.rem(i, NY * NC) * R, D), 1)
    bi_f[...] = tile[0:1, :R]
    for a, b in ((mem_f, gmem), (sw_f, gsw), (sp_f, gsp), (cw_f, gcw), (cp_f, gcp), (wi_f, gwi), (wo_f, gwo), (bi_f, gbi), (bo_f, gbo), (g_f, gg), (s_f, gs)):
        outs.append(copy(a, b))
    for cp in outs:
        cp.wait()


def finish_call(mix, mixed, gtok, gmem, tot, rx, ins, out, vec):
    S, D = tot.shape[1:]
    R = out.shape[0]
    outs = [(mixed.shape, B16), (gtok.shape, F32), (gmem.shape, F32), ((3, S, D), F32), ((S, D), F32), ((3, S, D), F32), ((S, D), F32),
            ((S, NZ * D), F32), ((R, D), F32), ((1, R), F32), ((1, S), F32), ((3, S), F32), ((3, S), F32)]
    ins_ = (mix, mixed, gtok, gmem, tot, rx, ins, out, vec)
    scratch = [VMEM(v.shape, v.dtype) for v in ins_[1:]] + [VMEM(s, d) for s, d in outs[1:]]
    return pl.pallas_call(
        finish_kernel,
        out_shape=[jax.ShapeDtypeStruct(s, d) for s, d in outs],
        in_specs=[HBM_SPEC] * len(ins_),
        out_specs=[HBM_SPEC] * len(outs),
        scratch_shapes=scratch + [DMA((32,))],
        compiler_params=pltpu.CompilerParams(vmem_limit_bytes=62 * 1024 * 1024),
        name="finish",
    )(*ins_)


def paired_body(tokens, memory, cotangent, text_len, mem_len, image_flag, self_qkv, self_out, cross_qkv, cross_out,
                w_in, w_out, b_in, b_out, norm_gain, norm_bias):
    fw = forward_call(text_len, mem_len, image_flag, tokens, memory, cotangent, self_qkv, self_out, cross_qkv, cross_out,
                      w_in, w_out, pack_small(norm_gain, norm_bias, b_out, b_in))
    outs = finish_call(fw[0], *backward_call(text_len, mem_len, image_flag, fw))
    return (*outs[:9], outs[9][0], outs[10][0], *outs[11:])


def layer_norm(values, gain, shift):
    centre = values - jnp.mean(values, -1, keepdims=True)
    spread = jnp.mean(centre * centre, -1, keepdims=True)
    return centre * lax.rsqrt(spread + EPSILON) * gain + shift


def gelu_exact(values):
    return jax.nn.gelu(values, approximate=False)


def split_heads(values):
    return values.reshape(values.shape[0], values.shape[1], -1, HEAD).transpose(2, 0, 1, 3)


def merge_heads(values):
    return values.transpose(1, 2, 0, 3).reshape(values.shape[1], values.shape[2], -1)


def head_scores(query_matrix, key_matrix, allowed):
    logit_scores = jnp.einsum(
        "cti,cvi->ctv", query_matrix, key_matrix, preferred_element_type=jnp.float32
    ) * HEAD ** (-0.5)
    return jnp.where(allowed, logit_scores, -1000000000.0)


def attend(query_matrix, key_matrix, values, allowed):

    def one_head(parts):
        head_query_rows, head_key_rows, head_value_rows = parts
        logit_scores = head_scores(head_query_rows, head_key_rows, allowed)
        row_max = jnp.max(logit_scores, -1, keepdims=True)
        expo = jnp.exp(logit_scores - row_max)
        row_sum = jnp.sum(expo, -1, keepdims=True)
        reduced_probabilities = (expo / row_sum).astype(jnp.bfloat16)
        attention_output = jnp.einsum(
            "zqf,zfm->zqm",
            reduced_probabilities,
            head_value_rows,
            preferred_element_type=jnp.float32,
        )
        return (attention_output, row_max, row_sum)

    attention_output, row_max, row_sum = lax.map(
        one_head, (split_heads(query_matrix), split_heads(key_matrix), split_heads(values))
    )
    return (merge_heads(attention_output).astype(jnp.bfloat16), row_max, row_sum)


def attend_back(query_matrix, key_matrix, values, allowed, row_max, row_sum, grad_out):

    def one_head(parts):
        (
            head_query_rows,
            head_key_rows,
            head_value_rows,
            head_output_gradient,
            head_max,
            head_sum,
        ) = parts
        logit_scores = head_scores(head_query_rows, head_key_rows, allowed)
        probs = jnp.exp(logit_scores - head_max) / head_sum
        reduced_probabilities = probs.astype(jnp.bfloat16)
        probs_gradient = jnp.einsum(
            "cti,cvi->ctv",
            head_output_gradient,
            head_value_rows,
            preferred_element_type=jnp.float32,
        )
        delta_sum = jnp.sum(probs * probs_gradient, -1, keepdims=True)
        scores_gradient = (probs * (probs_gradient - delta_sum)).astype(jnp.bfloat16)
        d_query = jnp.einsum(
            "zqf,zfm->zqm", scores_gradient, head_key_rows, preferred_element_type=jnp.float32
        ) * HEAD ** (-0.5)
        d_keys = jnp.einsum(
            "pum,pug->pmg", scores_gradient, head_query_rows, preferred_element_type=jnp.float32
        ) * HEAD ** (-0.5)
        values_gradient = jnp.einsum(
            "pum,pug->pmg",
            reduced_probabilities,
            head_output_gradient,
            preferred_element_type=jnp.float32,
        )
        return (d_query, d_keys, values_gradient)

    d_query, d_keys, values_gradient = lax.map(
        one_head,
        (
            split_heads(query_matrix),
            split_heads(key_matrix),
            split_heads(values),
            split_heads(grad_out),
            row_max,
            row_sum,
        ),
    )
    return (merge_heads(d_query), merge_heads(d_keys), merge_heads(values_gradient))


def general_body(
    tokens,
    memory,
    cotangent,
    text_len,
    mem_len,
    image_flag,
    self_qkv,
    self_out,
    cross_qkv,
    cross_out,
    w_in,
    w_out,
    b_in,
    b_out,
    norm_gain,
    norm_bias,
):
    f32 = jnp.float32
    b16 = jnp.bfloat16
    seq_count, own_rows, width = tokens.shape
    offset = lax.axis_index("mem") * own_rows
    gathered = (
        lax.all_gather(self_qkv, "fsdp", axis=1, tiled=True),
        lax.all_gather(self_out, "fsdp", axis=0, tiled=True),
        lax.all_gather(cross_qkv, "fsdp", axis=1, tiled=True),
        lax.all_gather(cross_out, "fsdp", axis=0, tiled=True),
        lax.all_gather(w_in, "fsdp", axis=0, tiled=True),
        lax.all_gather(w_out, "fsdp", axis=0, tiled=True),
        lax.all_gather(b_in, "fsdp", axis=0, tiled=True),
        lax.all_gather(b_out, "fsdp", axis=0, tiled=True),
        lax.all_gather(norm_gain, "fsdp", axis=1, tiled=True),
        lax.all_gather(norm_bias, "fsdp", axis=1, tiled=True),
    )
    (
        self_w,
        self_proj,
        cross_w,
        cross_proj,
        inner_w,
        outer_w,
        inner_bias,
        outer_bias,
        gains,
        shifts,
    ) = gathered
    gains = gains.astype(f32)
    shifts = shifts.astype(f32)
    x0 = tokens.astype(f32)
    h1_full, norm0_back = jax.vjp(layer_norm, x0, gains[0], shifts[0])
    h1 = h1_full.astype(b16)
    qkv = jnp.einsum("srd,kde->ksre", h1, self_w, preferred_element_type=f32).astype(b16)
    keys_all, values_all = (
        lax.all_gather(qkv[1], "mem", axis=1, tiled=True),
        lax.all_gather(qkv[2], "mem", axis=1, tiled=True),
    )
    key_pos = jnp.arange(keys_all.shape[1], dtype=jnp.int32)
    query_pos = offset + jnp.arange(own_rows, dtype=jnp.int32)
    self_mask = (key_pos[None, None, :] <= query_pos[None, :, None]) & (
        key_pos[None, None, :] < text_len[:, None, None]
    )
    attended, self_max, self_sum = attend(qkv[0], keys_all, values_all, self_mask)
    x1 = x0 + jnp.einsum("srd,de->sre", attended, self_proj, preferred_element_type=f32)
    h2_full, norm1_back = jax.vjp(layer_norm, x1, gains[1], shifts[1])
    h2 = h2_full.astype(b16)
    cross_q = jnp.einsum("srd,de->sre", h2, cross_w[0], preferred_element_type=f32).astype(b16)
    memory_all = lax.all_gather(memory, "mem", axis=1, tiled=True)
    cross_kv = jnp.einsum(
        "snd,kde->ksne", memory_all, cross_w[1:], preferred_element_type=f32
    ).astype(b16)
    cross_keys, cross_values = (cross_kv[0], cross_kv[1])
    mem_pos = jnp.arange(cross_keys.shape[1], dtype=jnp.int32)
    cross_mask = mem_pos[None, None, :] < mem_len[:, None, None]
    crossed, cross_max, cross_sum = attend(cross_q, cross_keys, cross_values, cross_mask)
    flag = image_flag.astype(f32)[:, None, None]
    x2 = x1 + jnp.einsum("srd,de->sre", crossed, cross_proj, preferred_element_type=f32) * flag
    h3_full, norm2_back = jax.vjp(layer_norm, x2, gains[2], shifts[2])
    h3 = h3_full.astype(b16)
    pre = jnp.einsum("srd,df->srf", h3, inner_w, preferred_element_type=f32) + inner_bias.astype(
        f32
    )
    act_full, gelu_back = jax.vjp(gelu_exact, pre)
    act_low = act_full.astype(b16)
    attention_output = (
        x2
        + jnp.einsum("srf,fd->srd", act_low, outer_w, preferred_element_type=f32)
        + outer_bias.astype(f32)
    )
    mixed = attention_output.astype(b16)
    grad_top = cotangent.astype(f32)
    grad_low = grad_top.astype(b16)
    grad_outer_bias = jnp.sum(grad_low.astype(f32), (0, 1))
    grad_outer = jnp.einsum("srf,srd->fd", act_low, grad_low, preferred_element_type=f32)
    d_act = jnp.einsum("srd,fd->srf", grad_low, outer_w, preferred_element_type=f32)
    d_pre = gelu_back(d_act)[0].astype(b16)
    grad_inner_bias = jnp.sum(d_pre.astype(f32), (0, 1))
    grad_inner = jnp.einsum("srd,srf->df", h3, d_pre, preferred_element_type=f32)
    d_h3 = jnp.einsum("srf,df->srd", d_pre, inner_w, preferred_element_type=f32)
    d_x2, gain_two, shift_two = norm2_back(d_h3)
    grad_two = grad_top + d_x2
    grad_cross = (grad_two * flag).astype(b16)
    grad_cross_proj = jnp.einsum("srd,sre->de", crossed, grad_cross, preferred_element_type=f32)
    d_crossed = jnp.einsum(
        "sre,de->srd", grad_cross, cross_proj, preferred_element_type=f32
    ).astype(b16)
    d_cross_q, d_cross_k, d_cross_v = attend_back(
        cross_q, cross_keys, cross_values, cross_mask, cross_max, cross_sum, d_crossed
    )
    own_cross_k, own_cross_v = (
        lax.psum_scatter(
            d_cross_k.astype(jnp.bfloat16), "mem", scatter_dimension=1, tiled=True
        ).astype(jnp.float32),
        lax.psum_scatter(
            d_cross_v.astype(jnp.bfloat16), "mem", scatter_dimension=1, tiled=True
        ).astype(jnp.float32),
    )
    d_cross_kv = jnp.stack([own_cross_k, own_cross_v]).astype(b16)
    grad_cross_kv = jnp.einsum("snd,ksne->kde", memory, d_cross_kv, preferred_element_type=f32)
    grad_memory = jnp.einsum("ksne,kde->snd", d_cross_kv, cross_w[1:], preferred_element_type=f32)
    d_cross_low = d_cross_q.astype(b16)
    grad_cross_q = jnp.einsum("srd,sre->de", h2, d_cross_low, preferred_element_type=f32)
    d_h2 = jnp.einsum("sre,de->srd", d_cross_low, cross_w[0], preferred_element_type=f32)
    d_x1, gain_one, shift_one = norm1_back(d_h2)
    grad_one = grad_two + d_x1
    grad_cross_w = jnp.concatenate([grad_cross_q[None], grad_cross_kv], 0)
    grad_one_low = grad_one.astype(b16)
    grad_self_proj = jnp.einsum("srd,sre->de", attended, grad_one_low, preferred_element_type=f32)
    d_attended = jnp.einsum(
        "sre,de->srd", grad_one_low, self_proj, preferred_element_type=f32
    ).astype(b16)
    d_query, d_keys, values_gradient = attend_back(
        qkv[0], keys_all, values_all, self_mask, self_max, self_sum, d_attended
    )
    own_keys, own_values = (
        lax.psum_scatter(
            d_keys.astype(jnp.bfloat16), "mem", scatter_dimension=1, tiled=True
        ).astype(jnp.float32),
        lax.psum_scatter(
            values_gradient.astype(jnp.bfloat16), "mem", scatter_dimension=1, tiled=True
        ).astype(jnp.float32),
    )
    d_qkv = jnp.stack([d_query, own_keys, own_values]).astype(b16)
    grad_self_w = jnp.einsum("srd,ksre->kde", h1, d_qkv, preferred_element_type=f32)
    d_h1 = jnp.einsum("ksre,kde->srd", d_qkv, self_w, preferred_element_type=f32)
    d_x0, gain_zero, shift_zero = norm0_back(d_h1)
    grad_tokens = grad_one + d_x0
    gain_grads = jnp.stack([gain_zero, gain_one, gain_two])
    shift_grads = jnp.stack([shift_zero, shift_one, shift_two])
    full_grads = (
        grad_self_w,
        grad_self_proj,
        grad_cross_w,
        grad_cross_proj,
        grad_inner,
        grad_outer,
        grad_inner_bias,
        grad_outer_bias,
        gain_grads,
        shift_grads,
    )
    shards = (
        lax.psum_scatter(
            full_grads[0].astype(jnp.bfloat16), "fsdp", scatter_dimension=1, tiled=True
        ).astype(jnp.float32),
        lax.psum_scatter(
            full_grads[1].astype(jnp.bfloat16), "fsdp", scatter_dimension=0, tiled=True
        ).astype(jnp.float32),
        lax.psum_scatter(
            full_grads[2].astype(jnp.bfloat16), "fsdp", scatter_dimension=1, tiled=True
        ).astype(jnp.float32),
        lax.psum_scatter(
            full_grads[3].astype(jnp.bfloat16), "fsdp", scatter_dimension=0, tiled=True
        ).astype(jnp.float32),
        lax.psum_scatter(
            full_grads[4].astype(jnp.bfloat16), "fsdp", scatter_dimension=0, tiled=True
        ).astype(jnp.float32),
        lax.psum_scatter(
            full_grads[5].astype(jnp.bfloat16), "fsdp", scatter_dimension=0, tiled=True
        ).astype(jnp.float32),
        lax.psum_scatter(
            full_grads[6].astype(jnp.bfloat16), "fsdp", scatter_dimension=0, tiled=True
        ).astype(jnp.float32),
        lax.psum_scatter(
            full_grads[7].astype(jnp.bfloat16), "fsdp", scatter_dimension=0, tiled=True
        ).astype(jnp.float32),
        lax.psum_scatter(
            full_grads[8].astype(jnp.bfloat16), "fsdp", scatter_dimension=1, tiled=True
        ).astype(jnp.float32),
        lax.psum_scatter(
            full_grads[9].astype(jnp.bfloat16), "fsdp", scatter_dimension=1, tiled=True
        ).astype(jnp.float32),
    )
    totals = (
        lax.psum(shards[0].astype(jnp.bfloat16), "mem").astype(jnp.float32),
        lax.psum(shards[1].astype(jnp.bfloat16), "mem").astype(jnp.float32),
        lax.psum(shards[2].astype(jnp.bfloat16), "mem").astype(jnp.float32),
        lax.psum(shards[3].astype(jnp.bfloat16), "mem").astype(jnp.float32),
        lax.psum(shards[4].astype(jnp.bfloat16), "mem").astype(jnp.float32),
        lax.psum(shards[5].astype(jnp.bfloat16), "mem").astype(jnp.float32),
        lax.psum(shards[6].astype(jnp.bfloat16), "mem").astype(jnp.float32),
        lax.psum(shards[7].astype(jnp.bfloat16), "mem").astype(jnp.float32),
        lax.psum(shards[8].astype(jnp.bfloat16), "mem").astype(jnp.float32),
        lax.psum(shards[9].astype(jnp.bfloat16), "mem").astype(jnp.float32),
    )
    return (
        mixed,
        grad_tokens,
        grad_memory,
        totals[0],
        totals[1],
        totals[2],
        totals[3],
        totals[4],
        totals[5],
        totals[6],
        totals[7],
        totals[8],
        totals[9],
    )


def body(*args):
    if lax.axis_size("mem") == 2 and lax.axis_size("fsdp") == NZ * NY * NC:
        return paired_body(*args)
    return general_body(*args)


def solution(mesh):
    placed = (
        P("fsdp", "mem", None),
        P("fsdp", "mem", None),
        P("fsdp", "mem", None),
        P("fsdp"),
        P("fsdp"),
        P("fsdp"),
        P(None, "fsdp", None),
        P("fsdp", None),
        P(None, "fsdp", None),
        P("fsdp", None),
        P("fsdp", None),
        P("fsdp", None),
        P("fsdp"),
        P("fsdp"),
        P(None, "fsdp"),
        P(None, "fsdp"),
    )
    return jax.shard_map(
        body,
        mesh=mesh,
        in_specs=placed,
        out_specs=(
            P("fsdp", "mem", None),
            P("fsdp", "mem", None),
            P("fsdp", "mem", None),
            P(None, "fsdp", None),
            P("fsdp", None),
            P(None, "fsdp", None),
            P("fsdp", None),
            P("fsdp", None),
            P("fsdp", None),
            P("fsdp"),
            P("fsdp"),
            P(None, "fsdp"),
            P(None, "fsdp"),
        ),
        check_vma=False,
    )
```
